32 devices in a mesh: dp: 4 (over z), gy: 4 (over y, core), gz: 2 (over x).
Axes of the slice: x: 2, y: 2, z: 4, core: 2. Of those that a mesh axis runs over, the one named last changes fastest.
Arguments:
- volume: bfloat16 [4, 4, 16, 32, 128], P('dp', None, 'gy', 'gz'), may hold values from -6 to 6
- pooled_first: bfloat16 [4, 16, 8, 16, 64], P('dp', None, 'gy', 'gz'), may hold values from -6 to 6
- where_first: int32 [4, 16, 8, 16, 64], P('dp', None, 'gy', 'gz'), may hold values from 0 to 7
- pooled_second: bfloat16 [4, 32, 4, 8, 32], P('dp', None, 'gy', 'gz'), may hold values from -6 to 6
- where_second: int32 [4, 32, 4, 8, 32], P('dp', None, 'gy', 'gz'), may hold values from 0 to 7
- upstream: bfloat16 [4, 32, 4, 8, 32], P('dp', None, 'gy', 'gz'), may hold values from -6 to 6
- kernel_first: bfloat16 [16, 4, 3, 3, 3], replicated, may hold values from -0.625 to 0.625
- kernel_second: bfloat16 [32, 16, 3, 3, 3], replicated, may hold values from -0.3125 to 0.3125
Outputs:
- grad_volume: bfloat16 [4, 4, 16, 32, 128], P('dp', None, 'gy', 'gz')
- grad_kernel_first: float32 [1728], P('dp')
- grad_kernel_second: float32 [13824], P('dp')
The draws below stay inside these ranges and needn't reach their ends.
All inputs are finite; a program needn't handle non-finite values.
Results may differ from the reference program's by a relative error of at most 0.005.
Values may be sent and summed in bfloat16 or wider, within the bound.
No kernel may reach another device: no remote copies, remote signals or barrier semaphores. Data moves between devices by JAX's collectives and lax.ppermute only.
A program may use at most 64 MiB of HBM per device.

```python
import math
import jax
import jax.numpy as jnp
from jax import lax

C0 = 4
C1 = 16
C2 = 32
NX = 128
VOLUMES = 4
NY = 16
NZ = 32


def touch_ends(result, key, smallest, largest):
    shape = result.shape
    index_at = [jax.random.randint(jax.random.fold_in(key, axis), (), 0, shape[axis]) for axis in range(len(shape))]
    result = result.at[tuple(index_at)].set(smallest)
    longest = shape.index(max(shape))
    index_at[longest] = (index_at[longest] + 1) % shape[longest]
    return result.at[tuple(index_at)].set(largest)


def levels(rng, extent, split, low, high):
    gain, own = 1.0, jax.random.fold_in(rng, 6)
    for axis_at, blocks in split:
        steps = jnp.exp(jax.random.uniform(jax.random.fold_in(own, axis_at), (blocks,), jnp.float32, low / len(split), high / len(split)))
        gain = gain * jnp.repeat(steps, extent[axis_at] // blocks).reshape([-1 if axis == axis_at else 1 for axis in range(len(extent))])
    return gain


def gaussian(stream_key, shape, scale, bound, shards=(), dtype=jnp.bfloat16):
    gain = levels(stream_key, shape, shards, -0.22, 0.18) if shards else 1.0
    result = jax.random.normal(stream_key, shape, jnp.float32) * scale * gain
    return jnp.minimum(jnp.maximum(result, -bound), bound).astype(dtype)


def setup_inputs(seed: int = 0) -> dict:
    key_of = jax.random.split(jax.random.key(seed), 9)
    volume = gaussian(key_of[0], (VOLUMES, C0, NY, NZ, NX), 1.0, 6.0, ((0, 4), (2, 4), (3, 2)))
    pooled_first = gaussian(key_of[1], (VOLUMES, C1, NY // 2, NZ // 2, NX // 2), 1.0, 6.0, ((0, 4), (2, 4), (3, 2)))
    where_first = touch_ends(jax.random.randint(key_of[2], (VOLUMES, C1, NY // 2, NZ // 2, NX // 2), 0, 8), jax.random.fold_in(key_of[2], 1), 0, 7).astype(jnp.int32)
    pooled_second = gaussian(key_of[3], (VOLUMES, C2, NY // 4, NZ // 4, NX // 4), 1.0, 6.0, ((0, 4), (2, 4), (3, 2)))
    where_second = touch_ends(jax.random.randint(key_of[4], (VOLUMES, C2, NY // 4, NZ // 4, NX // 4), 0, 8), jax.random.fold_in(key_of[4], 1), 0, 7).astype(jnp.int32)
    upstream = gaussian(key_of[5], (VOLUMES, C2, NY // 4, NZ // 4, NX // 4), 1.0, 6.0, ((0, 4), (2, 4), (3, 2)))
    kernel_first = gaussian(key_of[6], (C1, C0, 3, 3, 3), (27 * C0) ** -0.5, 0.625)
    kernel_second = gaussian(key_of[7], (C2, C1, 3, 3, 3), (27 * C1) ** -0.5, 0.3125)
    return {"volume": volume, "pooled_first": pooled_first, "where_first": where_first, "pooled_second": pooled_second, "where_second": where_second, "upstream": upstream, "kernel_first": kernel_first, "kernel_second": kernel_second}


leak_rate = 0.3

def slope_of(pre):
    return jnp.where(pre > 0, 1.0, leak_rate).astype(jnp.float32)

def unpool(values, where):
    parts = [jnp.where(where == k, values, jnp.zeros_like(values)) for k in range(8)]
    stacked = jnp.stack(parts, axis=-1)
    b, c, y, z, x = values.shape
    stacked = stacked.reshape(b, c, y, z, x, 2, 2, 2)
    stacked = jnp.transpose(stacked, (0, 1, 2, 5, 3, 6, 4, 7))
    return stacked.reshape(b, c, 2 * y, 2 * z, 2 * x).astype(jnp.bfloat16)

def input_grad(grad, kernel):
    flipped = jnp.transpose(kernel[:, :, ::-1, ::-1, ::-1], (1, 0, 2, 3, 4)).astype(jnp.float32)
    return lax.conv_general_dilated(grad.astype(jnp.float32), flipped, (1, 1, 1), ((1, 1), (1, 1), (1, 1)), dimension_numbers=('NCDHW', 'OIDHW', 'NCDHW'), precision=lax.Precision.HIGHEST)

def weight_grad(grad, source):
    b, o, y, z, x = grad.shape
    padded = jnp.pad(source.astype(jnp.float32), ((0, 0), (0, 0), (1, 1), (1, 1), (1, 1)))
    upper = grad.astype(jnp.float32)
    taps = []
    for ty in range(3):
        for tz in range(3):
            for tx in range(3):
                shifted = padded[:, :, ty:ty + y, tz:tz + z, tx:tx + x]
                taps.append(jnp.einsum('boyzx,biyzx->oi', upper, shifted, precision=lax.Precision.HIGHEST))
    return jnp.stack(taps, axis=-1).reshape(-1)

def reference(volume, pooled_first, where_first, pooled_second, where_second, upstream, kernel_first, kernel_second):

    def one_volume(items):
        vol, first, wfirst, second, wsecond, grad_out = items
        vol, first, wfirst = (vol[None], first[None], wfirst[None])
        second, wsecond, grad_out = (second[None], wsecond[None], grad_out[None])
        grad_pre2 = unpool(grad_out.astype(jnp.float32) * slope_of(second), wsecond)
        first_f = first.astype(jnp.float32)
        input_second = jnp.where(first_f > 0, first_f, leak_rate * first_f).astype(jnp.bfloat16)
        second_grad = weight_grad(grad_pre2, input_second)
        grad_pooled = input_grad(grad_pre2, kernel_second)
        grad_pre1 = unpool(grad_pooled * slope_of(first), wfirst)
        first_grad = weight_grad(grad_pre1, vol)
        grad_vol = input_grad(grad_pre1, kernel_first).astype(jnp.bfloat16)
        return (grad_vol[0], first_grad, second_grad)
    grad_vol, first_all, second_all = lax.map(one_volume, (volume, pooled_first, where_first, pooled_second, where_second, upstream))
    total = VOLUMES * NY * NZ * NX
    first_out = lax.optimization_barrier(jnp.sum(first_all, axis=0)) * math.sqrt(8.0 / total)
    second_out = lax.optimization_barrier(jnp.sum(second_all, axis=0)) * math.sqrt(64.0 / total)
    return (grad_vol, first_out, second_out)
```

```python
import functools
import math

import jax
import jax.numpy as jnp
from jax import lax
from jax.experimental import pallas as pl
from jax.experimental.pallas import tpu as pltpu
from jax.sharding import PartitionSpec as P

leak_rate = 0.3
lanes = 128
f32, bf16 = jnp.float32, jnp.bfloat16


def dot(a, b):
    return lax.dot_general(a, b, (((1,), (0,)), ((), ())), preferred_element_type=f32)


def dot_nt(a, b):
    return lax.dot_general(a, b, (((1,), (1,)), ((), ())), preferred_element_type=f32)


def spread_matrix(first_row, count):
    row = lax.broadcasted_iota(jnp.int32, (lanes, lanes), 0)
    lane = lax.broadcasted_iota(jnp.int32, (lanes, lanes), 1)
    hit = (lane >> 1) + first_row == row
    return jnp.where(hit & (lane < 2 * count), 1.0, 0.0).astype(bf16)


def order_matrix(ins, step, outs, tap):
    row = lax.broadcasted_iota(jnp.int32, (3 * step, outs), 0)
    column = lax.broadcasted_iota(jnp.int32, (3 * step, outs), 1)
    hit = column == (row % step) * 27 + 3 * tap + row // step
    return jnp.where(hit & (row % step < ins), 1.0, 0.0).astype(bf16)


def main_kernel(
    sizes,
    side_ref,
    own_ref,
    ylow_ref,
    yhigh_ref,
    zlow_refs,
    zhigh_refs,
    volume_ref,
    first_ref,
    second_ref,
    grad_ref,
    sums_ref,
    up_ref,
    down_ref,
    cells_ref,
):
    ys, zs, xs, shards_dp, c1, c2 = sizes
    low_on, high_on = side_ref[0] > 0, side_ref[1] > 0

    def layer(refs, flag):
        return [jnp.where(flag, ref[...], jnp.zeros_like(ref[...])) for ref in refs]

    zlow, zhigh = layer(zlow_refs, low_on), layer(zhigh_refs, high_on)

    def half_row(y, z):
        if 0 <= z < zs:
            if y < 0:
                return ylow_ref[z]
            return own_ref[y, z] if y < ys else yhigh_ref[z]
        layers, at = (zlow, 1) if z < 0 else (zhigh, 0)
        if y < 0:
            return layers[1][ys - 1, at]
        return layers[0][y, at] if y < ys else layers[2][0, at]

    def quarter_row(y, z, part):
        if 0 <= z < zs // 2:
            if y < 0:
                return ylow_ref[2 * z + part]
            return own_ref[2 * y, 2 * z + part] if y < ys // 2 else yhigh_ref[2 * z + part]
        layers = zlow if z < 0 else zhigh
        if y < 0:
            return layers[1][ys - 1, part]
        return layers[0][2 * y, part] if y < ys // 2 else layers[2][0, part]

    lane = lax.broadcasted_iota(jnp.int32, (1, lanes), 1)
    parity = (lane & 1).astype(f32) + 1.0

    spread = spread_matrix(xs, xs // 2)
    for y in range(-1, ys // 2 + 1):
        zr = range(-1, zs // 2 + 1)
        values = dot(jnp.concatenate([quarter_row(y, z, 0) for z in zr], 0), spread)
        places = dot(jnp.concatenate([quarter_row(y, z, 1) for z in zr], 0), spread)
        for n, z in enumerate(zr):
            value, place = values[n * c2 : (n + 1) * c2], places[n * c2 : (n + 1) * c2]
            for dy in range(2):
                for dz in range(2):
                    up_ref[2 * y + 2 + dy, 2 * z + 2 + dz] = jnp.where(
                        place == parity + (4 * dy + 2 * dz), value, 0.0
                    ).astype(bf16)

    spread = spread_matrix(0, xs)
    weights = second_ref[...]
    second_sum = None
    for y in range(-1, ys + 1):
        zr = range(-1, zs + 1)
        around = jnp.concatenate(
            [
                jnp.concatenate([up_ref[y + 3 - ty, z + 3 - tz] for z in zr], 1)
                for ty in range(3)
                for tz in range(3)
            ],
            0,
        )
        terms = dot(weights, around)
        rows = [half_row(y, z) for z in zr]
        grads = []
        for n, row in enumerate(rows):
            at = slice(n * lanes, (n + 1) * lanes)
            pooled = row[:c1].astype(f32)
            total = (
                pltpu.roll(terms[:c1, at], lanes - 1, 1)
                + terms[c1 : 2 * c1, at]
                + pltpu.roll(terms[2 * c1 :, at], 1, 1)
            )
            grads.append((total * jnp.where(pooled > 0, 1.0, leak_rate)).astype(bf16))
        values = dot(jnp.concatenate(grads, 0), spread)
        places = dot(jnp.concatenate([row[c1:] for row in rows], 0), spread)
        for n, z in enumerate(zr):
            value, place = values[n * c1 : (n + 1) * c1], places[n * c1 : (n + 1) * c1]
            for dy in range(2):
                for dz in range(2):
                    down_ref[2 * y + 2 + dy, 2 * z + 2 + dz] = jnp.where(
                        place == parity + (4 * dy + 2 * dz), value, 0.0
                    ).astype(bf16)
        if 0 <= y < ys:
            inputs = []
            for row in rows[1:-1]:
                pooled = row[:c1].astype(f32)
                act = jnp.where(pooled > 0, pooled, leak_rate * pooled)
                act = jnp.where(lane < xs, act, 0.0).astype(bf16).astype(f32)
                inputs.append(
                    jnp.concatenate(
                        [pltpu.roll(act, 1, 1), act, pltpu.roll(act, lanes - 1, 1)], 0
                    ).astype(bf16)
                )
            term = dot_nt(around[:, lanes:-lanes], jnp.concatenate(inputs, 1))
            second_sum = term if second_sum is None else second_sum + term

    weights = first_ref[...]
    first_sum = None
    c0 = grad_ref.shape[0]
    for y in range(2 * ys):
        zr = range(2 * zs)
        around = jnp.concatenate(
            [
                jnp.concatenate([down_ref[y + 3 - ty, z + 3 - tz] for z in zr], 1)
                for ty in range(3)
                for tz in range(3)
            ],
            0,
        )
        terms = dot(weights, around)
        inputs = []
        for z in zr:
            at = slice(z * lanes, (z + 1) * lanes)
            left = jnp.where(lane < lanes - 1, pltpu.roll(terms[:8, at], lanes - 1, 1), 0.0)
            right = jnp.where(lane > 0, pltpu.roll(terms[16:, at], 1, 1), 0.0)
            total = left + terms[8:16, at] + right
            for i in range(c0):
                cells_ref[i, y, z : z + 1, :] = total[i : i + 1]
            cell = volume_ref[y, z].astype(f32)
            inputs.append(
                jnp.concatenate(
                    [
                        jnp.where(lane > 0, pltpu.roll(cell, 1, 1), 0.0),
                        cell,
                        jnp.where(lane < lanes - 1, pltpu.roll(cell, lanes - 1, 1), 0.0),
                    ],
                    0,
                ).astype(bf16)
            )
        term = dot_nt(around, jnp.concatenate(inputs, 1))
        first_sum = term if first_sum is None else first_sum + term
    grad_ref[...] = cells_ref[...].astype(bf16)

    first, second = 0.0, 0.0
    for tap in range(9):
        rows = first_sum[tap * c1 : (tap + 1) * c1].astype(bf16)
        first += dot(rows, order_matrix(c0, 8, lanes, tap))
        rows = second_sum[tap * c2 : (tap + 1) * c2].astype(bf16)
        second += dot(rows, order_matrix(c1, c1, 27 * c1, tap))
    keep1, keep2 = c1 // shards_dp, c2 // shards_dp
    wide = second.shape[1]
    pad = sums_ref.shape[2] - lanes - wide
    blank = jnp.zeros((keep2, pad), f32)
    for d in range(shards_dp):
        low = jnp.concatenate(
            [first[d * keep1 : (d + 1) * keep1], jnp.zeros((keep2 - keep1, lanes), f32)], 0
        )
        sums_ref[d] = jnp.concatenate(
            [second[d * keep2 : (d + 1) * keep2], blank, low], 1
        )


def shards(
    volume,
    pooled_first,
    where_first,
    pooled_second,
    where_second,
    upstream,
    kernel_first,
    kernel_second,
):
    dp, gy, gz = (lax.axis_size(a) for a in ("dp", "gy", "gz"))
    c0, c1, c2 = volume.shape[1], pooled_first.shape[1], pooled_second.shape[1]
    ys, zs, xs = pooled_first.shape[2:]

    slope = jnp.where(pooled_second[0] > 0, 1.0, leak_rate).astype(f32)
    value = (upstream[0].astype(f32) * slope).astype(bf16)
    place = (where_second[0] + 1).astype(bf16)
    quarter = jnp.transpose(jnp.stack([value, place]), (2, 3, 0, 1, 4))
    quarter = jnp.repeat(quarter.reshape(ys // 2, zs, c2, xs // 2), 2, axis=0)
    half = jnp.concatenate([pooled_first[0], (where_first[0] + 1).astype(bf16)], 0)
    half = jnp.transpose(half, (1, 2, 0, 3))
    blank = jnp.zeros((ys, zs, c2, lanes - xs - xs // 2), bf16)
    own = jnp.concatenate([half, quarter, blank], 3)

    up = [(i, i + 1) for i in range(gy - 1)]
    down = [(b, a) for a, b in up]
    ylow = lax.ppermute(own[ys - 1], "gy", up)
    yhigh = lax.ppermute(own[0], "gy", down)

    def around(block, pairs):
        def diagonal(shift):
            return [
                (y * gz + a, (y + shift) * gz + b)
                for a, b in pairs
                for y in range(gy)
                if 0 <= y + shift < gy
            ]

        return [
            lax.ppermute(block, "gz", pairs),
            lax.ppermute(block, ("gy", "gz"), diagonal(1)),
            lax.ppermute(block, ("gy", "gz"), diagonal(-1)),
        ]

    at = lax.axis_index("gz")
    if gz == 2:
        edge = jnp.where(at == 0, own[:, zs - 2 :], own[:, :2])
        zlow = zhigh = around(edge, [(0, 1), (1, 0)])
    else:
        ahead = [(i, i + 1) for i in range(gz - 1)]
        zlow = around(own[:, zs - 2 :], ahead)
        zhigh = around(own[:, :2], [(b, a) for a, b in ahead])
    side = jnp.stack([at > 0, at < gz - 1]).astype(jnp.int32)

    cells = jnp.transpose(volume[0], (1, 2, 0, 3))
    cells = jnp.pad(cells, ((0, 0), (0, 0), (0, 8 - c0), (0, 0)))
    first = jnp.transpose(kernel_first, (4, 1, 2, 3, 0))
    first = jnp.pad(first, ((0, 0), (0, 8 - c0), (0, 0), (0, 0), (0, 0)))
    first = first.reshape(24, 9 * c1)
    second = jnp.transpose(kernel_second, (4, 1, 2, 3, 0)).reshape(3 * c1, 9 * c2)

    width = -(-27 * c1 // lanes) * lanes + lanes
    vmem = pl.BlockSpec(memory_space=pltpu.VMEM)
    grad_vol, sums = pl.pallas_call(
        functools.partial(main_kernel, (ys, zs, xs, dp, c1, c2)),
        out_shape=(
            jax.ShapeDtypeStruct(volume.shape[1:], bf16),
            jax.ShapeDtypeStruct((dp, c2 // dp, width), f32),
        ),
        in_specs=[
            pl.BlockSpec(memory_space=pltpu.SMEM),
            vmem,
            vmem,
            vmem,
            [vmem] * 3,
            [vmem] * 3,
            vmem,
            vmem,
            vmem,
        ],
        out_specs=(vmem, vmem),
        scratch_shapes=[
            pltpu.VMEM((ys + 4, zs + 4, c2, lanes), bf16),
            pltpu.VMEM((2 * ys + 4, 2 * zs + 4, c1, lanes), bf16),
            pltpu.VMEM(volume.shape[1:], f32),
        ],
        compiler_params=pltpu.CompilerParams(vmem_limit_bytes=48 * 1024 * 1024),
        cost_estimate=pl.CostEstimate(
            flops=200_000_000, bytes_accessed=2_000_000, transcendentals=0
        ),
    )(side, own, ylow, yhigh, zlow, zhigh, cells, first, second)

    sent = jnp.broadcast_to(sums.astype(bf16)[:, None], (dp, gy * gz) + sums.shape[1:])
    sent = sent.reshape((dp * gy * gz,) + sums.shape[1:])
    got = lax.all_to_all(sent, ("dp", "gy", "gz"), 0, 0, tiled=True)
    total = jnp.sum(got.astype(f32), axis=0)
    count = volume.shape[2] * volume.shape[3] * volume.shape[4] * dp * gy * gz
    count *= volume.shape[0]
    first_out = total[: c1 // dp, width - lanes :][:, : 27 * c0].reshape(-1)
    second_out = total[:, : 27 * c1].reshape(-1)
    return (
        grad_vol[None],
        first_out * math.sqrt(8.0 / count),
        second_out * math.sqrt(64.0 / count),
    )


def solution(mesh):
    cells = P("dp", None, "gy", "gz", None)
    return jax.shard_map(
        shards,
        mesh=mesh,
        in_specs=(cells,) * 6 + (P(), P()),
        out_specs=(cells, P("dp"), P("dp")),
        check_vma=False,
    )
```

```python
import functools
import math

import jax
import jax.numpy as jnp
from jax import lax
from jax.experimental import pallas as pl
from jax.experimental.pallas import tpu as pltpu
from jax.sharding import PartitionSpec as P

leak_rate = 0.3
lanes = 128
f32, bf16 = jnp.float32, jnp.bfloat16


def dot(a, b):
    return lax.dot_general(a, b, (((1,), (0,)), ((), ())), preferred_element_type=f32)


def dot_nt(a, b):
    return lax.dot_general(a, b, (((1,), (1,)), ((), ())), preferred_element_type=f32)


def spread_matrix(first_row, count):
    row = lax.broadcasted_iota(jnp.int32, (lanes, lanes), 0)
    lane = lax.broadcasted_iota(jnp.int32, (lanes, lanes), 1)
    hit = (lane >> 1) + first_row == row
    return jnp.where(hit & (lane < 2 * count), 1.0, 0.0).astype(bf16)


def order_matrix(ins, step, outs, tap):
    row = lax.broadcasted_iota(jnp.int32, (3 * step, outs), 0)
    column = lax.broadcasted_iota(jnp.int32, (3 * step, outs), 1)
    hit = column == (row % step) * 27 + 3 * tap + row // step
    return jnp.where(hit & (row % step < ins), 1.0, 0.0).astype(bf16)


def main_kernel(
    sizes,
    side_ref,
    own_ref,
    ylow_ref,
    yhigh_ref,
    zlow_refs,
    zhigh_refs,
    volume_ref,
    first_ref,
    second_ref,
    grad_ref,
    sums_ref,
    up_ref,
    down_ref,
    cells_ref,
):
    ys, zs, xs, shards_dp, c1, c2 = sizes
    low_on, high_on = side_ref[0] > 0, side_ref[1] > 0

    def layer(refs, flag):
        return [jnp.where(flag, ref[...], jnp.zeros_like(ref[...])) for ref in refs]

    zlow, zhigh = layer(zlow_refs, low_on), layer(zhigh_refs, high_on)

    def half_row(y, z):
        if 0 <= z < zs:
            if y < 0:
                return ylow_ref[z]
            return own_ref[y, z] if y < ys else yhigh_ref[z]
        layers, at = (zlow, 1) if z < 0 else (zhigh, 0)
        if y < 0:
            return layers[1][ys - 1, at]
        return layers[0][y, at] if y < ys else layers[2][0, at]

    def quarter_row(y, z, part):
        if 0 <= z < zs // 2:
            if y < 0:
                return ylow_ref[2 * z + part]
            return own_ref[2 * y, 2 * z + part] if y < ys // 2 else yhigh_ref[2 * z + part]
        layers = zlow if z < 0 else zhigh
        if y < 0:
            return layers[1][ys - 1, part]
        return layers[0][2 * y, part] if y < ys // 2 else layers[2][0, part]

    lane = lax.broadcasted_iota(jnp.int32, (1, lanes), 1)
    parity = (lane & 1).astype(f32) + 1.0

    spread = spread_matrix(xs, xs // 2)
    for y in range(-1, ys // 2 + 1):
        zr = range(-1, zs // 2 + 1)
        values = dot(jnp.concatenate([quarter_row(y, z, 0) for z in zr], 0), spread)
        places = dot(jnp.concatenate([quarter_row(y, z, 1) for z in zr], 0), spread)
        for n, z in enumerate(zr):
            value, place = values[n * c2 : (n + 1) * c2], places[n * c2 : (n + 1) * c2]
            for dy in range(2):
                for dz in range(2):
                    up_ref[2 * y + 2 + dy, 2 * z + 2 + dz] = jnp.where(
                        place == parity + (4 * dy + 2 * dz), value, 0.0
                    ).astype(bf16)

    spread = spread_matrix(0, xs)
    weights = second_ref[...]
    second_sum = None
    for y in range(-1, ys + 1):
        zr = range(-1, zs + 1)
        around = jnp.concatenate(
            [
                jnp.concatenate([up_ref[y + 3 - ty, z + 3 - tz] for z in zr], 1)
                for ty in range(3)
                for tz in range(3)
            ],
            0,
        )
        terms = dot(weights, around)
        rows = [half_row(y, z) for z in zr]
        grads = []
        for n, row in enumerate(rows):
            at = slice(n * lanes, (n + 1) * lanes)
            pooled = row[:c1].astype(f32)
            total = (
                pltpu.roll(terms[:c1, at], lanes - 1, 1)
                + terms[c1 : 2 * c1, at]
                + pltpu.roll(terms[2 * c1 :, at], 1, 1)
            )
            grads.append((total * jnp.where(pooled > 0, 1.0, leak_rate)).astype(bf16))
        values = dot(jnp.concatenate(grads, 0), spread)
        places = dot(jnp.concatenate([row[c1:] for row in rows], 0), spread)
        for n, z in enumerate(zr):
            value, place = values[n * c1 : (n + 1) * c1], places[n * c1 : (n + 1) * c1]
            for dy in range(2):
                for dz in range(2):
                    down_ref[2 * y + 2 + dy, 2 * z + 2 + dz] = jnp.where(
                        place == parity + (4 * dy + 2 * dz), value, 0.0
                    ).astype(bf16)
        if 0 <= y < ys:
            inputs = []
            for row in rows[1:-1]:
                pooled = row[:c1].astype(f32)
                act = jnp.where(pooled > 0, pooled, leak_rate * pooled)
                act = jnp.where(lane < xs, act, 0.0).astype(bf16).astype(f32)
                inputs.append(
                    jnp.concatenate(
                        [pltpu.roll(act, 1, 1), act, pltpu.roll(act, lanes - 1, 1)], 0
                    ).astype(bf16)
                )
            term = dot_nt(around[:, lanes:-lanes], jnp.concatenate(inputs, 1))
            second_sum = term if second_sum is None else second_sum + term

    weights = first_ref[...]
    first_sum = None
    c0 = grad_ref.shape[0]
    for y in range(2 * ys):
        zr = range(2 * zs)
        around = jnp.concatenate(
            [
                jnp.concatenate([down_ref[y + 3 - ty, z + 3 - tz] for z in zr], 1)
                for ty in range(3)
                for tz in range(3)
            ],
            0,
        )
        terms = dot(weights, around)
        inputs = []
        for z in zr:
            at = slice(z * lanes, (z + 1) * lanes)
            left = jnp.where(lane < lanes - 1, pltpu.roll(terms[:8, at], lanes - 1, 1), 0.0)
            right = jnp.where(lane > 0, pltpu.roll(terms[16:, at], 1, 1), 0.0)
            total = left + terms[8:16, at] + right
            for i in range(c0):
                cells_ref[i, y, z : z + 1, :] = total[i : i + 1]
            cell = volume_ref[y, z].astype(f32)
            inputs.append(
                jnp.concatenate(
                    [
                        jnp.where(lane > 0, pltpu.roll(cell, 1, 1), 0.0),
                        cell,
                        jnp.where(lane < lanes - 1, pltpu.roll(cell, lanes - 1, 1), 0.0),
                    ],
                    0,
                ).astype(bf16)
            )
        term = dot_nt(around, jnp.concatenate(inputs, 1))
        first_sum = term if first_sum is None else first_sum + term
    grad_ref[...] = cells_ref[...].astype(bf16)

    first, second = 0.0, 0.0
    for tap in range(9):
        rows = first_sum[tap * c1 : (tap + 1) * c1].astype(bf16)
        first += dot(rows, order_matrix(c0, 8, lanes, tap))
        rows = second_sum[tap * c2 : (tap + 1) * c2].astype(bf16)
        second += dot(rows, order_matrix(c1, c1, 27 * c1, tap))
    keep1, keep2 = c1 // shards_dp, c2 // shards_dp
    wide = second.shape[1]
    pad = sums_ref.shape[2] - lanes - wide
    blank = jnp.zeros((keep2, pad), f32)
    for d in range(shards_dp):
        low = jnp.concatenate(
            [first[d * keep1 : (d + 1) * keep1], jnp.zeros((keep2 - keep1, lanes), f32)], 0
        )
        sums_ref[d] = jnp.concatenate(
            [second[d * keep2 : (d + 1) * keep2], blank, low], 1
        )


def shards(
    volume,
    pooled_first,
    where_first,
    pooled_second,
    where_second,
    upstream,
    kernel_first,
    kernel_second,
):
    dp, gy, gz = (lax.axis_size(a) for a in ("dp", "gy", "gz"))
    c0, c1, c2 = volume.shape[1], pooled_first.shape[1], pooled_second.shape[1]
    ys, zs, xs = pooled_first.shape[2:]

    slope = jnp.where(pooled_second[0] > 0, 1.0, leak_rate).astype(f32)
    value = (upstream[0].astype(f32) * slope).astype(bf16)
    place = (where_second[0] + 1).astype(bf16)
    quarter = jnp.transpose(jnp.stack([value, place]), (2, 3, 0, 1, 4))
    quarter = jnp.repeat(quarter.reshape(ys // 2, zs, c2, xs // 2), 2, axis=0)
    half = jnp.concatenate([pooled_first[0], (where_first[0] + 1).astype(bf16)], 0)
    half = jnp.transpose(half, (1, 2, 0, 3))
    blank = jnp.zeros((ys, zs, c2, lanes - xs - xs // 2), bf16)
    own = jnp.concatenate([half, quarter, blank], 3)

    up = [(i, i + 1) for i in range(gy - 1)]
    down = [(b, a) for a, b in up]
    ylow = lax.ppermute(own[ys - 1], "gy", up)
    yhigh = lax.ppermute(own[0], "gy", down)

    def around(block, pairs):
        def diagonal(shift):
            return [
                (y * gz + a, (y + shift) * gz + b)
                for a, b in pairs
                for y in range(gy)
                if 0 <= y + shift < gy
            ]

        return [
            lax.ppermute(block, "gz", pairs),
            lax.ppermute(block, ("gy", "gz"), diagonal(1)),
            lax.ppermute(block, ("gy", "gz"), diagonal(-1)),
        ]

    at = lax.axis_index("gz")
    if gz == 2:
        edge = jnp.where(at == 0, own[:, zs - 2 :], own[:, :2])
        zlow = zhigh = around(edge, [(0, 1), (1, 0)])
    else:
        ahead = [(i, i + 1) for i in range(gz - 1)]
        zlow = around(own[:, zs - 2 :], ahead)
        zhigh = around(own[:, :2], [(b, a) for a, b in ahead])
    side = jnp.stack([at > 0, at < gz - 1]).astype(jnp.int32)

    cells = jnp.transpose(volume[0], (1, 2, 0, 3))
    cells = jnp.pad(cells, ((0, 0), (0, 0), (0, 8 - c0), (0, 0)))
    first = jnp.transpose(kernel_first, (4, 1, 2, 3, 0))
    first = jnp.pad(first, ((0, 0), (0, 8 - c0), (0, 0), (0, 0), (0, 0)))
    first = first.reshape(24, 9 * c1)
    second = jnp.transpose(kernel_second, (4, 1, 2, 3, 0)).reshape(3 * c1, 9 * c2)

    width = -(-27 * c1 // lanes) * lanes + lanes
    vmem = pl.BlockSpec(memory_space=pltpu.VMEM)
    grad_vol, sums = pl.pallas_call(
        functools.partial(main_kernel, (ys, zs, xs, dp, c1, c2)),
        out_shape=(
            jax.ShapeDtypeStruct(volume.shape[1:], bf16),
            jax.ShapeDtypeStruct((dp, c2 // dp, width), f32),
        ),
        in_specs=[
            pl.BlockSpec(memory_space=pltpu.SMEM),
            vmem,
            vmem,
            vmem,
            [vmem] * 3,
            [vmem] * 3,
            vmem,
            vmem,
            vmem,
        ],
        out_specs=(vmem, vmem),
        scratch_shapes=[
            pltpu.VMEM((ys + 4, zs + 4, c2, lanes), bf16),
            pltpu.VMEM((2 * ys + 4, 2 * zs + 4, c1, lanes), bf16),
            pltpu.VMEM(volume.shape[1:], f32),
        ],
        compiler_params=pltpu.CompilerParams(vmem_limit_bytes=48 * 1024 * 1024),
        cost_estimate=pl.CostEstimate(
            flops=200_000_000, bytes_accessed=2_000_000, transcendentals=0
        ),
    )(side, own, ylow, yhigh, zlow, zhigh, cells, first, second)

    got = lax.all_to_all(sums.astype(bf16), "dp", 0, 0, tiled=True)
    part = jnp.sum(got.astype(f32), axis=0).astype(bf16)
    sent = jnp.broadcast_to(part[None], (gy * gz,) + part.shape)
    got = lax.all_to_all(sent, ("gy", "gz"), 0, 0, tiled=True)
    total = jnp.sum(got.astype(f32), axis=0)
    count = volume.shape[2] * volume.shape[3] * volume.shape[4] * dp * gy * gz
    count *= volume.shape[0]
    first_out = total[: c1 // dp, width - lanes :][:, : 27 * c0].reshape(-1)
    second_out = total[:, : 27 * c1].reshape(-1)
    return (
        grad_vol[None],
        first_out * math.sqrt(8.0 / count),
        second_out * math.sqrt(64.0 / count),
    )


def solution(mesh):
    cells = P("dp", None, "gy", "gz", None)
    return jax.shard_map(
        shards,
        mesh=mesh,
        in_specs=(cells,) * 6 + (P(), P()),
        out_specs=(cells, P("dp"), P("dp")),
        check_vma=False,
    )
```

```python
import functools
import math

import jax
import jax.numpy as jnp
from jax import lax
from jax.experimental import pallas as pl
from jax.experimental.pallas import tpu as pltpu
from jax.sharding import PartitionSpec as P

leak_rate = 0.3
lanes = 128
f32, bf16 = jnp.float32, jnp.bfloat16


def dot(a, b):
    return lax.dot_general(a, b, (((1,), (0,)), ((), ())), preferred_element_type=f32)


def dot_nt(a, b):
    return lax.dot_general(a, b, (((1,), (1,)), ((), ())), preferred_element_type=f32)


def spread_matrix(first_row, count):
    row = lax.broadcasted_iota(jnp.int32, (lanes, lanes), 0)
    lane = lax.broadcasted_iota(jnp.int32, (lanes, lanes), 1)
    hit = (lane >> 1) + first_row == row
    return jnp.where(hit & (lane < 2 * count), 1.0, 0.0).astype(bf16)


def order_matrix(ins, step, outs, tap):
    row = lax.broadcasted_iota(jnp.int32, (3 * step, outs), 0)
    column = lax.broadcasted_iota(jnp.int32, (3 * step, outs), 1)
    hit = column == (row % step) * 27 + 3 * tap + row // step
    return jnp.where(hit & (row % step < ins), 1.0, 0.0).astype(bf16)


def rows_of(count):
    return -(-count // lanes)


def lay_flat(values, length, keep, base, out_ref):
    shards_dp = out_ref.shape[0]
    out_ref[:, base : base + rows_of(length * keep)] = jnp.zeros(
        (shards_dp, rows_of(length * keep), lanes), f32
    )
    for d in range(shards_dp):
        for k in range(keep):
            row = values[d * keep + k : d * keep + k + 1]
            start = length * k % lanes
            total = rows_of(start + length)
            width = total * lanes
            if row.shape[1] < width:
                row = jnp.concatenate(
                    [row, jnp.zeros((1, width - row.shape[1]), f32)], 1
                )
            row = pltpu.roll(row, start, 1) if start else row
            top = base + length * k // lanes
            for t in range(total):
                out_ref[d, top + t : top + t + 1] += row[:, t * lanes : (t + 1) * lanes]


def main_kernel(
    sizes,
    side_ref,
    own_ref,
    ylow_ref,
    yhigh_ref,
    zlow_refs,
    zhigh_refs,
    volume_ref,
    first_ref,
    second_ref,
    grad_ref,
    sums_ref,
    up_ref,
    down_ref,
    cells_ref,
):
    ys, zs, xs, shards_dp, c1, c2 = sizes
    low_on, high_on = side_ref[0] > 0, side_ref[1] > 0

    def layer(refs, flag):
        return [jnp.where(flag, ref[...], jnp.zeros_like(ref[...])) for ref in refs]

    zlow, zhigh = layer(zlow_refs, low_on), layer(zhigh_refs, high_on)

    def half_row(y, z):
        if 0 <= z < zs:
            if y < 0:
                return ylow_ref[z]
            return own_ref[y, z] if y < ys else yhigh_ref[z]
        layers, at = (zlow, 1) if z < 0 else (zhigh, 0)
        if y < 0:
            return layers[1][ys - 1, at]
        return layers[0][y, at] if y < ys else layers[2][0, at]

    def quarter_row(y, z, part):
        if 0 <= z < zs // 2:
            if y < 0:
                return ylow_ref[2 * z + part]
            return own_ref[2 * y, 2 * z + part] if y < ys // 2 else yhigh_ref[2 * z + part]
        layers = zlow if z < 0 else zhigh
        if y < 0:
            return layers[1][ys - 1, part]
        return layers[0][2 * y, part] if y < ys // 2 else layers[2][0, part]

    lane = lax.broadcasted_iota(jnp.int32, (1, lanes), 1)
    parity = (lane & 1).astype(f32) + 1.0

    spread = spread_matrix(xs, xs // 2)
    for y in range(-1, ys // 2 + 1):
        zr = range(-1, zs // 2 + 1)
        values = dot(jnp.concatenate([quarter_row(y, z, 0) for z in zr], 0), spread)
        places = dot(jnp.concatenate([quarter_row(y, z, 1) for z in zr], 0), spread)
        for n, z in enumerate(zr):
            value, place = values[n * c2 : (n + 1) * c2], places[n * c2 : (n + 1) * c2]
            for dy in range(2):
                for dz in range(2):
                    up_ref[2 * y + 2 + dy, 2 * z + 2 + dz] = jnp.where(
                        place == parity + (4 * dy + 2 * dz), value, 0.0
                    ).astype(bf16)

    spread = spread_matrix(0, xs)
    weights = second_ref[...]
    second_sum = None
    for y in range(-1, ys + 1):
        zr = range(-1, zs + 1)
        around = jnp.concatenate(
            [
                jnp.concatenate([up_ref[y + 3 - ty, z + 3 - tz] for z in zr], 1)
                for ty in range(3)
                for tz in range(3)
            ],
            0,
        )
        terms = dot(weights, around)
        rows = [half_row(y, z) for z in zr]
        grads = []
        for n, row in enumerate(rows):
            at = slice(n * lanes, (n + 1) * lanes)
            pooled = row[:c1].astype(f32)
            total = (
                pltpu.roll(terms[:c1, at], lanes - 1, 1)
                + terms[c1 : 2 * c1, at]
                + pltpu.roll(terms[2 * c1 :, at], 1, 1)
            )
            grads.append((total * jnp.where(pooled > 0, 1.0, leak_rate)).astype(bf16))
        values = dot(jnp.concatenate(grads, 0), spread)
        places = dot(jnp.concatenate([row[c1:] for row in rows], 0), spread)
        for n, z in enumerate(zr):
            value, place = values[n * c1 : (n + 1) * c1], places[n * c1 : (n + 1) * c1]
            for dy in range(2):
                for dz in range(2):
                    down_ref[2 * y + 2 + dy, 2 * z + 2 + dz] = jnp.where(
                        place == parity + (4 * dy + 2 * dz), value, 0.0
                    ).astype(bf16)
        if 0 <= y < ys:
            inputs = []
            for row in rows[1:-1]:
                pooled = row[:c1].astype(f32)
                act = jnp.where(pooled > 0, pooled, leak_rate * pooled)
                act = jnp.where(lane < xs, act, 0.0).astype(bf16).astype(f32)
                inputs.append(
                    jnp.concatenate(
                        [pltpu.roll(act, 1, 1), act, pltpu.roll(act, lanes - 1, 1)], 0
                    ).astype(bf16)
                )
            term = dot_nt(around[:, lanes:-lanes], jnp.concatenate(inputs, 1))
            second_sum = term if second_sum is None else second_sum + term

    weights = first_ref[...]
    first_sum = None
    c0 = grad_ref.shape[0]
    for y in range(2 * ys):
        zr = range(2 * zs)
        around = jnp.concatenate(
            [
                jnp.concatenate([down_ref[y + 3 - ty, z + 3 - tz] for z in zr], 1)
                for ty in range(3)
                for tz in range(3)
            ],
            0,
        )
        terms = dot(weights, around)
        inputs = []
        for z in zr:
            at = slice(z * lanes, (z + 1) * lanes)
            left = jnp.where(lane < lanes - 1, pltpu.roll(terms[:8, at], lanes - 1, 1), 0.0)
            right = jnp.where(lane > 0, pltpu.roll(terms[16:, at], 1, 1), 0.0)
            total = left + terms[8:16, at] + right
            for i in range(c0):
                cells_ref[i, y, z : z + 1, :] = total[i : i + 1]
            cell = volume_ref[y, z].astype(f32)
            inputs.append(
                jnp.concatenate(
                    [
                        jnp.where(lane > 0, pltpu.roll(cell, 1, 1), 0.0),
                        cell,
                        jnp.where(lane < lanes - 1, pltpu.roll(cell, lanes - 1, 1), 0.0),
                    ],
                    0,
                ).astype(bf16)
            )
        term = dot_nt(around, jnp.concatenate(inputs, 1))
        first_sum = term if first_sum is None else first_sum + term
    grad_ref[...] = cells_ref[...].astype(bf16)

    first, second = 0.0, 0.0
    for tap in range(9):
        rows = first_sum[tap * c1 : (tap + 1) * c1].astype(bf16)
        first += dot(rows, order_matrix(c0, 8, lanes, tap))
        rows = second_sum[tap * c2 : (tap + 1) * c2].astype(bf16)
        second += dot(rows, order_matrix(c1, c1, rows_of(27 * c1) * lanes, tap))
    lay_flat(second, 27 * c1, c2 // shards_dp, 0, sums_ref)
    lay_flat(first, 27 * c0, c1 // shards_dp, rows_of(27 * c1 * c2 // shards_dp), sums_ref)


def shards(
    volume,
    pooled_first,
    where_first,
    pooled_second,
    where_second,
    upstream,
    kernel_first,
    kernel_second,
):
    dp, gy, gz = (lax.axis_size(a) for a in ("dp", "gy", "gz"))
    c0, c1, c2 = volume.shape[1], pooled_first.shape[1], pooled_second.shape[1]
    ys, zs, xs = pooled_first.shape[2:]

    slope = jnp.where(pooled_second[0] > 0, 1.0, leak_rate).astype(f32)
    value = (upstream[0].astype(f32) * slope).astype(bf16)
    place = (where_second[0] + 1).astype(bf16)
    quarter = jnp.transpose(jnp.stack([value, place]), (2, 3, 0, 1, 4))
    quarter = jnp.repeat(quarter.reshape(ys // 2, zs, c2, xs // 2), 2, axis=0)
    half = jnp.concatenate([pooled_first[0], (where_first[0] + 1).astype(bf16)], 0)
    half = jnp.transpose(half, (1, 2, 0, 3))
    blank = jnp.zeros((ys, zs, c2, lanes - xs - xs // 2), bf16)
    own = jnp.concatenate([half, quarter, blank], 3)

    up = [(i, i + 1) for i in range(gy - 1)]
    down = [(b, a) for a, b in up]
    ylow = lax.ppermute(own[ys - 1], "gy", up)
    yhigh = lax.ppermute(own[0], "gy", down)

    def around(block, pairs):
        def diagonal(shift):
            return [
                (y * gz + a, (y + shift) * gz + b)
                for a, b in pairs
                for y in range(gy)
                if 0 <= y + shift < gy
            ]

        return [
            lax.ppermute(block, "gz", pairs),
            lax.ppermute(block, ("gy", "gz"), diagonal(1)),
            lax.ppermute(block, ("gy", "gz"), diagonal(-1)),
        ]

    at = lax.axis_index("gz")
    if gz == 2:
        edge = jnp.where(at == 0, own[:, zs - 2 :], own[:, :2])
        zlow = zhigh = around(edge, [(0, 1), (1, 0)])
    else:
        ahead = [(i, i + 1) for i in range(gz - 1)]
        zlow = around(own[:, zs - 2 :], ahead)
        zhigh = around(own[:, :2], [(b, a) for a, b in ahead])
    side = jnp.stack([at > 0, at < gz - 1]).astype(jnp.int32)

    cells = jnp.transpose(volume[0], (1, 2, 0, 3))
    cells = jnp.pad(cells, ((0, 0), (0, 0), (0, 8 - c0), (0, 0)))
    first = jnp.transpose(kernel_first, (4, 1, 2, 3, 0))
    first = jnp.pad(first, ((0, 0), (0, 8 - c0), (0, 0), (0, 0), (0, 0)))
    first = first.reshape(24, 9 * c1)
    second = jnp.transpose(kernel_second, (4, 1, 2, 3, 0)).reshape(3 * c1, 9 * c2)

    sizes1, sizes2 = 27 * c0 * c1 // dp, 27 * c1 * c2 // dp
    sum_rows = -(-(rows_of(sizes1) + rows_of(sizes2)) // 8) * 8
    vmem = pl.BlockSpec(memory_space=pltpu.VMEM)
    grad_vol, sums = pl.pallas_call(
        functools.partial(main_kernel, (ys, zs, xs, dp, c1, c2)),
        out_shape=(
            jax.ShapeDtypeStruct(volume.shape[1:], bf16),
            jax.ShapeDtypeStruct((dp, sum_rows, lanes), f32),
        ),
        in_specs=[
            pl.BlockSpec(memory_space=pltpu.SMEM),
            vmem,
            vmem,
            vmem,
            [vmem] * 3,
            [vmem] * 3,
            vmem,
            vmem,
            vmem,
        ],
        out_specs=(vmem, vmem),
        scratch_shapes=[
            pltpu.VMEM((ys + 4, zs + 4, c2, lanes), bf16),
            pltpu.VMEM((2 * ys + 4, 2 * zs + 4, c1, lanes), bf16),
            pltpu.VMEM(volume.shape[1:], f32),
        ],
        compiler_params=pltpu.CompilerParams(vmem_limit_bytes=48 * 1024 * 1024),
        cost_estimate=pl.CostEstimate(
            flops=200_000_000, bytes_accessed=2_000_000, transcendentals=0
        ),
    )(side, own, ylow, yhigh, zlow, zhigh, cells, first, second)

    at = lax.axis_index("dp")
    half = dp // 2
    while half:
        pairs = [(i, i ^ half) for i in range(dp)]
        upper = (at & half) > 0
        mine = jnp.where(upper, sums[half:], sums[:half])
        sums = mine + lax.ppermute(jnp.where(upper, sums[:half], sums[half:]), "dp", pairs)
        half //= 2
    total = sums[0]
    for axis, size in (("gz", gz), ("gy", gy)):
        half = 1
        while half < size:
            total = total + lax.ppermute(total, axis, [(i, i ^ half) for i in range(size)])
            half *= 2
    count = volume.shape[2] * volume.shape[3] * volume.shape[4] * dp * gy * gz
    count *= volume.shape[0]
    split = rows_of(sizes2)
    second_out = total[:split].reshape(-1)[:sizes2]
    first_out = total[split : split + rows_of(sizes1)].reshape(-1)[:sizes1]
    return (
        grad_vol[None],
        first_out * math.sqrt(8.0 / count),
        second_out * math.sqrt(64.0 / count),
    )


def solution(mesh):
    cells = P("dp", None, "gy", "gz", None)
    return jax.shard_map(
        shards,
        mesh=mesh,
        in_specs=(cells,) * 6 + (P(), P()),
        out_specs=(cells, P("dp"), P("dp")),
        check_vma=False,
    )
```

```python
import functools
import math

import jax
import jax.numpy as jnp
from jax import lax
from jax.experimental import pallas as pl
from jax.experimental.pallas import tpu as pltpu
from jax.sharding import PartitionSpec as P

leak_rate = 0.3
lanes = 128
f32, bf16 = jnp.float32, jnp.bfloat16


def dot(a, b):
    return lax.dot_general(a, b, (((1,), (0,)), ((), ())), preferred_element_type=f32)


def dot_nt(a, b):
    return lax.dot_general(a, b, (((1,), (1,)), ((), ())), preferred_element_type=f32)


def spread_matrix(first_row, count):
    row = lax.broadcasted_iota(jnp.int32, (lanes, lanes), 0)
    lane = lax.broadcasted_iota(jnp.int32, (lanes, lanes), 1)
    hit = (lane >> 1) + first_row == row
    return jnp.where(hit & (lane < 2 * count), 1.0, 0.0).astype(bf16)


def order_matrix(ins, step, outs, tap):
    row = lax.broadcasted_iota(jnp.int32, (3 * step, outs), 0)
    column = lax.broadcasted_iota(jnp.int32, (3 * step, outs), 1)
    hit = column == (row % step) * 27 + 3 * tap + row // step
    return jnp.where(hit & (row % step < ins), 1.0, 0.0).astype(bf16)


def rows_of(count):
    return -(-count // lanes)


def lay_flat(values, length, keep, base, out_ref):
    shards_dp = out_ref.shape[0]
    for d in range(shards_dp):
        for k in range(keep):
            row = values[d * keep + k : d * keep + k + 1]
            start = length * k % lanes
            total = rows_of(start + length)
            width = total * lanes
            if row.shape[1] < width:
                row = jnp.concatenate(
                    [row, jnp.zeros((1, width - row.shape[1]), f32)], 1
                )
            row = pltpu.roll(row, start, 1) if start else row
            top = base + length * k // lanes
            for t in range(total):
                out_ref[d, top + t : top + t + 1] += row[:, t * lanes : (t + 1) * lanes]


def main_kernel(
    sizes,
    odd_ref,
    own_ref,
    rim_refs,
    plane_refs,
    volume_ref,
    first_ref,
    second_ref,
    grad_ref,
    sums_ref,
    up_ref,
    down_ref,
    cells_ref,
    flat_ref,
):
    ys, zs, xs, c1, c2 = sizes
    odd_z, odd_y = odd_ref[0] > 0, odd_ref[1] > 0

    def sides(even, odd, flag):
        return jnp.where(flag, even, odd), jnp.where(flag, odd, even)

    def rims(even, odd):
        return sides(even, odd, odd_z)

    def second_of(refs):
        return refs[1][...] if len(refs) > 1 else jnp.zeros(refs[0].shape, bf16)

    nothing = jnp.zeros(rim_refs[0].shape, bf16)
    zlow, zhigh = rims(rim_refs[0][...], second_of(rim_refs))
    ylow, yhigh = sides(plane_refs[0][...], second_of(plane_refs), odd_y)
    ylow_rims = rims(ylow[zs : zs + 2], ylow[zs + 2 :] if len(rim_refs) > 1 else nothing)
    yhigh_rims = rims(yhigh[zs : zs + 2], yhigh[zs + 2 :] if len(rim_refs) > 1 else nothing)

    def half_row(y, z):
        if 0 <= z < zs:
            if y < 0:
                return ylow[z]
            return own_ref[y, z] if y < ys else yhigh[z]
        side = 0 if z < 0 else 1
        if y < 0:
            return ylow_rims[side][ys - 1]
        return (zlow, zhigh)[side][y] if y < ys else yhigh_rims[side][0]

    def quarter_row(y, z, part):
        if 0 <= z < zs // 2:
            if y < 0:
                return ylow[2 * z + part]
            return own_ref[0, 2 * z + part] if y < 1 else yhigh[2 * z + part]
        side = 0 if z < 0 else 1
        if y < 0:
            return ylow_rims[side][part]
        return (zlow, zhigh)[side][part] if y < 1 else yhigh_rims[side][part]

    lane = lax.broadcasted_iota(jnp.int32, (1, lanes), 1)
    parity = (lane & 1).astype(f32) + 1.0

    spread = spread_matrix(xs, xs // 2)
    for y in range(-1, ys // 2 + 1):
        zr = range(-1, zs // 2 + 1)
        values = dot(jnp.concatenate([quarter_row(y, z, 0) for z in zr], 0), spread)
        places = dot(jnp.concatenate([quarter_row(y, z, 1) for z in zr], 0), spread)
        for n, z in enumerate(zr):
            value, place = values[n * c2 : (n + 1) * c2], places[n * c2 : (n + 1) * c2]
            for dy in range(2):
                for dz in range(2):
                    up_ref[2 * y + 2 + dy, 2 * z + 2 + dz] = jnp.where(
                        place == parity + (4 * dy + 2 * dz), value, 0.0
                    ).astype(bf16)

    spread = spread_matrix(0, xs)
    weights = second_ref[...]
    second_sum = None
    for y in range(-1, ys + 1):
        zr = range(-1, zs + 1)
        around = jnp.concatenate(
            [
                jnp.concatenate([up_ref[y + 3 - ty, z + 3 - tz] for z in zr], 1)
                for ty in range(3)
                for tz in range(3)
            ],
            0,
        )
        terms = dot(weights, around)
        rows = [half_row(y, z) for z in zr]
        grads = []
        for n, row in enumerate(rows):
            at = slice(n * lanes, (n + 1) * lanes)
            pooled = row[:c1].astype(f32)
            total = (
                pltpu.roll(terms[:c1, at], lanes - 1, 1)
                + terms[c1 : 2 * c1, at]
                + pltpu.roll(terms[2 * c1 :, at], 1, 1)
            )
            grads.append((total * jnp.where(pooled > 0, 1.0, leak_rate)).astype(bf16))
        values = dot(jnp.concatenate(grads, 0), spread)
        places = dot(jnp.concatenate([row[c1:] for row in rows], 0), spread)
        for n, z in enumerate(zr):
            value, place = values[n * c1 : (n + 1) * c1], places[n * c1 : (n + 1) * c1]
            for dy in range(2):
                for dz in range(2):
                    down_ref[2 * y + 2 + dy, 2 * z + 2 + dz] = jnp.where(
                        place == parity + (4 * dy + 2 * dz), value, 0.0
                    ).astype(bf16)
        if 0 <= y < ys:
            inputs = []
            for row in rows[1:-1]:
                pooled = row[:c1].astype(f32)
                act = jnp.where(pooled > 0, pooled, leak_rate * pooled)
                act = jnp.where(lane < xs, act, 0.0).astype(bf16).astype(f32)
                inputs.append(
                    jnp.concatenate(
                        [pltpu.roll(act, 1, 1), act, pltpu.roll(act, lanes - 1, 1)], 0
                    ).astype(bf16)
                )
            term = dot_nt(around[:, lanes:-lanes], jnp.concatenate(inputs, 1))
            second_sum = term if second_sum is None else second_sum + term

    weights = first_ref[...]
    first_sum = None
    c0 = grad_ref.shape[0]
    for y in range(2 * ys):
        zr = range(2 * zs)
        around = jnp.concatenate(
            [
                jnp.concatenate([down_ref[y + 3 - ty, z + 3 - tz] for z in zr], 1)
                for ty in range(3)
                for tz in range(3)
            ],
            0,
        )
        terms = dot(weights, around)
        inputs = []
        for z in zr:
            at = slice(z * lanes, (z + 1) * lanes)
            left = jnp.where(lane < lanes - 1, pltpu.roll(terms[:8, at], lanes - 1, 1), 0.0)
            right = jnp.where(lane > 0, pltpu.roll(terms[16:, at], 1, 1), 0.0)
            total = left + terms[8:16, at] + right
            for i in range(c0):
                cells_ref[i, y, z : z + 1, :] = total[i : i + 1]
            cell = volume_ref[y, z].astype(f32)
            inputs.append(
                jnp.concatenate(
                    [
                        jnp.where(lane > 0, pltpu.roll(cell, 1, 1), 0.0),
                        cell,
                        jnp.where(lane < lanes - 1, pltpu.roll(cell, lanes - 1, 1), 0.0),
                    ],
                    0,
                ).astype(bf16)
            )
        term = dot_nt(around, jnp.concatenate(inputs, 1))
        first_sum = term if first_sum is None else first_sum + term
    grad_ref[...] = cells_ref[...].astype(bf16)

    first, second = 0.0, 0.0
    for tap in range(9):
        rows = first_sum[tap * c1 : (tap + 1) * c1].astype(bf16)
        first += dot(rows, order_matrix(c0, 8, lanes, tap))
        rows = second_sum[tap * c2 : (tap + 1) * c2].astype(bf16)
        second += dot(rows, order_matrix(c1, c1, rows_of(27 * c1) * lanes, tap))
    shards_dp = sums_ref.shape[0]
    flat_ref[...] = jnp.zeros(flat_ref.shape, f32)
    lay_flat(second, 27 * c1, c2 // shards_dp, 0, flat_ref)
    lay_flat(first, 27 * c0, c1 // shards_dp, rows_of(27 * c1 * c2 // shards_dp), flat_ref)
    sums_ref[...] = flat_ref[...].astype(bf16)


def last_kernel(scales, got_ref, first_ref, second_ref):
    total = jnp.sum(got_ref[...].astype(f32), axis=0)
    base = 0
    for ref, scale in ((second_ref, scales[1]), (first_ref, scales[0])):
        count = ref.shape[0]
        for row in range(rows_of(count)):
            at, size = row * lanes, min(lanes, count - row * lanes)
            ref[at : at + size] = total[base + row, :size] * scale
        base += rows_of(count)


def shards(
    volume,
    pooled_first,
    where_first,
    pooled_second,
    where_second,
    upstream,
    kernel_first,
    kernel_second,
):
    dp, gy, gz = (lax.axis_size(a) for a in ("dp", "gy", "gz"))
    c0, c1, c2 = volume.shape[1], pooled_first.shape[1], pooled_second.shape[1]
    ys, zs, xs = pooled_first.shape[2:]

    slope = jnp.where(pooled_second[0] > 0, 1.0, leak_rate).astype(f32)
    value = (upstream[0].astype(f32) * slope).astype(bf16)
    place = (where_second[0] + 1).astype(bf16)
    quarter = jnp.transpose(jnp.stack([value, place]), (2, 3, 0, 1, 4))
    quarter = jnp.repeat(quarter.reshape(ys // 2, zs, c2, xs // 2), 2, axis=0)
    half = jnp.concatenate([pooled_first[0], (where_first[0] + 1).astype(bf16)], 0)
    half = jnp.transpose(half, (1, 2, 0, 3))
    blank = jnp.zeros((ys, zs, c2, lanes - xs - xs // 2), bf16)
    own = jnp.concatenate([half, quarter, blank], 3)

    odd_z, odd_y = lax.axis_index("gz") % 2 == 1, lax.axis_index("gy") % 2 == 1

    def swapped(low, high, axis, odd):
        count = lax.axis_size(axis)
        got = []
        for begin, mine in ((0, jnp.where(odd, low, high)), (1, jnp.where(odd, high, low))):
            pairs = [(i, i + 1) for i in range(begin, count - 1, 2)]
            if pairs:
                got.append(lax.ppermute(mine, axis, pairs + [(b, a) for a, b in pairs]))
        return got

    def edge(z, first):
        return jnp.concatenate([own[:, z, :, :xs], own[0, first : first + 2, :, xs:]], 2)

    rims = swapped(edge(0, 0), edge(zs - 1, zs - 2), "gz", odd_z)
    low = jnp.concatenate([own[0]] + rims, 0)
    high = jnp.concatenate([own[ys - 1]] + rims, 0)
    planes = swapped(low, high, "gy", odd_y)
    odd = jnp.stack([odd_z, odd_y]).astype(jnp.int32)

    cells = jnp.transpose(volume[0], (1, 2, 0, 3))
    cells = jnp.pad(cells, ((0, 0), (0, 0), (0, 8 - c0), (0, 0)))
    first = jnp.transpose(kernel_first, (4, 1, 2, 3, 0))
    first = jnp.pad(first, ((0, 0), (0, 8 - c0), (0, 0), (0, 0), (0, 0)))
    first = first.reshape(24, 9 * c1)
    second = jnp.transpose(kernel_second, (4, 1, 2, 3, 0)).reshape(3 * c1, 9 * c2)

    sizes1, sizes2 = 27 * c0 * c1 // dp, 27 * c1 * c2 // dp
    sum_rows = -(-(rows_of(sizes1) + rows_of(sizes2)) // 16) * 16
    vmem = pl.BlockSpec(memory_space=pltpu.VMEM)
    grad_vol, sums = pl.pallas_call(
        functools.partial(main_kernel, (ys, zs, xs, c1, c2)),
        out_shape=(
            jax.ShapeDtypeStruct(volume.shape[1:], bf16),
            jax.ShapeDtypeStruct((dp, sum_rows, lanes), bf16),
        ),
        in_specs=[
            pl.BlockSpec(memory_space=pltpu.SMEM),
            vmem,
            [vmem] * len(rims),
            [vmem] * len(planes),
            vmem,
            vmem,
            vmem,
        ],
        out_specs=(vmem, vmem),
        scratch_shapes=[
            pltpu.VMEM((ys + 4, zs + 4, c2, lanes), bf16),
            pltpu.VMEM((2 * ys + 4, 2 * zs + 4, c1, lanes), bf16),
            pltpu.VMEM(volume.shape[1:], f32),
            pltpu.VMEM((dp, sum_rows, lanes), f32),
        ],
        compiler_params=pltpu.CompilerParams(vmem_limit_bytes=48 * 1024 * 1024),
        cost_estimate=pl.CostEstimate(
            flops=200_000_000, bytes_accessed=2_000_000, transcendentals=0
        ),
    )(odd, own, rims, planes, cells, first, second)

    sent = jnp.broadcast_to(sums[:, None], (dp, gy * gz) + sums.shape[1:])
    sent = sent.reshape((dp * gy * gz,) + sums.shape[1:])
    got = lax.all_to_all(sent, ("dp", "gy", "gz"), 0, 0, tiled=True)
    count = volume.shape[0] * volume.shape[2] * volume.shape[3] * volume.shape[4] * dp * gy * gz
    first_out, second_out = pl.pallas_call(
        functools.partial(last_kernel, (math.sqrt(8.0 / count), math.sqrt(64.0 / count))),
        out_shape=(
            jax.ShapeDtypeStruct((sizes1,), f32),
            jax.ShapeDtypeStruct((sizes2,), f32),
        ),
        in_specs=[vmem],
        out_specs=(vmem, vmem),
    )(got)
    return grad_vol[None], first_out, second_out


def solution(mesh):
    cells = P("dp", None, "gy", "gz", None)
    return jax.shard_map(
        shards,
        mesh=mesh,
        in_specs=(cells,) * 6 + (P(), P()),
        out_specs=(cells, P("dp"), P("dp")),
        check_vma=False,
    )
```

```python
import functools
import math

import jax
import jax.numpy as jnp
from jax import lax
from jax.experimental import pallas as pl
from jax.experimental.pallas import tpu as pltpu
from jax.sharding import PartitionSpec as P

leak_rate = 0.3
lanes = 128
f32, bf16 = jnp.float32, jnp.bfloat16


def dot(a, b):
    return lax.dot_general(a, b, (((1,), (0,)), ((), ())), preferred_element_type=f32)


def dot_nt(a, b):
    return lax.dot_general(a, b, (((1,), (1,)), ((), ())), preferred_element_type=f32)


def spread_matrix(first_row, count):
    row = lax.broadcasted_iota(jnp.int32, (lanes, lanes), 0)
    lane = lax.broadcasted_iota(jnp.int32, (lanes, lanes), 1)
    hit = (lane >> 1) + first_row == row
    return jnp.where(hit & (lane < 2 * count), 1.0, 0.0).astype(bf16)


def order_matrix(ins, step, outs, tap):
    row = lax.broadcasted_iota(jnp.int32, (3 * step, outs), 0)
    column = lax.broadcasted_iota(jnp.int32, (3 * step, outs), 1)
    hit = column == (row % step) * 27 + 3 * tap + row // step
    return jnp.where(hit & (row % step < ins), 1.0, 0.0).astype(bf16)


def rows_of(count):
    return -(-count // lanes)


def lay_flat(values, length, keep, base, out_ref):
    shards_dp = out_ref.shape[0]
    for d in range(shards_dp):
        for k in range(keep):
            row = values[d * keep + k : d * keep + k + 1]
            start = length * k % lanes
            total = rows_of(start + length)
            width = total * lanes
            if row.shape[1] < width:
                row = jnp.concatenate(
                    [row, jnp.zeros((1, width - row.shape[1]), f32)], 1
                )
            row = pltpu.roll(row, start, 1) if start else row
            top = base + length * k // lanes
            for t in range(total):
                out_ref[d, top + t : top + t + 1] += row[:, t * lanes : (t + 1) * lanes]


def main_kernel(
    sizes,
    odd_ref,
    own_ref,
    rim_refs,
    plane_refs,
    volume_ref,
    first_ref,
    second_ref,
    grad_ref,
    sums_ref,
    up_ref,
    down_ref,
    cells_ref,
):
    ys, zs, xs, c1, c2 = sizes
    odd_z, odd_y = odd_ref[0] > 0, odd_ref[1] > 0

    def sides(even, odd, flag):
        return jnp.where(flag, even, odd), jnp.where(flag, odd, even)

    def rims(even, odd):
        return sides(even, odd, odd_z)

    def second_of(refs):
        return refs[1][...] if len(refs) > 1 else jnp.zeros(refs[0].shape, bf16)

    nothing = jnp.zeros(rim_refs[0].shape, bf16)
    zlow, zhigh = rims(rim_refs[0][...], second_of(rim_refs))
    ylow, yhigh = sides(plane_refs[0][...], second_of(plane_refs), odd_y)
    ylow_rims = rims(ylow[zs : zs + 2], ylow[zs + 2 :] if len(rim_refs) > 1 else nothing)
    yhigh_rims = rims(yhigh[zs : zs + 2], yhigh[zs + 2 :] if len(rim_refs) > 1 else nothing)

    def half_row(y, z):
        if 0 <= z < zs:
            if y < 0:
                return ylow[z]
            return own_ref[y, z] if y < ys else yhigh[z]
        side = 0 if z < 0 else 1
        if y < 0:
            return ylow_rims[side][ys - 1]
        return (zlow, zhigh)[side][y] if y < ys else yhigh_rims[side][0]

    def quarter_row(y, z, part):
        if 0 <= z < zs // 2:
            if y < 0:
                return ylow[2 * z + part]
            return own_ref[0, 2 * z + part] if y < 1 else yhigh[2 * z + part]
        side = 0 if z < 0 else 1
        if y < 0:
            return ylow_rims[side][part]
        return (zlow, zhigh)[side][part] if y < 1 else yhigh_rims[side][part]

    lane = lax.broadcasted_iota(jnp.int32, (1, lanes), 1)
    parity = (lane & 1).astype(f32) + 1.0

    spread = spread_matrix(xs, xs // 2)
    for y in range(-1, ys // 2 + 1):
        zr = range(-1, zs // 2 + 1)
        values = dot(jnp.concatenate([quarter_row(y, z, 0) for z in zr], 0), spread)
        places = dot(jnp.concatenate([quarter_row(y, z, 1) for z in zr], 0), spread)
        for n, z in enumerate(zr):
            value, place = values[n * c2 : (n + 1) * c2], places[n * c2 : (n + 1) * c2]
            for dy in range(2):
                for dz in range(2):
                    up_ref[2 * y + 2 + dy, 2 * z + 2 + dz] = jnp.where(
                        place == parity + (4 * dy + 2 * dz), value, 0.0
                    ).astype(bf16)

    spread = spread_matrix(0, xs)
    weights = second_ref[...]
    second_sum = None
    for y in range(-1, ys + 1):
        zr = range(-1, zs + 1)
        around = jnp.concatenate(
            [
                jnp.concatenate([up_ref[y + 3 - ty, z + 3 - tz] for z in zr], 1)
                for ty in range(3)
                for tz in range(3)
            ],
            0,
        )
        terms = dot(weights, around)
        rows = [half_row(y, z) for z in zr]
        grads = []
        for n, row in enumerate(rows):
            at = slice(n * lanes, (n + 1) * lanes)
            pooled = row[:c1].astype(f32)
            total = (
                pltpu.roll(terms[:c1, at], lanes - 1, 1)
                + terms[c1 : 2 * c1, at]
                + pltpu.roll(terms[2 * c1 :, at], 1, 1)
            )
            grads.append((total * jnp.where(pooled > 0, 1.0, leak_rate)).astype(bf16))
        values = dot(jnp.concatenate(grads, 0), spread)
        places = dot(jnp.concatenate([row[c1:] for row in rows], 0), spread)
        for n, z in enumerate(zr):
            value, place = values[n * c1 : (n + 1) * c1], places[n * c1 : (n + 1) * c1]
            for dy in range(2):
                for dz in range(2):
                    down_ref[2 * y + 2 + dy, 2 * z + 2 + dz] = jnp.where(
                        place == parity + (4 * dy + 2 * dz), value, 0.0
                    ).astype(bf16)
        if 0 <= y < ys:
            inputs = []
            for row in rows[1:-1]:
                pooled = row[:c1].astype(f32)
                act = jnp.where(pooled > 0, pooled, leak_rate * pooled)
                act = jnp.where(lane < xs, act, 0.0).astype(bf16).astype(f32)
                inputs.append(
                    jnp.concatenate(
                        [pltpu.roll(act, 1, 1), act, pltpu.roll(act, lanes - 1, 1)], 0
                    ).astype(bf16)
                )
            term = dot_nt(around[:, lanes:-lanes], jnp.concatenate(inputs, 1))
            second_sum = term if second_sum is None else second_sum + term

    weights = first_ref[...]
    first_sum = None
    c0 = grad_ref.shape[0]
    for y in range(2 * ys):
        zr = range(2 * zs)
        around = jnp.concatenate(
            [
                jnp.concatenate([down_ref[y + 3 - ty, z + 3 - tz] for z in zr], 1)
                for ty in range(3)
                for tz in range(3)
            ],
            0,
        )
        terms = dot(weights, around)
        inputs = []
        for z in zr:
            at = slice(z * lanes, (z + 1) * lanes)
            left = jnp.where(lane < lanes - 1, pltpu.roll(terms[:8, at], lanes - 1, 1), 0.0)
            right = jnp.where(lane > 0, pltpu.roll(terms[16:, at], 1, 1), 0.0)
            total = left + terms[8:16, at] + right
            for i in range(c0):
                cells_ref[i, y, z : z + 1, :] = total[i : i + 1]
            cell = volume_ref[y, z].astype(f32)
            inputs.append(
                jnp.concatenate(
                    [
                        jnp.where(lane > 0, pltpu.roll(cell, 1, 1), 0.0),
                        cell,
                        jnp.where(lane < lanes - 1, pltpu.roll(cell, lanes - 1, 1), 0.0),
                    ],
                    0,
                ).astype(bf16)
            )
        term = dot_nt(around, jnp.concatenate(inputs, 1))
        first_sum = term if first_sum is None else first_sum + term
    grad_ref[...] = cells_ref[...].astype(bf16)

    first, second = 0.0, 0.0
    for tap in range(9):
        rows = first_sum[tap * c1 : (tap + 1) * c1].astype(bf16)
        first += dot(rows, order_matrix(c0, 8, lanes, tap))
        rows = second_sum[tap * c2 : (tap + 1) * c2].astype(bf16)
        second += dot(rows, order_matrix(c1, c1, rows_of(27 * c1) * lanes, tap))
    shards_dp = sums_ref.shape[0]
    sums_ref[...] = jnp.zeros(sums_ref.shape, f32)
    lay_flat(second, 27 * c1, c2 // shards_dp, 0, sums_ref)
    lay_flat(first, 27 * c0, c1 // shards_dp, rows_of(27 * c1 * c2 // shards_dp), sums_ref)


def last_kernel(scales, odd_ref, mine_ref, other_ref, first_ref, second_ref):
    mine, other = mine_ref[...], other_ref[...]
    odd = odd_ref[1] > 0
    total = jnp.concatenate([jnp.where(odd, other, mine), jnp.where(odd, mine, other)], 0)
    base = 0
    for ref, scale in ((second_ref, scales[1]), (first_ref, scales[0])):
        count = ref.shape[0]
        for row in range(rows_of(count)):
            at, size = row * lanes, min(lanes, count - row * lanes)
            ref[at : at + size] = total[base + row, :size] * scale
        base += rows_of(count)


def shards(
    volume,
    pooled_first,
    where_first,
    pooled_second,
    where_second,
    upstream,
    kernel_first,
    kernel_second,
):
    dp, gy, gz = (lax.axis_size(a) for a in ("dp", "gy", "gz"))
    c0, c1, c2 = volume.shape[1], pooled_first.shape[1], pooled_second.shape[1]
    ys, zs, xs = pooled_first.shape[2:]

    slope = jnp.where(pooled_second[0] > 0, 1.0, leak_rate).astype(f32)
    value = (upstream[0].astype(f32) * slope).astype(bf16)
    place = (where_second[0] + 1).astype(bf16)
    quarter = jnp.transpose(jnp.stack([value, place]), (2, 3, 0, 1, 4))
    quarter = jnp.repeat(quarter.reshape(ys // 2, zs, c2, xs // 2), 2, axis=0)
    half = jnp.concatenate([pooled_first[0], (where_first[0] + 1).astype(bf16)], 0)
    half = jnp.transpose(half, (1, 2, 0, 3))
    blank = jnp.zeros((ys, zs, c2, lanes - xs - xs // 2), bf16)
    own = jnp.concatenate([half, quarter, blank], 3)

    odd_z, odd_y = lax.axis_index("gz") % 2 == 1, lax.axis_index("gy") % 2 == 1

    def swapped(low, high, axis, odd):
        count = lax.axis_size(axis)
        got = []
        for begin, mine in ((0, jnp.where(odd, low, high)), (1, jnp.where(odd, high, low))):
            pairs = [(i, i + 1) for i in range(begin, count - 1, 2)]
            if pairs:
                got.append(lax.ppermute(mine, axis, pairs + [(b, a) for a, b in pairs]))
        return got

    def edge(z, first):
        return jnp.concatenate([own[:, z, :, :xs], own[0, first : first + 2, :, xs:]], 2)

    rims = swapped(edge(0, 0), edge(zs - 1, zs - 2), "gz", odd_z)
    low = jnp.concatenate([own[0]] + rims, 0)
    high = jnp.concatenate([own[ys - 1]] + rims, 0)
    planes = swapped(low, high, "gy", odd_y)
    odd = jnp.stack([odd_z, odd_y]).astype(jnp.int32)

    cells = jnp.transpose(volume[0], (1, 2, 0, 3))
    cells = jnp.pad(cells, ((0, 0), (0, 0), (0, 8 - c0), (0, 0)))
    first = jnp.transpose(kernel_first, (4, 1, 2, 3, 0))
    first = jnp.pad(first, ((0, 0), (0, 8 - c0), (0, 0), (0, 0), (0, 0)))
    first = first.reshape(24, 9 * c1)
    second = jnp.transpose(kernel_second, (4, 1, 2, 3, 0)).reshape(3 * c1, 9 * c2)

    sizes1, sizes2 = 27 * c0 * c1 // dp, 27 * c1 * c2 // dp
    sum_rows = -(-(rows_of(sizes1) + rows_of(sizes2)) // 32) * 32
    vmem = pl.BlockSpec(memory_space=pltpu.VMEM)
    grad_vol, sums = pl.pallas_call(
        functools.partial(main_kernel, (ys, zs, xs, c1, c2)),
        out_shape=(
            jax.ShapeDtypeStruct(volume.shape[1:], bf16),
            jax.ShapeDtypeStruct((dp, sum_rows, lanes), f32),
        ),
        in_specs=[
            pl.BlockSpec(memory_space=pltpu.SMEM),
            vmem,
            [vmem] * len(rims),
            [vmem] * len(planes),
            vmem,
            vmem,
            vmem,
        ],
        out_specs=(vmem, vmem),
        scratch_shapes=[
            pltpu.VMEM((ys + 4, zs + 4, c2, lanes), bf16),
            pltpu.VMEM((2 * ys + 4, 2 * zs + 4, c1, lanes), bf16),
            pltpu.VMEM(volume.shape[1:], f32),
        ],
        compiler_params=pltpu.CompilerParams(vmem_limit_bytes=48 * 1024 * 1024),
        cost_estimate=pl.CostEstimate(
            flops=200_000_000, bytes_accessed=2_000_000, transcendentals=0
        ),
    )(odd, own, rims, planes, cells, first, second)

    half = sum_rows // 2
    pairs = [(i, i ^ 1) for i in range(gy)]
    mine = jnp.where(odd_y, sums[:, half:], sums[:, :half])
    other = jnp.where(odd_y, sums[:, :half], sums[:, half:])
    part = (mine + lax.ppermute(other, "gy", pairs)).astype(bf16)
    sent = jnp.broadcast_to(part[:, None], (dp, gy // 2 * gz) + part.shape[1:])
    sent = sent.reshape((dp * (gy // 2) * gz,) + part.shape[1:])
    groups = [
        [(d * gy + y) * gz + z for d in range(dp) for y in range(kind, gy, 2) for z in range(gz)]
        for kind in range(2)
    ]
    got = lax.all_to_all(
        sent, ("dp", "gy", "gz"), 0, 0, axis_index_groups=groups, tiled=True
    )
    mine = jnp.sum(got.astype(f32), axis=0)
    other = lax.ppermute(mine, "gy", pairs)
    count = volume.shape[0] * volume.shape[2] * volume.shape[3] * volume.shape[4] * dp * gy * gz
    first_out, second_out = pl.pallas_call(
        functools.partial(last_kernel, (math.sqrt(8.0 / count), math.sqrt(64.0 / count))),
        out_shape=(
            jax.ShapeDtypeStruct((sizes1,), f32),
            jax.ShapeDtypeStruct((sizes2,), f32),
        ),
        in_specs=[pl.BlockSpec(memory_space=pltpu.SMEM), vmem, vmem],
        out_specs=(vmem, vmem),
    )(odd, mine, other)
    return grad_vol[None], first_out, second_out


def solution(mesh):
    cells = P("dp", None, "gy", "gz", None)
    return jax.shard_map(
        shards,
        mesh=mesh,
        in_specs=(cells,) * 6 + (P(), P()),
        out_specs=(cells, P("dp"), P("dp")),
        check_vma=False,
    )
```

```python
import functools
import math

import jax
import jax.numpy as jnp
from jax import lax
from jax.experimental import pallas as pl
from jax.experimental.pallas import tpu as pltpu
from jax.sharding import PartitionSpec as P

leak_rate = 0.3
lanes = 128
f32, bf16 = jnp.float32, jnp.bfloat16


def dot(a, b):
    return lax.dot_general(a, b, (((1,), (0,)), ((), ())), preferred_element_type=f32)


def dot_nt(a, b):
    return lax.dot_general(a, b, (((1,), (1,)), ((), ())), preferred_element_type=f32)


def spread_matrix(first_row, count):
    row = lax.broadcasted_iota(jnp.int32, (lanes, lanes), 0)
    lane = lax.broadcasted_iota(jnp.int32, (lanes, lanes), 1)
    hit = (lane >> 1) + first_row == row
    return jnp.where(hit & (lane < 2 * count), 1.0, 0.0).astype(bf16)


def order_matrix(ins, step, outs, tap):
    row = lax.broadcasted_iota(jnp.int32, (3 * step, outs), 0)
    column = lax.broadcasted_iota(jnp.int32, (3 * step, outs), 1)
    hit = column == (row % step) * 27 + 3 * tap + row // step
    return jnp.where(hit & (row % step < ins), 1.0, 0.0).astype(bf16)


def rows_of(count):
    return -(-count // lanes)


def lay_flat(values, length, keep, base, out_ref):
    shards_dp = out_ref.shape[0]
    for d in range(shards_dp):
        for k in range(keep):
            row = values[d * keep + k : d * keep + k + 1]
            start = length * k % lanes
            total = rows_of(start + length)
            width = total * lanes
            if row.shape[1] < width:
                row = jnp.concatenate(
                    [row, jnp.zeros((1, width - row.shape[1]), f32)], 1
                )
            row = pltpu.roll(row, start, 1) if start else row
            top = base + length * k // lanes
            for t in range(total):
                out_ref[d, top + t : top + t + 1] += row[:, t * lanes : (t + 1) * lanes]


def prepare_kernel(kinds, odd_ref, *refs):
    inputs, outputs, copies, arrived = refs[:5], refs[5 : 7 + kinds], refs[-6:-1], refs[-1]
    moves = [
        pltpu.make_async_copy(source, target, arrived.at[n])
        for n, (source, target) in enumerate(zip(inputs, copies))
    ]
    for move in moves:
        move.start()
    for move in moves:
        move.wait()
    prepare(odd_ref, *copies, *outputs[:3], outputs[3] if kinds > 1 else None)


def prepare(
    odd_ref,
    upstream_ref,
    pooled_second_ref,
    where_second_ref,
    pooled_first_ref,
    where_first_ref,
    half_ref,
    quarter_ref,
    rim_even_ref,
    rim_odd_ref,
):
    c1, ys, zs, xs = pooled_first_ref.shape[1:]
    zq = zs // 2
    odd = odd_ref[0] > 0
    slope = jnp.where(pooled_second_ref[0, :, 0].astype(f32) > 0, 1.0, leak_rate)
    value = upstream_ref[0, :, 0].astype(f32) * slope
    place = (where_second_ref[0, :, 0] + 1).astype(f32)
    quarter = []
    for n, part in enumerate((value, place)):
        turned = jnp.transpose(part, (1, 0, 2))
        quarter.append([turned[z] for z in range(zq)])
        quarter_ref[n] = jnp.concatenate(quarter[n], 1).astype(bf16)
    blank = jnp.zeros((2 * c1, lanes - xs), f32)
    for y in range(ys):
        pooled = jnp.transpose(pooled_first_ref[0, :, y].astype(f32), (1, 0, 2))
        places = jnp.transpose((where_first_ref[0, :, y] + 1).astype(f32), (1, 0, 2))
        rows = [jnp.concatenate([pooled[z], places[z]], 0) for z in range(zs)]
        for z in range(zs):
            half_ref[y, z] = jnp.concatenate([rows[z], blank], 1).astype(bf16)
        fill = jnp.zeros((2 * c1, lanes - xs - xs // 2), f32)
        low = jnp.concatenate([rows[0], quarter[y][0], fill], 1)
        high = jnp.concatenate([rows[-1], quarter[y][-1], fill], 1)
        rim_even_ref[y] = jnp.where(odd, low, high).astype(bf16)
        if rim_odd_ref is not None:
            rim_odd_ref[y] = jnp.where(odd, high, low).astype(bf16)


def sides_of(refs, odd):
    even = refs[0][...]
    other = refs[1][...] if len(refs) > 1 else jnp.zeros_like(even)
    return jnp.where(odd, even, other), jnp.where(odd, other, even)


def unpooled(values, places, parity):
    return [
        [
            jnp.where(places == parity + (4 * dy + 2 * dz), values, 0.0).astype(bf16)
            for dz in range(2)
        ]
        for dy in range(2)
    ]


def lane_parity():
    lane = lax.broadcasted_iota(jnp.int32, (1, lanes), 1)
    return (lane & 1).astype(f32) + 1.0


def spread_quarter(values, places, xs, c2, zq):
    wide = jnp.concatenate([spread_matrix(z * xs // 2, xs // 2) for z in range(zq)], 1)
    found = dot(jnp.concatenate([values, places], 0), wide)
    return [
        (found[:c2, z * lanes : (z + 1) * lanes], found[c2:, z * lanes : (z + 1) * lanes])
        for z in range(zq)
    ]


def side_kernel(
    sizes,
    odd_ref,
    half_ref,
    quarter_ref,
    rim_refs,
    volume_ref,
    first_ref,
    second_ref,
    up_ref,
    places_ref,
    cells_ref,
    first_out_ref,
    second_out_ref,
):
    ys, zs, xs, c1, c2 = sizes
    zlow, zhigh = sides_of(rim_refs, odd_ref[0] > 0)
    parity = lane_parity()
    rows = spread_quarter(quarter_ref[0], quarter_ref[1], xs, c2, zs // 2)
    rims = jnp.concatenate([zlow[0], zlow[1], zhigh[0], zhigh[1]], 0)
    rims = dot(rims, spread_matrix(xs, xs // 2))
    rims = [rims[n * c2 : (n + 1) * c2] for n in range(4)]
    rows = [(rims[0], rims[1])] + rows + [(rims[2], rims[3])]
    for n, (value, place) in enumerate(rows):
        cells = unpooled(value, place, parity)
        for dy in range(2):
            for dz in range(2):
                up_ref[dy, 2 * n + dz] = cells[dy][dz]
    spread = spread_matrix(0, xs)
    for y in range(ys):
        found = [zlow[y][c1:]] + [half_ref[y, z][c1:] for z in range(zs)] + [zhigh[y][c1:]]
        found = dot(jnp.concatenate(found, 0), spread).astype(bf16)
        for n in range(zs + 2):
            places_ref[y, n] = found[n * c1 : (n + 1) * c1]

    lane = lax.broadcasted_iota(jnp.int32, (1, 1, lanes), 2)
    c0, _, zf = volume_ref.shape[1:4]
    for y in range(2 * ys):
        cell = volume_ref[0, :, y].astype(f32)
        moved = [
            jnp.where(lane > 0, pltpu.roll(cell, 1, 2), 0.0),
            cell,
            jnp.where(lane < lanes - 1, pltpu.roll(cell, lanes - 1, 2), 0.0),
            jnp.zeros_like(cell),
        ]
        turned = jnp.transpose(jnp.concatenate(moved, 0), (1, 0, 2))
        for z in range(zf):
            cells_ref[y, :, z * lanes : (z + 1) * lanes] = turned[z].astype(bf16)

    wide = []
    for tap in range(9):
        parts = []
        for tx in range(3):
            parts += [first_ref[3 * tap + tx].astype(f32), jnp.zeros((8 - c0, c1), f32)]
        wide.append(jnp.concatenate(parts, 0))
    first_out_ref[...] = jnp.concatenate(wide, 1).astype(bf16)
    wide = [
        jnp.concatenate([second_ref[3 * tap + tx].astype(f32) for tx in range(3)], 0)
        for tap in range(9)
    ]
    second_out_ref[...] = jnp.concatenate(wide, 1).astype(bf16)


def main_kernel(
    sizes,
    odd_ref,
    half_ref,
    rim_refs,
    plane_refs,
    own_up_ref,
    own_places_ref,
    volume_ref,
    first_ref,
    second_ref,
    grad_ref,
    sums_ref,
    up_ref,
    down_ref,
    cells_ref,
    flat_ref,
):
    ys, zs, xs, c1, c2 = sizes
    zq = zs // 2
    odd_z = odd_ref[0] > 0
    zlow, zhigh = sides_of(rim_refs, odd_z)
    planes = sides_of(plane_refs, odd_ref[1] > 0)
    rims_at = zq + 2
    plane_rims = [
        sides_of([plane[rims_at + n] for n in range(len(rim_refs))], odd_z) for plane in planes
    ]
    parity = lane_parity()
    lane = lax.broadcasted_iota(jnp.int32, (1, lanes), 1)

    near, far = spread_matrix(xs, xs // 2), spread_matrix(xs + xs // 2, xs // 2)
    for side in range(2):
        plane, (low, high) = planes[side], plane_rims[side]
        ends = jnp.concatenate([low, high], 0)
        values, places = dot(ends, near), dot(ends, far)
        rows = spread_quarter(plane[zq], plane[zq + 1], xs, c2, zq)
        rows = [(values[:c2], places[:c2])] + rows + [(values[c2:], places[c2:])]
        for n, (value, place) in enumerate(rows):
            cells = unpooled(value, place, parity)
            for dy in range(2):
                for dz in range(2):
                    up_ref[side, dy, 2 * n + dz] = cells[dy][dz]

    def up_row(y, z):
        if y < 0:
            return up_ref[0, y + 2, z + 2]
        return own_up_ref[y, z + 2] if y < ys else up_ref[1, y - ys, z + 2]

    def pooled_row(y, z):
        side = None if 0 <= y < ys else int(y >= ys)
        if 0 <= z < zs:
            if side is None:
                return half_ref[y, z][:c1].astype(f32)
            row = planes[side][z // 2][:c1].astype(f32)
            return pltpu.roll(row, lanes - xs, 1) if z % 2 else row
        at = int(z >= 0)
        rim = (zlow, zhigh)[at][y] if side is None else plane_rims[side][at]
        return rim[:c1].astype(f32)

    wide = jnp.concatenate([spread_matrix(0, xs), spread_matrix(xs, xs)], 1)
    plane_places = []
    for side in range(2):
        rows = [planes[side][n][c1:] for n in range(zq)] + [r[c1:] for r in plane_rims[side]]
        found = dot(jnp.concatenate(rows, 0), wide)
        pick = [
            found[n * c1 : (n + 1) * c1, m * lanes : (m + 1) * lanes]
            for n in range(zq)
            for m in range(2)
        ]
        low, high = found[zq * c1 : (zq + 1) * c1, :lanes], found[(zq + 1) * c1 :, :lanes]
        plane_places.append([low] + pick + [high])

    spread = spread_matrix(0, xs)
    weights = second_ref[...]
    second_sum = None
    for y in range(-1, ys + 1):
        zr = range(-1, zs + 1)
        around = jnp.concatenate(
            [
                jnp.concatenate([up_row(y + 1 - ty, z + 1 - tz) for z in zr], 1)
                for ty in range(3)
                for tz in range(3)
            ],
            0,
        )
        terms = dot(weights, around)
        rows = [pooled_row(y, z) for z in zr]
        grads = []
        for n, pooled in enumerate(rows):
            at = slice(n * lanes, (n + 1) * lanes)
            total = (
                pltpu.roll(terms[:c1, at], lanes - 1, 1)
                + terms[c1 : 2 * c1, at]
                + pltpu.roll(terms[2 * c1 :, at], 1, 1)
            )
            grads.append((total * jnp.where(pooled > 0, 1.0, leak_rate)).astype(bf16))
        values = dot(jnp.concatenate(grads, 0), spread)
        for n, z in enumerate(zr):
            if 0 <= y < ys:
                place = own_places_ref[y, n].astype(f32)
            else:
                place = plane_places[int(y >= ys)][n]
            cells = unpooled(values[n * c1 : (n + 1) * c1], place, parity)
            for dy in range(2):
                for dz in range(2):
                    down_ref[2 * y + 2 + dy, 2 * z + 2 + dz] = cells[dy][dz]
        if 0 <= y < ys:
            inputs = []
            for pooled in rows[1:-1]:
                act = jnp.where(pooled > 0, pooled, leak_rate * pooled)
                act = jnp.where(lane < xs, act, 0.0).astype(bf16).astype(f32)
                inputs.append(
                    jnp.concatenate(
                        [pltpu.roll(act, 1, 1), act, pltpu.roll(act, lanes - 1, 1)], 0
                    ).astype(bf16)
                )
            term = dot_nt(around[:, lanes:-lanes], jnp.concatenate(inputs, 1))
            second_sum = term if second_sum is None else second_sum + term

    weights = first_ref[...]
    first_sum = None
    c0 = grad_ref.shape[0]
    for y in range(2 * ys):
        zr = range(2 * zs)
        around = jnp.concatenate(
            [
                jnp.concatenate([down_ref[y + 3 - ty, z + 3 - tz] for z in zr], 1)
                for ty in range(3)
                for tz in range(3)
            ],
            0,
        )
        terms = dot(weights, around)
        for z in zr:
            at = slice(z * lanes, (z + 1) * lanes)
            left = jnp.where(lane < lanes - 1, pltpu.roll(terms[:8, at], lanes - 1, 1), 0.0)
            right = jnp.where(lane > 0, pltpu.roll(terms[16:, at], 1, 1), 0.0)
            total = left + terms[8:16, at] + right
            for i in range(c0):
                cells_ref[i, y, z : z + 1, :] = total[i : i + 1]
        term = dot_nt(around, volume_ref[y])
        first_sum = term if first_sum is None else first_sum + term
    grad_ref[...] = cells_ref[...].astype(bf16)

    first, second = 0.0, 0.0
    for tap in range(9):
        rows = first_sum[tap * c1 : (tap + 1) * c1, : 3 * c0].astype(bf16)
        first += dot(rows, order_matrix(c0, c0, lanes, tap))
        rows = second_sum[tap * c2 : (tap + 1) * c2].astype(bf16)
        second += dot(rows, order_matrix(c1, c1, rows_of(27 * c1) * lanes, tap))
    shards_dp = sums_ref.shape[0]
    flat_ref[...] = jnp.zeros(flat_ref.shape, f32)
    lay_flat(second, 27 * c1, c2 // shards_dp, 0, flat_ref)
    lay_flat(first, 27 * c0, c1 // shards_dp, rows_of(27 * c1 * c2 // shards_dp), flat_ref)
    sums_ref[...] = flat_ref[...].astype(bf16)


def last_kernel(scales, got_ref, first_ref, second_ref):
    total = jnp.sum(got_ref[...].astype(f32), axis=0)
    base = second_ref.shape[0]
    second_ref[...] = total[:base] * scales[1]
    count = first_ref.shape[0]
    for row in range(rows_of(count)):
        at, size = row * lanes, min(lanes, count - row * lanes)
        first_ref[at : at + size] = total[base + row, :size] * scales[0]


def shards(
    volume,
    pooled_first,
    where_first,
    pooled_second,
    where_second,
    upstream,
    kernel_first,
    kernel_second,
):
    dp, gy, gz = (lax.axis_size(a) for a in ("dp", "gy", "gz"))
    c0, c1, c2 = volume.shape[1], pooled_first.shape[1], pooled_second.shape[1]
    ys, zs, xs = pooled_first.shape[2:]

    odd_z, odd_y = lax.axis_index("gz") % 2 == 1, lax.axis_index("gy") % 2 == 1
    odd = jnp.stack([odd_z, odd_y]).astype(jnp.int32)
    smem = pl.BlockSpec(memory_space=pltpu.SMEM)
    vmem = pl.BlockSpec(memory_space=pltpu.VMEM)
    params = pltpu.CompilerParams(vmem_limit_bytes=48 * 1024 * 1024)

    def like(*shape):
        return jax.ShapeDtypeStruct(shape, bf16)

    def pairs_of(axis, begin):
        count = lax.axis_size(axis)
        pairs = [(i, i + 1) for i in range(begin, count - 1, 2)]
        return pairs + [(b, a) for a, b in pairs]

    kinds = 2 if gz > 2 else 1
    raw = (upstream, pooled_second, where_second, pooled_first, where_first)
    half, quarter, *rims = pl.pallas_call(
        functools.partial(prepare_kernel, kinds),
        out_shape=(like(ys, zs, 2 * c1, lanes), like(2, c2, lanes))
        + (like(2, 2 * c1, lanes),) * kinds,
        in_specs=[smem] + [pl.BlockSpec(memory_space=pltpu.HBM)] * 5,
        out_specs=(vmem,) * (2 + kinds),
        scratch_shapes=[pltpu.VMEM(a.shape, a.dtype) for a in raw]
        + [pltpu.SemaphoreType.DMA((5,))],
        compiler_params=pltpu.CompilerParams(vmem_limit_bytes=55191 * 1024),
    )(odd, *raw)
    rims = [lax.ppermute(rim, "gz", pairs_of("gz", n)) for n, rim in enumerate(rims)]

    def plane_of(y):
        packed = jnp.concatenate([half[y, 0::2, :, :xs], half[y, 1::2, :, :xs]], 2)
        ends = [
            jnp.concatenate([rim[y, :, :xs]] + [rim[n, :, xs : xs + xs // 2] for n in range(2)], 1)[None]
            for rim in rims
        ]
        return jnp.concatenate([packed, quarter] + ends, 0)

    low, high = plane_of(0), plane_of(ys - 1)
    planes = [
        lax.ppermute(jnp.where(odd_y == (n == 0), low, high), "gy", pairs_of("gy", n))
        for n in ((1, 0) if gy > 2 else (0,))
    ][::-1]

    first = jnp.transpose(kernel_first, (2, 3, 4, 1, 0)).reshape(27, c0, c1)
    second = jnp.transpose(kernel_second, (2, 3, 4, 1, 0)).reshape(27, c1, c2)
    sizes = (ys, zs, xs, c1, c2)
    up, places, cells, first, second = pl.pallas_call(
        functools.partial(side_kernel, sizes),
        out_shape=(
            like(ys, zs + 4, c2, lanes),
            like(ys, zs + 2, c1, lanes),
            like(2 * ys, 4 * c0, 2 * zs * lanes),
            like(24, 9 * c1),
            like(3 * c1, 9 * c2),
        ),
        in_specs=[smem, vmem, vmem, [vmem] * kinds, vmem, vmem, vmem],
        out_specs=(vmem,) * 5,
        compiler_params=params,
        cost_estimate=pl.CostEstimate(flops=10**7, bytes_accessed=10**6, transcendentals=0),
    )(odd, half, quarter, rims, volume, first, second)

    sizes1, sizes2 = 27 * c0 * c1 // dp, 27 * c1 * c2 // dp
    sum_rows = -(-(rows_of(sizes1) + rows_of(sizes2)) // 16) * 16
    grad_vol, sums = pl.pallas_call(
        functools.partial(main_kernel, sizes),
        out_shape=(like(*volume.shape[1:]), like(dp, sum_rows, lanes)),
        in_specs=[smem, vmem, [vmem] * kinds, [vmem] * len(planes)] + [vmem] * 5,
        out_specs=(vmem, vmem),
        scratch_shapes=[
            pltpu.VMEM((2, 2, zs + 4, c2, lanes), bf16),
            pltpu.VMEM((2 * ys + 4, 2 * zs + 4, c1, lanes), bf16),
            pltpu.VMEM(volume.shape[1:], f32),
            pltpu.VMEM((dp, sum_rows, lanes), f32),
        ],
        compiler_params=params,
        cost_estimate=pl.CostEstimate(
            flops=200_000_000, bytes_accessed=2_000_000, transcendentals=0
        ),
    )(odd, half, rims, planes, up, places, cells, first, second)

    sent = jnp.broadcast_to(sums[:, None], (dp, gy * gz) + sums.shape[1:])
    sent = sent.reshape((dp * gy * gz,) + sums.shape[1:])
    got = lax.all_to_all(sent, ("dp", "gy", "gz"), 0, 0, tiled=True)
    count = volume.shape[0] * volume.shape[2] * volume.shape[3] * volume.shape[4] * dp * gy * gz
    first_out, second_out = pl.pallas_call(
        functools.partial(last_kernel, (math.sqrt(8.0 / count), math.sqrt(64.0 / count))),
        out_shape=(
            jax.ShapeDtypeStruct((sizes1,), f32),
            jax.ShapeDtypeStruct((rows_of(sizes2), lanes), f32),
        ),
        in_specs=[vmem],
        out_specs=(vmem, vmem),
    )(got)
    return grad_vol[None], first_out, second_out.reshape(-1)[:sizes2]


def solution(mesh):
    cells = P("dp", None, "gy", "gz", None)
    return jax.shard_map(
        shards,
        mesh=mesh,
        in_specs=(cells,) * 6 + (P(), P()),
        out_specs=(cells, P("dp"), P("dp")),
        check_vma=False,
    )
```

```python
import functools
import math

import jax
import jax.numpy as jnp
from jax import lax
from jax.experimental import pallas as pl
from jax.experimental.pallas import tpu as pltpu
from jax.sharding import PartitionSpec as P

leak_rate = 0.3
lanes = 128
f32, bf16 = jnp.float32, jnp.bfloat16


def dot(a, b):
    return lax.dot_general(a, b, (((1,), (0,)), ((), ())), preferred_element_type=f32)


def dot_nt(a, b):
    return lax.dot_general(a, b, (((1,), (1,)), ((), ())), preferred_element_type=f32)


def spread_matrix(first_row, count):
    row = lax.broadcasted_iota(jnp.int32, (lanes, lanes), 0)
    lane = lax.broadcasted_iota(jnp.int32, (lanes, lanes), 1)
    hit = (lane >> 1) + first_row == row
    return jnp.where(hit & (lane < 2 * count), 1.0, 0.0).astype(bf16)


def order_matrix(ins, shape, tap):
    row = lax.broadcasted_iota(jnp.int32, shape, 0)
    column = lax.broadcasted_iota(jnp.int32, shape, 1)
    hit = column == (row % ins) * 27 + 3 * tap + row // ins
    return jnp.where(hit & (row < 3 * ins), 1.0, 0.0).astype(bf16)


def rows_of(count):
    return -(-count // lanes)


def flat_rows(values, length, keep, shards_dp):
    starts = [length * k % lanes for k in range(keep)]
    width = rows_of(max(starts) + length) * lanes
    if values.shape[1] < width:
        blank = jnp.zeros((values.shape[0], width - values.shape[1]), f32)
        values = jnp.concatenate([values, blank], 1)
    turned = {n: pltpu.roll(values, n, 1) if n else values for n in sorted(set(starts))}
    shards = []
    for d in range(shards_dp):
        rows = [None] * rows_of(length * keep)
        for k, start in enumerate(starts):
            for t in range(rows_of(start + length)):
                at = length * k // lanes + t
                piece = turned[start][d * keep + k : d * keep + k + 1, t * lanes : (t + 1) * lanes]
                rows[at] = piece if rows[at] is None else rows[at] + piece
        shards.append(rows)
    return shards


def prepare_kernel(kinds, odd_ref, *refs):
    count = 2 + 2 * kinds
    inputs, outputs, refs = refs[:5], refs[5 : 5 + count], refs[5 + count :]
    copies, staged, arrived, left = refs[:5], refs[5 : 5 + count], refs[-2], refs[-1]
    moves = [
        pltpu.make_async_copy(source, target, arrived.at[n])
        for n, (source, target) in enumerate(zip(inputs, copies))
    ]
    for move in moves:
        move.start()
    for move in moves:
        move.wait()
    prepare(odd_ref, *copies, *staged[:2], staged[2 : 2 + kinds], staged[2 + kinds :])
    moves = [
        pltpu.make_async_copy(source, target, left.at[n])
        for n, (source, target) in enumerate(zip(staged, outputs))
    ]
    for move in moves:
        move.start()
    for move in moves:
        move.wait()


def prepare(
    odd_ref,
    upstream_ref,
    pooled_second_ref,
    where_second_ref,
    pooled_first_ref,
    where_first_ref,
    even_ref,
    odd_plane_ref,
    rim_refs,
    corner_refs,
):
    c1, ys, zs, xs = pooled_first_ref.shape[1:]
    zq = zs // 2
    odd_z, odd_y = odd_ref[0] > 0, odd_ref[1] > 0
    slope = jnp.where(pooled_second_ref[0, :, 0].astype(f32) > 0, 1.0, leak_rate)
    value = upstream_ref[0, :, 0].astype(f32) * slope
    place = (where_second_ref[0, :, 0] + 1).astype(f32)
    quarter = [jnp.transpose(part, (1, 0, 2)) for part in (value, place)]
    for n, part in enumerate(quarter):
        row = jnp.concatenate([part[z] for z in range(zq)], 1).astype(bf16)
        even_ref[zq + n] = row
        odd_plane_ref[zq + n] = row
    fill = jnp.zeros((2 * c1, lanes - xs - xs // 2), f32)
    packed, ends = [], []
    for y in range(ys):
        pooled = jnp.transpose(pooled_first_ref[0, :, y].astype(f32), (1, 0, 2))
        places = jnp.transpose((where_first_ref[0, :, y] + 1).astype(f32), (1, 0, 2))
        rows = [jnp.concatenate([pooled[z], places[z]], 0) for z in range(zs)]
        packed.append(
            [jnp.concatenate([rows[2 * n], rows[2 * n + 1]], 1).astype(bf16) for n in range(zq)]
        )
        ends.append((rows[0], rows[-1]))
        low = jnp.concatenate([rows[0], quarter[y][0], fill], 1)
        high = jnp.concatenate([rows[-1], quarter[y][-1], fill], 1)
        for n, ref in enumerate(rim_refs):
            ref[y] = jnp.where(odd_z == (n == 0), low, high).astype(bf16)
    for n in range(zq):
        even_ref[n] = jnp.where(odd_y, packed[0][n], packed[-1][n])
        odd_plane_ref[n] = jnp.where(odd_y, packed[-1][n], packed[0][n])
    facing = [jnp.where(odd_y, ends[-1][side], ends[0][side]) for side in range(2)]
    low = jnp.concatenate([facing[0], quarter[0][0], quarter[1][0]], 1)
    high = jnp.concatenate([facing[1], quarter[0][-1], quarter[1][-1]], 1)
    for n, ref in enumerate(corner_refs):
        ref[0] = jnp.where(odd_z == (n == 0), low, high).astype(bf16)


def join_kernel(xs, odd_ref, rim_refs, before_refs, joined_ref):
    odd_y = odd_ref[1] > 0
    lane = lax.broadcasted_iota(jnp.int32, (1, lanes), 1)
    for n, ref in enumerate(rim_refs):
        low, high = ref[0].astype(f32), ref[1].astype(f32)
        row = jnp.where(odd_y, low, high)
        row = jnp.where(lane < xs, row, low)
        row = jnp.where(lane < xs + xs // 2, row, pltpu.roll(high, xs // 2, 1))
        joined_ref[n] = row.astype(bf16)


def sides_of(refs, odd):
    even = refs[0][...]
    other = refs[1][...] if len(refs) > 1 else jnp.zeros_like(even)
    return jnp.where(odd, even, other), jnp.where(odd, other, even)


def unpooled(values, places, parity):
    return [
        [
            jnp.where(places == parity + (4 * dy + 2 * dz), values, 0.0).astype(bf16)
            for dz in range(2)
        ]
        for dy in range(2)
    ]


def lane_parity():
    lane = lax.broadcasted_iota(jnp.int32, (1, lanes), 1)
    return (lane & 1).astype(f32) + 1.0


def spread_quarter(values, places, xs, c2, zq):
    wide = jnp.concatenate([spread_matrix(z * xs // 2, xs // 2) for z in range(zq)], 1)
    found = dot(jnp.concatenate([values, places], 0), wide)
    return [
        (found[:c2, z * lanes : (z + 1) * lanes], found[c2:, z * lanes : (z + 1) * lanes])
        for z in range(zq)
    ]


def spread_places(plane, ends, xs, c1, zq):
    wide = jnp.concatenate([spread_matrix(0, xs), spread_matrix(xs, xs)], 1)
    rows = [plane[n][c1:] for n in range(zq)] + [end[c1:] for end in ends]
    found = dot(jnp.concatenate(rows, 0), wide)
    inner = [
        found[n * c1 : (n + 1) * c1, m * lanes : (m + 1) * lanes]
        for n in range(zq)
        for m in range(2)
    ]
    low, high = found[zq * c1 : (zq + 1) * c1, :lanes], found[(zq + 1) * c1 :, :lanes]
    return [low] + inner + [high]


def side_kernel(
    sizes,
    odd_ref,
    own_refs,
    rim_refs,
    volume_ref,
    first_ref,
    second_ref,
    up_ref,
    places_ref,
    cells_ref,
    first_out_ref,
    second_out_ref,
    first_order_ref,
    second_order_ref,
):
    ys, zs, xs, c1, c2 = sizes
    zlow, zhigh = sides_of(rim_refs, odd_ref[0] > 0)
    own = sides_of(own_refs, odd_ref[1] > 0)
    parity = lane_parity()
    zq = zs // 2
    rows = spread_quarter(own[0][zq], own[0][zq + 1], xs, c2, zq)
    rims = jnp.concatenate([zlow[0], zlow[1], zhigh[0], zhigh[1]], 0)
    rims = dot(rims, spread_matrix(xs, xs // 2))
    rims = [rims[n * c2 : (n + 1) * c2] for n in range(4)]
    rows = [(rims[0], rims[1])] + rows + [(rims[2], rims[3])]
    for n, (value, place) in enumerate(rows):
        cells = unpooled(value, place, parity)
        for dy in range(2):
            for dz in range(2):
                up_ref[dy, 2 * n + dz] = cells[dy][dz]
    for y in range(ys):
        for n, row in enumerate(spread_places(own[y], (zlow[y], zhigh[y]), xs, c1, zq)):
            places_ref[y, n] = row.astype(bf16)

    lane = lax.broadcasted_iota(jnp.int32, (1, 1, lanes), 2)
    c0, _, zf = volume_ref.shape[1:4]
    for y in range(2 * ys):
        cell = volume_ref[0, :, y].astype(f32)
        moved = [
            jnp.where(lane > 0, pltpu.roll(cell, 1, 2), 0.0),
            cell,
            jnp.where(lane < lanes - 1, pltpu.roll(cell, lanes - 1, 2), 0.0),
            jnp.zeros_like(cell),
        ]
        turned = jnp.transpose(jnp.concatenate(moved, 0), (1, 0, 2))
        for z in range(zf):
            cells_ref[y, :, z * lanes : (z + 1) * lanes] = turned[z].astype(bf16)

    wide = []
    for tap in range(9):
        parts = []
        for tx in range(3):
            parts += [first_ref[3 * tap + tx].astype(f32), jnp.zeros((8 - c0, c1), f32)]
        wide.append(jnp.concatenate(parts, 0))
    first_out_ref[...] = jnp.concatenate(wide, 1).astype(bf16)
    wide = [
        jnp.concatenate([second_ref[3 * tap + tx].astype(f32) for tx in range(3)], 0)
        for tap in range(9)
    ]
    second_out_ref[...] = jnp.concatenate(wide, 1).astype(bf16)
    for tap in range(9):
        first_order_ref[tap] = order_matrix(c0, first_order_ref.shape[1:], tap)
        second_order_ref[tap] = order_matrix(c1, second_order_ref.shape[1:], tap)


def main_kernel(
    sizes,
    odd_ref,
    own_refs,
    rim_refs,
    plane_refs,
    corner_refs,
    joined_ref,
    own_up_ref,
    own_places_ref,
    volume_ref,
    first_ref,
    second_ref,
    first_order_ref,
    second_order_ref,
    grad_ref,
    sums_ref,
    up_ref,
    down_ref,
    cells_ref,
    leaving_ref,
    sent,
):
    ys, zs, xs, c1, c2 = sizes
    zq = zs // 2
    odd_z, odd_y = odd_ref[0] > 0, odd_ref[1] > 0
    zlow, zhigh = sides_of(rim_refs, odd_z)
    own = sides_of(own_refs, odd_y)
    planes = sides_of(plane_refs, odd_y)
    even_rims = sides_of([joined_ref[n] for n in range(len(rim_refs))], odd_z)
    other_rims = sides_of([ref[0] for ref in corner_refs], odd_z)
    plane_rims = [
        [jnp.where(odd_y, even_rims[n], other_rims[n]) for n in range(2)],
        [jnp.where(odd_y, other_rims[n], even_rims[n]) for n in range(2)],
    ]
    parity = lane_parity()
    lane = lax.broadcasted_iota(jnp.int32, (1, lanes), 1)

    near, far = spread_matrix(xs, xs // 2), spread_matrix(xs + xs // 2, xs // 2)
    for side in range(2):
        plane, (low, high) = planes[side], plane_rims[side]
        ends = jnp.concatenate([low, high], 0)
        values, places = dot(ends, near), dot(ends, far)
        rows = spread_quarter(plane[zq], plane[zq + 1], xs, c2, zq)
        rows = [(values[:c2], places[:c2])] + rows + [(values[c2:], places[c2:])]
        for n, (value, place) in enumerate(rows):
            cells = unpooled(value, place, parity)
            for dy in range(2):
                for dz in range(2):
                    up_ref[side, dy, 2 * n + dz] = cells[dy][dz]

    def up_row(y, z):
        if y < 0:
            return up_ref[0, y + 2, z + 2]
        return own_up_ref[y, z + 2] if y < ys else up_ref[1, y - ys, z + 2]

    def pooled_row(y, z):
        side = None if 0 <= y < ys else int(y >= ys)
        if 0 <= z < zs:
            plane = own[y] if side is None else planes[side]
            row = plane[z // 2][:c1].astype(f32)
            return pltpu.roll(row, lanes - xs, 1) if z % 2 else row
        at = int(z >= 0)
        rim = (zlow, zhigh)[at][y] if side is None else plane_rims[side][at]
        return rim[:c1].astype(f32)

    plane_places = [
        spread_places(planes[side], plane_rims[side], xs, c1, zq) for side in range(2)
    ]

    spread = spread_matrix(0, xs)
    weights = second_ref[...]
    second_sum = None
    for y in range(-1, ys + 1):
        zr = range(-1, zs + 1)
        around = jnp.concatenate(
            [
                jnp.concatenate([up_row(y + 1 - ty, z + 1 - tz) for z in zr], 1)
                for ty in range(3)
                for tz in range(3)
            ],
            0,
        )
        terms = dot(weights, around)
        rows = [pooled_row(y, z) for z in zr]
        grads = []
        for n, pooled in enumerate(rows):
            at = slice(n * lanes, (n + 1) * lanes)
            total = (
                pltpu.roll(terms[:c1, at], lanes - 1, 1)
                + terms[c1 : 2 * c1, at]
                + pltpu.roll(terms[2 * c1 :, at], 1, 1)
            )
            grads.append((total * jnp.where(pooled > 0, 1.0, leak_rate)).astype(bf16))
        values = dot(jnp.concatenate(grads, 0), spread)
        for n, z in enumerate(zr):
            if 0 <= y < ys:
                place = own_places_ref[y, n].astype(f32)
            else:
                place = plane_places[int(y >= ys)][n]
            cells = unpooled(values[n * c1 : (n + 1) * c1], place, parity)
            for dy in range(2):
                for dz in range(2):
                    down_ref[2 * y + 2 + dy, 2 * z + 2 + dz] = cells[dy][dz]
        if 0 <= y < ys:
            inputs = []
            for pooled in rows[1:-1]:
                act = jnp.where(pooled > 0, pooled, leak_rate * pooled)
                act = jnp.where(lane < xs, act, 0.0).astype(bf16).astype(f32)
                inputs.append(
                    jnp.concatenate(
                        [pltpu.roll(act, 1, 1), act, pltpu.roll(act, lanes - 1, 1)], 0
                    ).astype(bf16)
                )
            term = dot_nt(around[:, lanes:-lanes], jnp.concatenate(inputs, 1))
            second_sum = term if second_sum is None else second_sum + term

    weights = first_ref[...]
    first_sum = None
    leaving = []
    c0 = grad_ref.shape[0]
    for y in range(2 * ys):
        zr = range(2 * zs)
        around = jnp.concatenate(
            [
                jnp.concatenate([down_ref[y + 3 - ty, z + 3 - tz] for z in zr], 1)
                for ty in range(3)
                for tz in range(3)
            ],
            0,
        )
        terms = dot(weights, around)
        for z in zr:
            at = slice(z * lanes, (z + 1) * lanes)
            left = jnp.where(lane < lanes - 1, pltpu.roll(terms[:8, at], lanes - 1, 1), 0.0)
            right = jnp.where(lane > 0, pltpu.roll(terms[16:, at], 1, 1), 0.0)
            total = left + terms[8:16, at] + right
            for i in range(c0):
                cells_ref[i, y, z : z + 1, :] = total[i : i + 1]
        leaving_ref[:, y] = cells_ref[:, y].astype(bf16)
        leaving.append(pltpu.make_async_copy(leaving_ref.at[:, y], grad_ref.at[:, y], sent.at[y]))
        leaving[y].start()
        term = dot_nt(around, volume_ref[y])
        first_sum = term if first_sum is None else first_sum + term

    first, second = 0.0, 0.0
    for tap in range(9):
        first += dot(first_sum[tap * c1 : (tap + 1) * c1].astype(bf16), first_order_ref[tap])
        second += dot(second_sum[tap * c2 : (tap + 1) * c2].astype(bf16), second_order_ref[tap])

    shards_dp, count = sums_ref.shape[:2]
    seconds = flat_rows(second, 27 * c1, c2 // shards_dp, shards_dp)
    firsts = flat_rows(first, 27 * c0, c1 // shards_dp, shards_dp)
    for d in range(shards_dp):
        rows = seconds[d] + firsts[d]
        if len(rows) < count:
            rows = rows + [jnp.zeros((count - len(rows), lanes), f32)]
        sums_ref[d] = jnp.concatenate(rows, 0).astype(bf16)
    for move in leaving:
        move.wait()


def last_kernel(scales, got_ref, first_ref, second_ref, low_ref, high_ref, left):
    total = jnp.sum(got_ref[...].astype(f32), axis=0)
    base = second_ref.shape[0]
    high_ref[...] = total[:base] * scales[1]
    count = first_ref.shape[0]
    for row in range(rows_of(count)):
        at, size = row * lanes, min(lanes, count - row * lanes)
        low_ref[at : at + size] = total[base + row, :size] * scales[0]
    moves = [
        pltpu.make_async_copy(high_ref, second_ref, left.at[0]),
        pltpu.make_async_copy(low_ref, first_ref, left.at[1]),
    ]
    for move in moves:
        move.start()
    for move in moves:
        move.wait()


def shards(
    volume,
    pooled_first,
    where_first,
    pooled_second,
    where_second,
    upstream,
    kernel_first,
    kernel_second,
):
    dp, gy, gz = (lax.axis_size(a) for a in ("dp", "gy", "gz"))
    c0, c1, c2 = volume.shape[1], pooled_first.shape[1], pooled_second.shape[1]
    ys, zs, xs = pooled_first.shape[2:]

    odd_z, odd_y = lax.axis_index("gz") % 2 == 1, lax.axis_index("gy") % 2 == 1
    odd = jnp.stack([odd_z, odd_y]).astype(jnp.int32)
    smem = pl.BlockSpec(memory_space=pltpu.SMEM)
    vmem = pl.BlockSpec(memory_space=pltpu.VMEM)
    params = pltpu.CompilerParams(vmem_limit_bytes=48 * 1024 * 1024)

    def like(*shape):
        return jax.ShapeDtypeStruct(shape, bf16)

    def pairs_of(axis, begin):
        count = lax.axis_size(axis)
        pairs = [(i, i + 1) for i in range(begin, count - 1, 2)]
        return pairs + [(b, a) for a, b in pairs]

    kinds = 2 if gz > 2 else 1
    raw = (upstream, pooled_second, where_second, pooled_first, where_first)
    plane = like(zs // 2 + 2, 2 * c1, lanes)
    prepared = (plane, plane) + (like(2, 2 * c1, lanes),) * kinds
    prepared += (like(1, 2 * c1, lanes),) * kinds
    even, other, *edges = pl.pallas_call(
        functools.partial(prepare_kernel, kinds),
        out_shape=prepared,
        in_specs=[smem] + [pl.BlockSpec(memory_space=pl.ANY)] * 5,
        out_specs=(pl.BlockSpec(memory_space=pl.ANY),) * (2 + 2 * kinds),
        scratch_shapes=[pltpu.VMEM(a.shape, a.dtype) for a in raw]
        + [pltpu.VMEM(a.shape, bf16) for a in prepared]
        + [pltpu.SemaphoreType.DMA((5,)), pltpu.SemaphoreType.DMA((2 + 2 * kinds,))],
        compiler_params=pltpu.CompilerParams(vmem_limit_bytes=61440 * 1024),
    )(odd, *raw)
    rims, corners = edges[:kinds], edges[kinds:]

    def moved(block, axes, pairs):
        return lax.ppermute(block, axes, pairs) if pairs else jnp.zeros_like(block)

    across = pairs_of("gy", 1)
    got_other = moved(other, "gy", across)
    got_rims = [moved(rim, "gz", pairs_of("gz", n)) for n, rim in enumerate(rims)]
    diagonal = [
        [(a * gz + c, b * gz + d) for a, b in across for c, d in pairs_of("gz", n)]
        for n in range(kinds)
    ]
    got_corners = [
        moved(corner, ("gy", "gz"), diagonal[n]) for n, corner in enumerate(corners)
    ]
    got_even = moved(even, "gy", pairs_of("gy", 0))
    joined = pl.pallas_call(
        functools.partial(join_kernel, xs),
        out_shape=like(kinds, 2 * c1, lanes),
        in_specs=[smem, [vmem] * kinds, [vmem] * (2 + kinds)],
        out_specs=vmem,
        compiler_params=params,
    )(odd, got_rims, [got_other, got_even] + got_corners)
    got_joined = moved(joined, "gy", pairs_of("gy", 0))

    first = jnp.transpose(kernel_first, (2, 3, 4, 1, 0)).reshape(27, c0, c1)
    second = jnp.transpose(kernel_second, (2, 3, 4, 1, 0)).reshape(27, c1, c2)
    sizes = (ys, zs, xs, c1, c2)
    wide = rows_of(27 * c1) * lanes
    up, places, cells, first, second, *orders = pl.pallas_call(
        functools.partial(side_kernel, sizes),
        out_shape=(
            like(ys, zs + 4, c2, lanes),
            like(ys, zs + 2, c1, lanes),
            like(2 * ys, 4 * c0, 2 * zs * lanes),
            like(24, 9 * c1),
            like(3 * c1, 9 * c2),
            like(9, 4 * c0, lanes),
            like(9, 3 * c1, wide),
        ),
        in_specs=[smem, [vmem] * 2, [vmem] * kinds, vmem, vmem, vmem],
        out_specs=(vmem,) * 7,
        compiler_params=params,
        cost_estimate=pl.CostEstimate(flops=10**7, bytes_accessed=10**6, transcendentals=0),
    )(odd, [even, other], got_rims, volume, first, second)

    sizes1, sizes2 = 27 * c0 * c1 // dp, 27 * c1 * c2 // dp
    sum_rows = -(-(rows_of(sizes1) + rows_of(sizes2)) // 16) * 16
    grad_vol, sums = pl.pallas_call(
        functools.partial(main_kernel, sizes),
        out_shape=(like(*volume.shape[1:]), like(dp, sum_rows, lanes)),
        in_specs=[smem, [vmem] * 2, [vmem] * kinds, [vmem] * 2, [vmem] * kinds] + [vmem] * 8,
        out_specs=(pl.BlockSpec(memory_space=pl.ANY), vmem),
        scratch_shapes=[
            pltpu.VMEM((2, 2, zs + 4, c2, lanes), bf16),
            pltpu.VMEM((2 * ys + 4, 2 * zs + 4, c1, lanes), bf16),
            pltpu.VMEM(volume.shape[1:], f32),
            pltpu.VMEM(volume.shape[1:], bf16),
            pltpu.SemaphoreType.DMA((2 * ys,)),
        ],
        compiler_params=params,
        cost_estimate=pl.CostEstimate(
            flops=200_000_000, bytes_accessed=2_000_000, transcendentals=0
        ),
    )(
        odd,
        [even, other],
        got_rims,
        [got_even, got_other],
        got_corners,
        got_joined,
        up,
        places,
        cells,
        first,
        second,
        *orders,
    )

    sent = jnp.broadcast_to(sums[:, None], (dp, gy * gz) + sums.shape[1:])
    sent = sent.reshape((dp * gy * gz,) + sums.shape[1:])
    got = lax.all_to_all(sent, ("dp", "gy", "gz"), 0, 0, tiled=True)
    count = volume.shape[0] * volume.shape[2] * volume.shape[3] * volume.shape[4] * dp * gy * gz
    first_out, second_out = pl.pallas_call(
        functools.partial(last_kernel, (math.sqrt(8.0 / count), math.sqrt(64.0 / count))),
        out_shape=(
            jax.ShapeDtypeStruct((sizes1,), f32),
            jax.ShapeDtypeStruct((rows_of(sizes2), lanes), f32),
        ),
        in_specs=[vmem],
        out_specs=(pl.BlockSpec(memory_space=pl.ANY),) * 2,
        scratch_shapes=[
            pltpu.VMEM((sizes1,), f32),
            pltpu.VMEM((rows_of(sizes2), lanes), f32),
            pltpu.SemaphoreType.DMA((2,)),
        ],
    )(got)
    return grad_vol[None], first_out, second_out.reshape(-1)[:sizes2]


def solution(mesh):
    cells = P("dp", None, "gy", "gz", None)
    return jax.shard_map(
        shards,
        mesh=mesh,
        in_specs=(cells,) * 6 + (P(), P()),
        out_specs=(cells, P("dp"), P("dp")),
        check_vma=False,
    )
```

```python
import functools
import math

import jax
import jax.numpy as jnp
from jax import lax
from jax.experimental import pallas as pl
from jax.experimental.pallas import tpu as pltpu
from jax.sharding import PartitionSpec as P

leak_rate = 0.3
lanes = 128
f32, bf16 = jnp.float32, jnp.bfloat16


def dot(a, b):
    return lax.dot_general(a, b, (((1,), (0,)), ((), ())), preferred_element_type=f32)


def dot_nt(a, b):
    return lax.dot_general(a, b, (((1,), (1,)), ((), ())), preferred_element_type=f32)


def spread_matrix(first_row, count):
    row = lax.broadcasted_iota(jnp.int32, (lanes, lanes), 0)
    lane = lax.broadcasted_iota(jnp.int32, (lanes, lanes), 1)
    hit = (lane >> 1) + first_row == row
    return jnp.where(hit & (lane < 2 * count), 1.0, 0.0).astype(bf16)


def order_matrix(ins, shape, tap):
    row = lax.broadcasted_iota(jnp.int32, shape, 0)
    column = lax.broadcasted_iota(jnp.int32, shape, 1)
    hit = column == (row % ins) * 27 + 3 * tap + row // ins
    return jnp.where(hit & (row < 3 * ins), 1.0, 0.0).astype(bf16)


def rows_of(count):
    return -(-count // lanes)


def flat_rows(values, length, keep, shards_dp):
    starts = [length * k % lanes for k in range(keep)]
    width = rows_of(max(starts) + length) * lanes
    if values.shape[1] < width:
        blank = jnp.zeros((values.shape[0], width - values.shape[1]), f32)
        values = jnp.concatenate([values, blank], 1)
    turned = {n: pltpu.roll(values, n, 1) if n else values for n in sorted(set(starts))}
    shards = []
    for d in range(shards_dp):
        rows = [None] * rows_of(length * keep)
        for k, start in enumerate(starts):
            for t in range(rows_of(start + length)):
                at = length * k // lanes + t
                piece = turned[start][d * keep + k : d * keep + k + 1, t * lanes : (t + 1) * lanes]
                rows[at] = piece if rows[at] is None else rows[at] + piece
        shards.append(rows)
    return shards


def prepare_kernel(kinds, odd_ref, *refs):
    count = 2 + kinds
    inputs, outputs, refs = refs[:5], refs[5 : 5 + count], refs[5 + count :]
    copies, arrived = refs[:5], refs[5]
    moves = [
        pltpu.make_async_copy(source, target, arrived.at[n])
        for n, (source, target) in enumerate(zip(inputs, copies))
    ]
    for move in moves:
        move.start()
    for move in moves:
        move.wait()
    prepare(odd_ref, *copies, *outputs[:2], outputs[2:])


def prepare(
    odd_ref,
    upstream_ref,
    pooled_second_ref,
    where_second_ref,
    pooled_first_ref,
    where_first_ref,
    even_ref,
    odd_plane_ref,
    rim_refs,
):
    c1, ys, zs, xs = pooled_first_ref.shape[1:]
    zq = zs // 2
    odd_z, odd_y = odd_ref[0] > 0, odd_ref[1] > 0
    slope = jnp.where(pooled_second_ref[0, :, 0].astype(f32) > 0, 1.0, leak_rate)
    value = upstream_ref[0, :, 0].astype(f32) * slope
    place = (where_second_ref[0, :, 0] + 1).astype(f32)
    quarter = [jnp.transpose(part, (1, 0, 2)) for part in (value, place)]
    for n, part in enumerate(quarter):
        row = jnp.concatenate([part[z] for z in range(zq)], 1).astype(bf16)
        even_ref[zq + n] = row
        odd_plane_ref[zq + n] = row
    fill = jnp.zeros((2 * c1, lanes - xs - xs // 2), f32)
    packed = []
    for y in range(ys):
        pooled = jnp.transpose(pooled_first_ref[0, :, y].astype(f32), (1, 0, 2))
        places = jnp.transpose((where_first_ref[0, :, y] + 1).astype(f32), (1, 0, 2))
        rows = [jnp.concatenate([pooled[z], places[z]], 0) for z in range(zs)]
        packed.append(
            [jnp.concatenate([rows[2 * n], rows[2 * n + 1]], 1).astype(bf16) for n in range(zq)]
        )
        low = jnp.concatenate([rows[0], quarter[y][0], fill], 1)
        high = jnp.concatenate([rows[-1], quarter[y][-1], fill], 1)
        for n, ref in enumerate(rim_refs):
            ref[y] = jnp.where(odd_z == (n == 0), low, high).astype(bf16)
    for n in range(zq):
        even_ref[n] = jnp.where(odd_y, packed[0][n], packed[-1][n])
        odd_plane_ref[n] = jnp.where(odd_y, packed[-1][n], packed[0][n])


def sides_of(refs, odd):
    even = refs[0][...]
    other = refs[1][...] if len(refs) > 1 else jnp.zeros_like(even)
    return jnp.where(odd, even, other), jnp.where(odd, other, even)


def unpooled(values, places, parity):
    return [
        [
            jnp.where(places == parity + (4 * dy + 2 * dz), values, 0.0).astype(bf16)
            for dz in range(2)
        ]
        for dy in range(2)
    ]


def lane_parity():
    lane = lax.broadcasted_iota(jnp.int32, (1, lanes), 1)
    return (lane & 1).astype(f32) + 1.0


def spread_quarter(values, places, xs, c2, zq):
    wide = jnp.concatenate([spread_matrix(z * xs // 2, xs // 2) for z in range(zq)], 1)
    found = dot(jnp.concatenate([values, places], 0), wide)
    return [
        (found[:c2, z * lanes : (z + 1) * lanes], found[c2:, z * lanes : (z + 1) * lanes])
        for z in range(zq)
    ]


def spread_places(plane, ends, xs, c1, zq):
    wide = jnp.concatenate([spread_matrix(0, xs), spread_matrix(xs, xs)], 1)
    rows = [plane[n][c1:] for n in range(zq)] + [end[c1:] for end in ends]
    found = dot(jnp.concatenate(rows, 0), wide)
    inner = [
        found[n * c1 : (n + 1) * c1, m * lanes : (m + 1) * lanes]
        for n in range(zq)
        for m in range(2)
    ]
    low, high = found[zq * c1 : (zq + 1) * c1, :lanes], found[(zq + 1) * c1 :, :lanes]
    return [low] + inner + [high]


def side_kernel(
    sizes,
    odd_ref,
    own_refs,
    rim_refs,
    volume_ref,
    first_ref,
    second_ref,
    up_ref,
    places_ref,
    cells_ref,
    first_out_ref,
    second_out_ref,
    first_order_ref,
    second_order_ref,
):
    ys, zs, xs, c1, c2 = sizes
    zlow, zhigh = sides_of(rim_refs, odd_ref[0] > 0)
    own = sides_of(own_refs, odd_ref[1] > 0)
    parity = lane_parity()
    zq = zs // 2
    rows = spread_quarter(own[0][zq], own[0][zq + 1], xs, c2, zq)
    rims = jnp.concatenate([zlow[0], zlow[1], zhigh[0], zhigh[1]], 0)
    rims = dot(rims, spread_matrix(xs, xs // 2))
    rims = [rims[n * c2 : (n + 1) * c2] for n in range(4)]
    rows = [(rims[0], rims[1])] + rows + [(rims[2], rims[3])]
    for n, (value, place) in enumerate(rows):
        cells = unpooled(value, place, parity)
        for dy in range(2):
            for dz in range(2):
                up_ref[dy, 2 * n + dz] = cells[dy][dz]
    for y in range(ys):
        for n, row in enumerate(spread_places(own[y], (zlow[y], zhigh[y]), xs, c1, zq)):
            places_ref[y, n] = row.astype(bf16)

    lane = lax.broadcasted_iota(jnp.int32, (1, 1, lanes), 2)
    c0, _, zf = volume_ref.shape[1:4]
    for y in range(2 * ys):
        cell = volume_ref[0, :, y].astype(f32)
        moved = [
            jnp.where(lane > 0, pltpu.roll(cell, 1, 2), 0.0),
            cell,
            jnp.where(lane < lanes - 1, pltpu.roll(cell, lanes - 1, 2), 0.0),
            jnp.zeros_like(cell),
        ]
        turned = jnp.transpose(jnp.concatenate(moved, 0), (1, 0, 2))
        for z in range(zf):
            cells_ref[y, :, z * lanes : (z + 1) * lanes] = turned[z].astype(bf16)

    wide = []
    for tap in range(9):
        parts = []
        for tx in range(3):
            parts += [first_ref[3 * tap + tx].astype(f32), jnp.zeros((8 - c0, c1), f32)]
        wide.append(jnp.concatenate(parts, 0))
    first_out_ref[...] = jnp.concatenate(wide, 1).astype(bf16)
    wide = [
        jnp.concatenate([second_ref[3 * tap + tx].astype(f32) for tx in range(3)], 0)
        for tap in range(9)
    ]
    second_out_ref[...] = jnp.concatenate(wide, 1).astype(bf16)
    for tap in range(9):
        first_order_ref[tap] = order_matrix(c0, first_order_ref.shape[1:], tap)
        second_order_ref[tap] = order_matrix(c1, second_order_ref.shape[1:], tap)


def main_kernel(
    sizes,
    odd_ref,
    own_refs,
    rim_refs,
    plane_refs,
    row_refs,
    own_up_ref,
    own_places_ref,
    volume_ref,
    first_ref,
    second_ref,
    first_order_ref,
    second_order_ref,
    grad_ref,
    sums_ref,
    up_ref,
    down_ref,
    cells_ref,
    leaving_ref,
    sent,
):
    ys, zs, xs, c1, c2 = sizes
    zq = zs // 2
    odd_z, odd_y = odd_ref[0] > 0, odd_ref[1] > 0
    zlow, zhigh = sides_of(rim_refs, odd_z)
    own = sides_of(own_refs, odd_y)
    planes = sides_of(plane_refs, odd_y)
    even_rims, other_rims = [
        sides_of([ref[n] for n in range(len(rim_refs))], odd_z) for ref in row_refs
    ]
    plane_rims = [
        [jnp.where(odd_y, even_rims[n], other_rims[n]) for n in range(2)],
        [jnp.where(odd_y, other_rims[n], even_rims[n]) for n in range(2)],
    ]
    parity = lane_parity()
    lane = lax.broadcasted_iota(jnp.int32, (1, lanes), 1)

    near, far = spread_matrix(xs, xs // 2), spread_matrix(xs + xs // 2, xs // 2)
    for side in range(2):
        plane, (low, high) = planes[side], plane_rims[side]
        ends = jnp.concatenate([low, high], 0)
        values, places = dot(ends, near), dot(ends, far)
        rows = spread_quarter(plane[zq], plane[zq + 1], xs, c2, zq)
        rows = [(values[:c2], places[:c2])] + rows + [(values[c2:], places[c2:])]
        for n, (value, place) in enumerate(rows):
            cells = unpooled(value, place, parity)
            for dy in range(2):
                for dz in range(2):
                    up_ref[side, dy, 2 * n + dz] = cells[dy][dz]

    def up_row(y, z):
        if y < 0:
            return up_ref[0, y + 2, z + 2]
        return own_up_ref[y, z + 2] if y < ys else up_ref[1, y - ys, z + 2]

    def pooled_row(y, z):
        side = None if 0 <= y < ys else int(y >= ys)
        if 0 <= z < zs:
            plane = own[y] if side is None else planes[side]
            row = plane[z // 2][:c1].astype(f32)
            return pltpu.roll(row, lanes - xs, 1) if z % 2 else row
        at = int(z >= 0)
        rim = (zlow, zhigh)[at][y] if side is None else plane_rims[side][at]
        return rim[:c1].astype(f32)

    plane_places = [
        spread_places(planes[side], plane_rims[side], xs, c1, zq) for side in range(2)
    ]

    spread = spread_matrix(0, xs)
    weights = second_ref[...]
    second_sum = None
    for y in range(-1, ys + 1):
        zr = range(-1, zs + 1)
        around = jnp.concatenate(
            [
                jnp.concatenate([up_row(y + 1 - ty, z + 1 - tz) for z in zr], 1)
                for ty in range(3)
                for tz in range(3)
            ],
            0,
        )
        terms = dot(weights, around)
        rows = [pooled_row(y, z) for z in zr]
        grads = []
        for n, pooled in enumerate(rows):
            at = slice(n * lanes, (n + 1) * lanes)
            total = (
                pltpu.roll(terms[:c1, at], lanes - 1, 1)
                + terms[c1 : 2 * c1, at]
                + pltpu.roll(terms[2 * c1 :, at], 1, 1)
            )
            grads.append((total * jnp.where(pooled > 0, 1.0, leak_rate)).astype(bf16))
        values = dot(jnp.concatenate(grads, 0), spread)
        for n, z in enumerate(zr):
            if 0 <= y < ys:
                place = own_places_ref[y, n].astype(f32)
            else:
                place = plane_places[int(y >= ys)][n]
            cells = unpooled(values[n * c1 : (n + 1) * c1], place, parity)
            for dy in range(2):
                for dz in range(2):
                    down_ref[2 * y + 2 + dy, 2 * z + 2 + dz] = cells[dy][dz]
        if 0 <= y < ys:
            inputs = []
            for pooled in rows[1:-1]:
                act = jnp.where(pooled > 0, pooled, leak_rate * pooled)
                act = jnp.where(lane < xs, act, 0.0).astype(bf16).astype(f32)
                inputs.append(
                    jnp.concatenate(
                        [pltpu.roll(act, 1, 1), act, pltpu.roll(act, lanes - 1, 1)], 0
                    ).astype(bf16)
                )
            term = dot_nt(around[:, lanes:-lanes], jnp.concatenate(inputs, 1))
            second_sum = term if second_sum is None else second_sum + term

    weights = first_ref[...]
    first_sum = None
    leaving = []
    c0 = grad_ref.shape[0]
    for y in range(2 * ys):
        zr = range(2 * zs)
        around = jnp.concatenate(
            [
                jnp.concatenate([down_ref[y + 3 - ty, z + 3 - tz] for z in zr], 1)
                for ty in range(3)
                for tz in range(3)
            ],
            0,
        )
        terms = dot(weights, around)
        for z in zr:
            at = slice(z * lanes, (z + 1) * lanes)
            left = jnp.where(lane < lanes - 1, pltpu.roll(terms[:8, at], lanes - 1, 1), 0.0)
            right = jnp.where(lane > 0, pltpu.roll(terms[16:, at], 1, 1), 0.0)
            total = left + terms[8:16, at] + right
            for i in range(c0):
                cells_ref[i, y, z : z + 1, :] = total[i : i + 1]
        leaving_ref[:, y] = cells_ref[:, y].astype(bf16)
        leaving.append(pltpu.make_async_copy(leaving_ref.at[:, y], grad_ref.at[:, y], sent.at[y]))
        leaving[y].start()
        term = dot_nt(around, volume_ref[y])
        first_sum = term if first_sum is None else first_sum + term

    first, second = 0.0, 0.0
    for tap in range(9):
        first += dot(first_sum[tap * c1 : (tap + 1) * c1].astype(bf16), first_order_ref[tap])
        second += dot(second_sum[tap * c2 : (tap + 1) * c2].astype(bf16), second_order_ref[tap])

    shards_dp, count = sums_ref.shape[:2]
    seconds = flat_rows(second, 27 * c1, c2 // shards_dp, shards_dp)
    firsts = flat_rows(first, 27 * c0, c1 // shards_dp, shards_dp)
    for d in range(shards_dp):
        rows = seconds[d] + firsts[d]
        if len(rows) < count:
            rows = rows + [jnp.zeros((count - len(rows), lanes), f32)]
        sums_ref[d] = jnp.concatenate(rows, 0).astype(bf16)
    for move in leaving:
        move.wait()


def shards(
    volume,
    pooled_first,
    where_first,
    pooled_second,
    where_second,
    upstream,
    kernel_first,
    kernel_second,
):
    dp, gy, gz = (lax.axis_size(a) for a in ("dp", "gy", "gz"))
    c0, c1, c2 = volume.shape[1], pooled_first.shape[1], pooled_second.shape[1]
    ys, zs, xs = pooled_first.shape[2:]

    odd_z, odd_y = lax.axis_index("gz") % 2 == 1, lax.axis_index("gy") % 2 == 1
    odd = jnp.stack([odd_z, odd_y]).astype(jnp.int32)
    smem = pl.BlockSpec(memory_space=pltpu.SMEM)
    vmem = pl.BlockSpec(memory_space=pltpu.VMEM)
    params = pltpu.CompilerParams(vmem_limit_bytes=48 * 1024 * 1024)

    def like(*shape):
        return jax.ShapeDtypeStruct(shape, bf16)

    def pairs_of(axis, begin):
        count = lax.axis_size(axis)
        pairs = [(i, i + 1) for i in range(begin, count - 1, 2)]
        return pairs + [(b, a) for a, b in pairs]

    kinds = 2 if gz > 2 else 1
    raw = (upstream, pooled_second, where_second, pooled_first, where_first)
    plane = like(zs // 2 + 2, 2 * c1, lanes)
    prepared = (plane, plane) + (like(2, 2 * c1, lanes),) * kinds
    even, other, *rims = pl.pallas_call(
        functools.partial(prepare_kernel, kinds),
        out_shape=tuple(pltpu.VMEM(a.shape, a.dtype) for a in prepared),
        in_specs=[smem] + [pl.BlockSpec(memory_space=pltpu.HBM)] * 5,
        out_specs=(vmem,) * (2 + kinds),
        scratch_shapes=[pltpu.VMEM(a.shape, a.dtype) for a in raw]
        + [pltpu.SemaphoreType.DMA((5,))],
        compiler_params=pltpu.CompilerParams(vmem_limit_bytes=49152 * 1024),
    )(odd, *[pltpu.with_memory_space_constraint(a, pltpu.HBM) for a in raw])

    def moved(block, axes, pairs):
        return lax.ppermute(block, axes, pairs) if pairs else jnp.zeros_like(block)

    got_rims = [moved(rim, "gz", pairs_of("gz", n)) for n, rim in enumerate(rims)]
    got_planes = [moved(plane, "gy", pairs_of("gy", n)) for n, plane in enumerate((even, other))]

    def facing(row, rim):
        return jnp.concatenate([row] + [rim[n, :, xs : xs + xs // 2] for n in range(2)], 1)

    low, high = ([facing(rim[y, :, :xs], rim) for rim in got_rims] for y in (0, ys - 1))
    low, high = jnp.stack(low), jnp.stack(high)
    got_rows = [
        moved(jnp.where(odd_y == (n == 0), low, high), "gy", pairs_of("gy", n)) for n in range(2)
    ]

    first = jnp.transpose(kernel_first, (2, 3, 4, 1, 0)).reshape(27, c0, c1)
    second = jnp.transpose(kernel_second, (2, 3, 4, 1, 0)).reshape(27, c1, c2)
    sizes = (ys, zs, xs, c1, c2)
    wide = rows_of(27 * c1) * lanes
    up, places, cells, first, second, *orders = pl.pallas_call(
        functools.partial(side_kernel, sizes),
        out_shape=(
            like(ys, zs + 4, c2, lanes),
            like(ys, zs + 2, c1, lanes),
            like(2 * ys, 4 * c0, 2 * zs * lanes),
            like(24, 9 * c1),
            like(3 * c1, 9 * c2),
            like(9, 4 * c0, lanes),
            like(9, 3 * c1, wide),
        ),
        in_specs=[smem, [vmem] * 2, [vmem] * kinds, vmem, vmem, vmem],
        out_specs=(vmem,) * 7,
        compiler_params=params,
        cost_estimate=pl.CostEstimate(flops=10**7, bytes_accessed=10**6, transcendentals=0),
    )(odd, [even, other], got_rims, volume, first, second)

    sizes1, sizes2 = 27 * c0 * c1 // dp, 27 * c1 * c2 // dp
    sum_rows = -(-(rows_of(sizes1) + rows_of(sizes2)) // 16) * 16
    grad_vol, sums = pl.pallas_call(
        functools.partial(main_kernel, sizes),
        out_shape=(like(*volume.shape[1:]), like(dp, sum_rows, lanes)),
        in_specs=[smem, [vmem] * 2, [vmem] * kinds, [vmem] * 2, [vmem] * 2] + [vmem] * 7,
        out_specs=(pl.BlockSpec(memory_space=pl.ANY), vmem),
        scratch_shapes=[
            pltpu.VMEM((2, 2, zs + 4, c2, lanes), bf16),
            pltpu.VMEM((2 * ys + 4, 2 * zs + 4, c1, lanes), bf16),
            pltpu.VMEM(volume.shape[1:], f32),
            pltpu.VMEM(volume.shape[1:], bf16),
            pltpu.SemaphoreType.DMA((2 * ys,)),
        ],
        compiler_params=params,
        cost_estimate=pl.CostEstimate(
            flops=200_000_000, bytes_accessed=2_000_000, transcendentals=0
        ),
    )(
        odd,
        [even, other],
        got_rims,
        got_planes,
        got_rows,
        up,
        places,
        cells,
        first,
        second,
        *orders,
    )

    sent = jnp.broadcast_to(sums[:, None], (dp, gy * gz) + sums.shape[1:])
    sent = sent.reshape((dp * gy * gz,) + sums.shape[1:])
    got = lax.all_to_all(sent, ("dp", "gy", "gz"), 0, 0, tiled=True)
    count = volume.shape[0] * volume.shape[2] * volume.shape[3] * volume.shape[4] * dp * gy * gz
    total = jnp.sum(got.astype(f32), axis=0)
    split = rows_of(sizes2)
    second_out = total[:split].reshape(-1)[:sizes2] * math.sqrt(64.0 / count)
    first_out = total[split : split + rows_of(sizes1)].reshape(-1)[:sizes1]
    return grad_vol[None], first_out * math.sqrt(8.0 / count), second_out


def solution(mesh):
    cells = P("dp", None, "gy", "gz", None)
    return jax.shard_map(
        shards,
        mesh=mesh,
        in_specs=(cells,) * 6 + (P(), P()),
        out_specs=(cells, P("dp"), P("dp")),
        check_vma=False,
    )
```

```python
import functools
import math

import jax
import jax.numpy as jnp
from jax import lax
from jax.experimental import pallas as pl
from jax.experimental.pallas import tpu as pltpu
from jax.sharding import PartitionSpec as P

leak_rate = 0.3
lanes = 128
f32, bf16 = jnp.float32, jnp.bfloat16


def dot(a, b):
    return lax.dot_general(a, b, (((1,), (0,)), ((), ())), preferred_element_type=f32)


def dot_nt(a, b):
    return lax.dot_general(a, b, (((1,), (1,)), ((), ())), preferred_element_type=f32)


def spread_matrix(first_row, count):
    row = lax.broadcasted_iota(jnp.int32, (lanes, lanes), 0)
    lane = lax.broadcasted_iota(jnp.int32, (lanes, lanes), 1)
    hit = (lane >> 1) + first_row == row
    return jnp.where(hit & (lane < 2 * count), 1.0, 0.0).astype(bf16)


def order_matrix(ins, shape, tap):
    row = lax.broadcasted_iota(jnp.int32, shape, 0)
    column = lax.broadcasted_iota(jnp.int32, shape, 1)
    hit = column == (row % ins) * 27 + 3 * tap + row // ins
    return jnp.where(hit & (row < 3 * ins), 1.0, 0.0).astype(bf16)


def rows_of(count):
    return -(-count // lanes)


def flat_rows(values, length, keep, shards_dp):
    starts = [length * k % lanes for k in range(keep)]
    width = rows_of(max(starts) + length) * lanes
    if values.shape[1] < width:
        blank = jnp.zeros((values.shape[0], width - values.shape[1]), f32)
        values = jnp.concatenate([values, blank], 1)
    turned = {n: pltpu.roll(values, n, 1) if n else values for n in sorted(set(starts))}
    shards = []
    for d in range(shards_dp):
        rows = [None] * rows_of(length * keep)
        for k, start in enumerate(starts):
            for t in range(rows_of(start + length)):
                at = length * k // lanes + t
                piece = turned[start][d * keep + k : d * keep + k + 1, t * lanes : (t + 1) * lanes]
                rows[at] = piece if rows[at] is None else rows[at] + piece
        shards.append(rows)
    return shards


def prepare_kernel(kinds, odd_ref, *refs):
    count = 2 + kinds
    inputs, outputs, refs = refs[:5], refs[5 : 5 + count], refs[5 + count :]
    copies, arrived = refs[:5], refs[5]
    moves = [
        pltpu.make_async_copy(source, target, arrived.at[n])
        for n, (source, target) in enumerate(zip(inputs, copies))
    ]
    for move in moves:
        move.start()
    for move in moves:
        move.wait()
    prepare(odd_ref, *copies, *outputs[:2], outputs[2:])


def prepare(
    odd_ref,
    upstream_ref,
    pooled_second_ref,
    where_second_ref,
    pooled_first_ref,
    where_first_ref,
    even_ref,
    odd_plane_ref,
    rim_refs,
):
    c1, ys, zs, xs = pooled_first_ref.shape[1:]
    zq = zs // 2
    odd_z, odd_y = odd_ref[0] > 0, odd_ref[1] > 0
    slope = jnp.where(pooled_second_ref[0, :, 0].astype(f32) > 0, 1.0, leak_rate)
    value = upstream_ref[0, :, 0].astype(f32) * slope
    place = (where_second_ref[0, :, 0] + 1).astype(f32)
    quarter = [jnp.transpose(part, (1, 0, 2)) for part in (value, place)]
    for n, part in enumerate(quarter):
        row = jnp.concatenate([part[z] for z in range(zq)], 1).astype(bf16)
        even_ref[zq + n] = row
        odd_plane_ref[zq + n] = row
    fill = jnp.zeros((2 * c1, lanes - xs - xs // 2), f32)
    packed = []
    for y in range(ys):
        pooled = jnp.transpose(pooled_first_ref[0, :, y].astype(f32), (1, 0, 2))
        places = jnp.transpose((where_first_ref[0, :, y] + 1).astype(f32), (1, 0, 2))
        rows = [jnp.concatenate([pooled[z], places[z]], 0) for z in range(zs)]
        packed.append(
            [jnp.concatenate([rows[2 * n], rows[2 * n + 1]], 1).astype(bf16) for n in range(zq)]
        )
        low = jnp.concatenate([rows[0], quarter[y][0], fill], 1)
        high = jnp.concatenate([rows[-1], quarter[y][-1], fill], 1)
        for n, ref in enumerate(rim_refs):
            ref[y] = jnp.where(odd_z == (n == 0), low, high).astype(bf16)
    for n in range(zq):
        even_ref[n] = jnp.where(odd_y, packed[0][n], packed[-1][n])
        odd_plane_ref[n] = jnp.where(odd_y, packed[-1][n], packed[0][n])


def sides_of(refs, odd):
    even = refs[0][...]
    other = refs[1][...] if len(refs) > 1 else jnp.zeros_like(even)
    return jnp.where(odd, even, other), jnp.where(odd, other, even)


def unpooled(values, places, parity):
    return [
        [
            jnp.where(places == parity + (4 * dy + 2 * dz), values, 0.0).astype(bf16)
            for dz in range(2)
        ]
        for dy in range(2)
    ]


def lane_parity():
    lane = lax.broadcasted_iota(jnp.int32, (1, lanes), 1)
    return (lane & 1).astype(f32) + 1.0


def spread_quarter(values, places, xs, c2, zq):
    wide = jnp.concatenate([spread_matrix(z * xs // 2, xs // 2) for z in range(zq)], 1)
    found = dot(jnp.concatenate([values, places], 0), wide)
    return [
        (found[:c2, z * lanes : (z + 1) * lanes], found[c2:, z * lanes : (z + 1) * lanes])
        for z in range(zq)
    ]


def spread_places(plane, ends, xs, c1, zq):
    wide = jnp.concatenate([spread_matrix(0, xs), spread_matrix(xs, xs)], 1)
    rows = [plane[n][c1:] for n in range(zq)] + [end[c1:] for end in ends]
    found = dot(jnp.concatenate(rows, 0), wide)
    inner = [
        found[n * c1 : (n + 1) * c1, m * lanes : (m + 1) * lanes]
        for n in range(zq)
        for m in range(2)
    ]
    outer = [found[n * c1 : (n + 1) * c1, :lanes] for n in range(zq, zq + len(ends))]
    return outer[:1] + inner + outer[1:]


def side_kernel(
    sizes,
    odd_ref,
    own_refs,
    rim_refs,
    plane_refs,
    volume_ref,
    first_ref,
    second_ref,
    up_ref,
    places_ref,
    side_up_ref,
    side_places_ref,
    cells_ref,
    first_out_ref,
    second_out_ref,
    first_order_ref,
    second_order_ref,
):
    ys, zs, xs, c1, c2 = sizes
    zlow, zhigh = sides_of(rim_refs, odd_ref[0] > 0)
    own = sides_of(own_refs, odd_ref[1] > 0)
    parity = lane_parity()
    zq = zs // 2
    rows = spread_quarter(own[0][zq], own[0][zq + 1], xs, c2, zq)
    rims = jnp.concatenate([zlow[0], zlow[1], zhigh[0], zhigh[1]], 0)
    rims = dot(rims, spread_matrix(xs, xs // 2))
    rims = [rims[n * c2 : (n + 1) * c2] for n in range(4)]
    rows = [(rims[0], rims[1])] + rows + [(rims[2], rims[3])]
    for n, (value, place) in enumerate(rows):
        cells = unpooled(value, place, parity)
        for dy in range(2):
            for dz in range(2):
                up_ref[dy, 2 * n + dz] = cells[dy][dz]
    for y in range(ys):
        for n, row in enumerate(spread_places(own[y], (zlow[y], zhigh[y]), xs, c1, zq)):
            places_ref[y, n] = row.astype(bf16)
    for side, plane in enumerate(sides_of(plane_refs, odd_ref[1] > 0)):
        for n, (value, place) in enumerate(spread_quarter(plane[zq], plane[zq + 1], xs, c2, zq)):
            cells = unpooled(value, place, parity)
            for dy in range(2):
                for dz in range(2):
                    side_up_ref[side, dy, 2 * n + dz] = cells[dy][dz]
        for n, row in enumerate(spread_places(plane, (), xs, c1, zq)):
            side_places_ref[side, n] = row.astype(bf16)

    lane = lax.broadcasted_iota(jnp.int32, (1, 1, lanes), 2)
    c0, _, zf = volume_ref.shape[1:4]
    for y in range(2 * ys):
        cell = volume_ref[0, :, y].astype(f32)
        moved = [
            jnp.where(lane > 0, pltpu.roll(cell, 1, 2), 0.0),
            cell,
            jnp.where(lane < lanes - 1, pltpu.roll(cell, lanes - 1, 2), 0.0),
            jnp.zeros_like(cell),
        ]
        turned = jnp.transpose(jnp.concatenate(moved, 0), (1, 0, 2))
        for z in range(zf):
            cells_ref[y, :, z * lanes : (z + 1) * lanes] = turned[z].astype(bf16)

    wide = []
    for tap in range(9):
        parts = []
        for tx in range(3):
            parts += [first_ref[3 * tap + tx].astype(f32), jnp.zeros((8 - c0, c1), f32)]
        wide.append(jnp.concatenate(parts, 0))
    first_out_ref[...] = jnp.concatenate(wide, 1).astype(bf16)
    wide = [
        jnp.concatenate([second_ref[3 * tap + tx].astype(f32) for tx in range(3)], 0)
        for tap in range(9)
    ]
    second_out_ref[...] = jnp.concatenate(wide, 1).astype(bf16)
    for tap in range(9):
        first_order_ref[tap] = order_matrix(c0, first_order_ref.shape[1:], tap)
        second_order_ref[tap] = order_matrix(c1, second_order_ref.shape[1:], tap)


def main_kernel(
    sizes,
    odd_ref,
    own_refs,
    rim_refs,
    plane_refs,
    row_refs,
    own_up_ref,
    own_places_ref,
    side_up_ref,
    side_places_ref,
    volume_ref,
    first_ref,
    second_ref,
    first_order_ref,
    second_order_ref,
    grad_ref,
    sums_ref,
    up_ref,
    down_ref,
    cells_ref,
    leaving_ref,
    sent,
):
    ys, zs, xs, c1, c2 = sizes
    zq = zs // 2
    odd_z, odd_y = odd_ref[0] > 0, odd_ref[1] > 0
    zlow, zhigh = sides_of(rim_refs, odd_z)
    own = sides_of(own_refs, odd_y)
    planes = sides_of(plane_refs, odd_y)
    even_rims, other_rims = [
        sides_of([ref[n] for n in range(len(rim_refs))], odd_z) for ref in row_refs
    ]
    plane_rims = [
        [jnp.where(odd_y, even_rims[n], other_rims[n]) for n in range(2)],
        [jnp.where(odd_y, other_rims[n], even_rims[n]) for n in range(2)],
    ]
    parity = lane_parity()
    lane = lax.broadcasted_iota(jnp.int32, (1, lanes), 1)

    near, far = spread_matrix(xs, xs // 2), spread_matrix(xs + xs // 2, xs // 2)
    for side in range(2):
        ends = jnp.concatenate(plane_rims[side], 0)
        values, places = dot(ends, near), dot(ends, far)
        for n in range(2):
            at = slice(n * c2, (n + 1) * c2)
            cells = unpooled(values[at], places[at], parity)
            for dy in range(2):
                for dz in range(2):
                    up_ref[side, dy, 2 * n + dz] = cells[dy][dz]

    def up_row(y, z):
        if 0 <= y < ys:
            return own_up_ref[y, z + 2]
        side, dy = (0, y + 2) if y < 0 else (1, y - ys)
        if 0 <= z < zs:
            return side_up_ref[side, dy, z]
        return up_ref[side, dy, z + 2 if z < 0 else z + 2 - zs]

    def pooled_row(y, z):
        side = None if 0 <= y < ys else int(y >= ys)
        if 0 <= z < zs:
            plane = own[y] if side is None else planes[side]
            row = plane[z // 2][:c1].astype(f32)
            return pltpu.roll(row, lanes - xs, 1) if z % 2 else row
        at = int(z >= 0)
        rim = (zlow, zhigh)[at][y] if side is None else plane_rims[side][at]
        return rim[:c1].astype(f32)

    rim_places = jnp.concatenate([end[c1:] for rims in plane_rims for end in rims], 0)
    rim_places = dot(rim_places, spread_matrix(0, xs))

    def place_row(y, n):
        if 0 <= y < ys:
            return own_places_ref[y, n].astype(f32)
        side = int(y >= ys)
        if 0 < n <= zs:
            return side_places_ref[side, n - 1].astype(f32)
        at = 2 * side + int(n > 0)
        return rim_places[at * c1 : (at + 1) * c1]

    spread = spread_matrix(0, xs)
    weights = second_ref[...]
    second_sum = None
    for y in range(-1, ys + 1):
        zr = range(-1, zs + 1)
        around = jnp.concatenate(
            [
                jnp.concatenate([up_row(y + 1 - ty, z + 1 - tz) for z in zr], 1)
                for ty in range(3)
                for tz in range(3)
            ],
            0,
        )
        terms = dot(weights, around)
        rows = [pooled_row(y, z) for z in zr]
        grads = []
        for n, pooled in enumerate(rows):
            at = slice(n * lanes, (n + 1) * lanes)
            total = (
                pltpu.roll(terms[:c1, at], lanes - 1, 1)
                + terms[c1 : 2 * c1, at]
                + pltpu.roll(terms[2 * c1 :, at], 1, 1)
            )
            grads.append((total * jnp.where(pooled > 0, 1.0, leak_rate)).astype(bf16))
        values = dot(jnp.concatenate(grads, 0), spread)
        for n, z in enumerate(zr):
            cells = unpooled(values[n * c1 : (n + 1) * c1], place_row(y, n), parity)
            for dy in range(2):
                for dz in range(2):
                    down_ref[2 * y + 2 + dy, 2 * z + 2 + dz] = cells[dy][dz]
        if 0 <= y < ys:
            inputs = []
            for pooled in rows[1:-1]:
                act = jnp.where(pooled > 0, pooled, leak_rate * pooled)
                act = jnp.where(lane < xs, act, 0.0).astype(bf16).astype(f32)
                inputs.append(
                    jnp.concatenate(
                        [pltpu.roll(act, 1, 1), act, pltpu.roll(act, lanes - 1, 1)], 0
                    ).astype(bf16)
                )
            term = dot_nt(jnp.concatenate(inputs, 1), around[:, lanes:-lanes])
            second_sum = term if second_sum is None else second_sum + term

    weights = first_ref[...]
    first_sum = None
    leaving = []
    c0 = grad_ref.shape[0]
    for y in range(2 * ys):
        zr = range(2 * zs)
        around = jnp.concatenate(
            [
                jnp.concatenate([down_ref[y + 3 - ty, z + 3 - tz] for z in zr], 1)
                for ty in range(3)
                for tz in range(3)
            ],
            0,
        )
        terms = dot(weights, around)
        for z in zr:
            at = slice(z * lanes, (z + 1) * lanes)
            left = jnp.where(lane < lanes - 1, pltpu.roll(terms[:8, at], lanes - 1, 1), 0.0)
            right = jnp.where(lane > 0, pltpu.roll(terms[16:, at], 1, 1), 0.0)
            total = left + terms[8:16, at] + right
            for i in range(c0):
                cells_ref[i, y, z : z + 1, :] = total[i : i + 1]
        leaving_ref[:, y] = cells_ref[:, y].astype(bf16)
        leaving.append(pltpu.make_async_copy(leaving_ref.at[:, y], grad_ref.at[:, y], sent.at[y]))
        leaving[y].start()
        term = dot_nt(volume_ref[y], around)
        first_sum = term if first_sum is None else first_sum + term

    first_sum, second_sum = first_sum.T, second_sum.T
    first, second = 0.0, 0.0
    for tap in range(9):
        first += dot(first_sum[tap * c1 : (tap + 1) * c1].astype(bf16), first_order_ref[tap])
        second += dot(second_sum[tap * c2 : (tap + 1) * c2].astype(bf16), second_order_ref[tap])

    shards_dp, count = sums_ref.shape[:2]
    seconds = flat_rows(second, 27 * c1, c2 // shards_dp, shards_dp)
    firsts = flat_rows(first, 27 * c0, c1 // shards_dp, shards_dp)
    for d in range(shards_dp):
        rows = seconds[d] + firsts[d]
        if len(rows) < count:
            rows = rows + [jnp.zeros((count - len(rows), lanes), f32)]
        sums_ref[d] = jnp.concatenate(rows, 0).astype(bf16)
    for move in leaving:
        move.wait()


def shards(
    volume,
    pooled_first,
    where_first,
    pooled_second,
    where_second,
    upstream,
    kernel_first,
    kernel_second,
):
    dp, gy, gz = (lax.axis_size(a) for a in ("dp", "gy", "gz"))
    c0, c1, c2 = volume.shape[1], pooled_first.shape[1], pooled_second.shape[1]
    ys, zs, xs = pooled_first.shape[2:]

    odd_z, odd_y = lax.axis_index("gz") % 2 == 1, lax.axis_index("gy") % 2 == 1
    odd = jnp.stack([odd_z, odd_y]).astype(jnp.int32)
    smem = pl.BlockSpec(memory_space=pltpu.SMEM)
    vmem = pl.BlockSpec(memory_space=pltpu.VMEM)
    params = pltpu.CompilerParams(vmem_limit_bytes=48 * 1024 * 1024)

    def like(*shape):
        return jax.ShapeDtypeStruct(shape, bf16)

    def pairs_of(axis, begin):
        count = lax.axis_size(axis)
        pairs = [(i, i + 1) for i in range(begin, count - 1, 2)]
        return pairs + [(b, a) for a, b in pairs]

    kinds = 2 if gz > 2 else 1
    raw = (upstream, pooled_second, where_second, pooled_first, where_first)
    plane = like(zs // 2 + 2, 2 * c1, lanes)
    prepared = (plane, plane) + (like(2, 2 * c1, lanes),) * kinds
    even, other, *rims = pl.pallas_call(
        functools.partial(prepare_kernel, kinds),
        out_shape=tuple(pltpu.VMEM(a.shape, a.dtype) for a in prepared),
        in_specs=[smem] + [pl.BlockSpec(memory_space=pltpu.HBM)] * 5,
        out_specs=(vmem,) * (2 + kinds),
        scratch_shapes=[pltpu.VMEM(a.shape, a.dtype) for a in raw]
        + [pltpu.SemaphoreType.DMA((5,))],
        compiler_params=pltpu.CompilerParams(vmem_limit_bytes=49152 * 1024),
    )(odd, *[pltpu.with_memory_space_constraint(a, pltpu.HBM) for a in raw])

    def moved(block, axes, pairs):
        return lax.ppermute(block, axes, pairs) if pairs else jnp.zeros_like(block)

    got_rims = [moved(rim, "gz", pairs_of("gz", n)) for n, rim in enumerate(rims)]
    got_planes = [moved(plane, "gy", pairs_of("gy", n)) for n, plane in enumerate((even, other))]

    def facing(row, rim):
        return jnp.concatenate([row] + [rim[n, :, xs : xs + xs // 2] for n in range(2)], 1)

    low, high = ([facing(rim[y, :, :xs], rim) for rim in got_rims] for y in (0, ys - 1))
    low, high = jnp.stack(low), jnp.stack(high)
    got_rows = [
        moved(jnp.where(odd_y == (n == 0), low, high), "gy", pairs_of("gy", n)) for n in range(2)
    ]

    first = jnp.transpose(kernel_first, (2, 3, 4, 1, 0)).reshape(27, c0, c1)
    second = jnp.transpose(kernel_second, (2, 3, 4, 1, 0)).reshape(27, c1, c2)
    sizes = (ys, zs, xs, c1, c2)
    wide = rows_of(27 * c1) * lanes
    up, places, side_up, side_places, cells, first, second, *orders = pl.pallas_call(
        functools.partial(side_kernel, sizes),
        out_shape=(
            like(ys, zs + 4, c2, lanes),
            like(ys, zs + 2, c1, lanes),
            like(2, 2, zs, c2, lanes),
            like(2, zs, c1, lanes),
            like(2 * ys, 4 * c0, 2 * zs * lanes),
            like(24, 9 * c1),
            like(3 * c1, 9 * c2),
            like(9, 4 * c0, lanes),
            like(9, 3 * c1, wide),
        ),
        in_specs=[smem, [vmem] * 2, [vmem] * kinds, [vmem] * 2, vmem, vmem, vmem],
        out_specs=(vmem,) * 9,
        compiler_params=params,
        cost_estimate=pl.CostEstimate(flops=10**7, bytes_accessed=10**6, transcendentals=0),
    )(odd, [even, other], got_rims, got_planes, volume, first, second)

    sizes1, sizes2 = 27 * c0 * c1 // dp, 27 * c1 * c2 // dp
    sum_rows = -(-(rows_of(sizes1) + rows_of(sizes2)) // 16) * 16
    grad_vol, sums = pl.pallas_call(
        functools.partial(main_kernel, sizes),
        out_shape=(like(*volume.shape[1:]), like(dp, sum_rows, lanes)),
        in_specs=[smem, [vmem] * 2, [vmem] * kinds, [vmem] * 2, [vmem] * 2] + [vmem] * 9,
        out_specs=(pl.BlockSpec(memory_space=pl.ANY), vmem),
        scratch_shapes=[
            pltpu.VMEM((2, 2, 4, c2, lanes), bf16),
            pltpu.VMEM((2 * ys + 4, 2 * zs + 4, c1, lanes), bf16),
            pltpu.VMEM(volume.shape[1:], f32),
            pltpu.VMEM(volume.shape[1:], bf16),
            pltpu.SemaphoreType.DMA((2 * ys,)),
        ],
        compiler_params=params,
        cost_estimate=pl.CostEstimate(
            flops=200_000_000, bytes_accessed=2_000_000, transcendentals=0
        ),
    )(
        odd,
        [even, other],
        got_rims,
        got_planes,
        got_rows,
        up,
        places,
        side_up,
        side_places,
        cells,
        first,
        second,
        *orders,
    )

    sent = jnp.broadcast_to(sums[:, None], (dp, gy * gz) + sums.shape[1:])
    sent = sent.reshape((dp * gy * gz,) + sums.shape[1:])
    got = lax.all_to_all(sent, ("dp", "gy", "gz"), 0, 0, tiled=True)
    count = volume.shape[0] * volume.shape[2] * volume.shape[3] * volume.shape[4] * dp * gy * gz
    total = jnp.sum(got.astype(f32), axis=0)
    split = rows_of(sizes2)
    second_out = total[:split].reshape(-1)[:sizes2] * math.sqrt(64.0 / count)
    first_out = total[split : split + rows_of(sizes1)].reshape(-1)[:sizes1]
    return grad_vol[None], first_out * math.sqrt(8.0 / count), second_out


def solution(mesh):
    cells = P("dp", None, "gy", "gz", None)
    return jax.shard_map(
        shards,
        mesh=mesh,
        in_specs=(cells,) * 6 + (P(), P()),
        out_specs=(cells, P("dp"), P("dp")),
        check_vma=False,
    )
```

```python
import functools
import math

import jax
import jax.numpy as jnp
from jax import lax
from jax.experimental import pallas as pl
from jax.experimental.pallas import tpu as pltpu
from jax.sharding import PartitionSpec as P

leak_rate = 0.3
lanes = 128
f32, bf16 = jnp.float32, jnp.bfloat16


def dot(a, b):
    return lax.dot_general(a, b, (((1,), (0,)), ((), ())), preferred_element_type=f32)


def dot_nt(a, b):
    return lax.dot_general(a, b, (((1,), (1,)), ((), ())), preferred_element_type=f32)


def spread_matrix(first_row, count):
    row = lax.broadcasted_iota(jnp.int32, (lanes, lanes), 0)
    lane = lax.broadcasted_iota(jnp.int32, (lanes, lanes), 1)
    hit = (lane >> 1) + first_row == row
    return jnp.where(hit & (lane < 2 * count), 1.0, 0.0).astype(bf16)


def order_matrix(ins, shape, tap):
    row = lax.broadcasted_iota(jnp.int32, shape, 0)
    column = lax.broadcasted_iota(jnp.int32, shape, 1)
    hit = column == (row % ins) * 27 + 3 * tap + row // ins
    return jnp.where(hit & (row < 3 * ins), 1.0, 0.0).astype(bf16)


def rows_of(count):
    return -(-count // lanes)


def flat_rows(values, length, keep, shards_dp):
    starts = [length * k % lanes for k in range(keep)]
    width = rows_of(max(starts) + length) * lanes
    if values.shape[1] < width:
        blank = jnp.zeros((values.shape[0], width - values.shape[1]), f32)
        values = jnp.concatenate([values, blank], 1)
    turned = {n: pltpu.roll(values, n, 1) if n else values for n in sorted(set(starts))}
    shards = []
    for d in range(shards_dp):
        rows = [None] * rows_of(length * keep)
        for k, start in enumerate(starts):
            for t in range(rows_of(start + length)):
                at = length * k // lanes + t
                piece = turned[start][d * keep + k : d * keep + k + 1, t * lanes : (t + 1) * lanes]
                rows[at] = piece if rows[at] is None else rows[at] + piece
        shards.append(rows)
    return shards


def prepare_kernel(kinds, odd_ref, *refs):
    count = 2 + kinds
    inputs, outputs, refs = refs[:5], refs[5 : 5 + count], refs[5 + count :]
    copies, arrived = refs[:5], refs[5]
    moves = [
        pltpu.make_async_copy(source, target, arrived.at[n])
        for n, (source, target) in enumerate(zip(inputs, copies))
    ]
    for move in moves:
        move.start()
    for move in moves:
        move.wait()
    prepare(odd_ref, *copies, *outputs[:2], outputs[2:])


def prepare(
    odd_ref,
    upstream_ref,
    pooled_second_ref,
    where_second_ref,
    pooled_first_ref,
    where_first_ref,
    even_ref,
    odd_plane_ref,
    rim_refs,
):
    c1, ys, zs, xs = pooled_first_ref.shape[1:]
    zq = zs // 2
    odd_z, odd_y = odd_ref[0] > 0, odd_ref[1] > 0
    slope = jnp.where(pooled_second_ref[0, :, 0].astype(f32) > 0, 1.0, leak_rate)
    value = upstream_ref[0, :, 0].astype(f32) * slope
    place = (where_second_ref[0, :, 0] + 1).astype(f32)
    quarter = [jnp.transpose(part, (1, 0, 2)) for part in (value, place)]
    for n, part in enumerate(quarter):
        row = jnp.concatenate([part[z] for z in range(zq)], 1).astype(bf16)
        even_ref[zq + n] = row
        odd_plane_ref[zq + n] = row
    fill = jnp.zeros((2 * c1, lanes - xs - xs // 2), f32)
    packed = []
    for y in range(ys):
        pooled = jnp.transpose(pooled_first_ref[0, :, y].astype(f32), (1, 0, 2))
        places = jnp.transpose((where_first_ref[0, :, y] + 1).astype(f32), (1, 0, 2))
        rows = [jnp.concatenate([pooled[z], places[z]], 0) for z in range(zs)]
        packed.append(
            [jnp.concatenate([rows[2 * n], rows[2 * n + 1]], 1).astype(bf16) for n in range(zq)]
        )
        low = jnp.concatenate([rows[0], quarter[y][0], fill], 1)
        high = jnp.concatenate([rows[-1], quarter[y][-1], fill], 1)
        for n, ref in enumerate(rim_refs):
            ref[y] = jnp.where(odd_z == (n == 0), low, high).astype(bf16)
    for n in range(zq):
        even_ref[n] = jnp.where(odd_y, packed[0][n], packed[-1][n])
        odd_plane_ref[n] = jnp.where(odd_y, packed[-1][n], packed[0][n])


def sides_of(refs, odd):
    even = refs[0][...]
    other = refs[1][...] if len(refs) > 1 else jnp.zeros_like(even)
    return jnp.where(odd, even, other), jnp.where(odd, other, even)


def unpooled(values, places, parity):
    return [
        [
            jnp.where(places == parity + (4 * dy + 2 * dz), values, 0.0).astype(bf16)
            for dz in range(2)
        ]
        for dy in range(2)
    ]


def lane_parity():
    lane = lax.broadcasted_iota(jnp.int32, (1, lanes), 1)
    return (lane & 1).astype(f32) + 1.0


def spread_quarter(values, places, xs, c2, zq):
    wide = jnp.concatenate([spread_matrix(z * xs // 2, xs // 2) for z in range(zq)], 1)
    found = dot(jnp.concatenate([values, places], 0), wide)
    return [
        (found[:c2, z * lanes : (z + 1) * lanes], found[c2:, z * lanes : (z + 1) * lanes])
        for z in range(zq)
    ]


def spread_places(plane, ends, xs, c1, zq):
    wide = jnp.concatenate([spread_matrix(0, xs), spread_matrix(xs, xs)], 1)
    rows = [plane[n][c1:] for n in range(zq)] + [end[c1:] for end in ends]
    found = dot(jnp.concatenate(rows, 0), wide)
    inner = [
        found[n * c1 : (n + 1) * c1, m * lanes : (m + 1) * lanes]
        for n in range(zq)
        for m in range(2)
    ]
    outer = [found[n * c1 : (n + 1) * c1, :lanes] for n in range(zq, zq + len(ends))]
    return outer[:1] + inner + outer[1:]


def side_kernel(
    sizes,
    odd_ref,
    own_refs,
    rim_refs,
    plane_refs,
    volume_ref,
    first_ref,
    second_ref,
    up_ref,
    places_ref,
    side_up_ref,
    side_places_ref,
    cells_ref,
    first_out_ref,
    second_out_ref,
    first_order_ref,
    second_order_ref,
):
    ys, zs, xs, c1, c2 = sizes
    zlow, zhigh = sides_of(rim_refs, odd_ref[0] > 0)
    own = sides_of(own_refs, odd_ref[1] > 0)
    parity = lane_parity()
    zq = zs // 2
    rows = spread_quarter(own[0][zq], own[0][zq + 1], xs, c2, zq)
    rims = jnp.concatenate([zlow[0], zlow[1], zhigh[0], zhigh[1]], 0)
    rims = dot(rims, spread_matrix(xs, xs // 2))
    rims = [rims[n * c2 : (n + 1) * c2] for n in range(4)]
    rows = [(rims[0], rims[1])] + rows + [(rims[2], rims[3])]
    for n, (value, place) in enumerate(rows):
        cells = unpooled(value, place, parity)
        for dy in range(2):
            for dz in range(2):
                up_ref[dy, 2 * n + dz] = cells[dy][dz]
    for y in range(ys):
        for n, row in enumerate(spread_places(own[y], (zlow[y], zhigh[y]), xs, c1, zq)):
            places_ref[y, n] = row.astype(bf16)
    for side, plane in enumerate(sides_of(plane_refs, odd_ref[1] > 0)):
        for n, (value, place) in enumerate(spread_quarter(plane[zq], plane[zq + 1], xs, c2, zq)):
            cells = unpooled(value, place, parity)
            for dy in range(2):
                for dz in range(2):
                    side_up_ref[side, dy, 2 * n + dz] = cells[dy][dz]
        for n, row in enumerate(spread_places(plane, (), xs, c1, zq)):
            side_places_ref[side, n] = row.astype(bf16)

    lane = lax.broadcasted_iota(jnp.int32, (1, 1, lanes), 2)
    c0, _, zf = volume_ref.shape[1:4]
    for y in range(2 * ys):
        cell = volume_ref[0, :, y].astype(f32)
        moved = [
            jnp.where(lane > 0, pltpu.roll(cell, 1, 2), 0.0),
            cell,
            jnp.where(lane < lanes - 1, pltpu.roll(cell, lanes - 1, 2), 0.0),
            jnp.zeros_like(cell),
        ]
        turned = jnp.transpose(jnp.concatenate(moved, 0), (1, 0, 2))
        for z in range(zf):
            cells_ref[y, :, z * lanes : (z + 1) * lanes] = turned[z].astype(bf16)

    wide = []
    for tap in range(9):
        parts = []
        for tx in range(3):
            parts += [first_ref[3 * tap + tx].astype(f32), jnp.zeros((8 - c0, c1), f32)]
        wide.append(jnp.concatenate(parts, 0))
    first_out_ref[...] = jnp.concatenate(wide, 1).astype(bf16)
    wide = [
        jnp.concatenate([second_ref[3 * tap + tx].astype(f32) for tx in range(3)], 0)
        for tap in range(9)
    ]
    second_out_ref[...] = jnp.concatenate(wide, 1).astype(bf16)
    for tap in range(9):
        first_order_ref[tap] = order_matrix(c0, first_order_ref.shape[1:], tap)
        second_order_ref[tap] = order_matrix(c1, second_order_ref.shape[1:], tap)


def main_kernel(
    sizes,
    odd_ref,
    own_refs,
    rim_refs,
    plane_refs,
    row_refs,
    own_up_ref,
    own_places_ref,
    side_up_ref,
    side_places_ref,
    volume_ref,
    first_ref,
    second_ref,
    first_order_ref,
    second_order_ref,
    grad_ref,
    sums_ref,
    up_ref,
    down_ref,
    cells_ref,
    leaving_ref,
    sent,
):
    ys, zs, xs, c1, c2 = sizes
    zq = zs // 2
    odd_z, odd_y = odd_ref[0] > 0, odd_ref[1] > 0
    zlow, zhigh = sides_of(rim_refs, odd_z)
    own = sides_of(own_refs, odd_y)
    planes = sides_of(plane_refs, odd_y)
    even_rims, other_rims = [
        sides_of([ref[n] for n in range(len(rim_refs))], odd_z) for ref in row_refs
    ]
    plane_rims = [
        [jnp.where(odd_y, even_rims[n], other_rims[n]) for n in range(2)],
        [jnp.where(odd_y, other_rims[n], even_rims[n]) for n in range(2)],
    ]
    parity = lane_parity()
    lane = lax.broadcasted_iota(jnp.int32, (1, lanes), 1)

    near, far = spread_matrix(xs, xs // 2), spread_matrix(xs + xs // 2, xs // 2)
    for side in range(2):
        ends = jnp.concatenate(plane_rims[side], 0)
        values, places = dot(ends, near), dot(ends, far)
        for n in range(2):
            at = slice(n * c2, (n + 1) * c2)
            cells = unpooled(values[at], places[at], parity)
            for dy in range(2):
                for dz in range(2):
                    up_ref[side, dy, 2 * n + dz] = cells[dy][dz]

    def up_row(y, z):
        if 0 <= y < ys:
            return own_up_ref[y, z + 2]
        side, dy = (0, y + 2) if y < 0 else (1, y - ys)
        if 0 <= z < zs:
            return side_up_ref[side, dy, z]
        return up_ref[side, dy, z + 2 if z < 0 else z + 2 - zs]

    def pooled_row(y, z):
        side = None if 0 <= y < ys else int(y >= ys)
        if 0 <= z < zs:
            plane = own[y] if side is None else planes[side]
            row = plane[z // 2][:c1].astype(f32)
            return pltpu.roll(row, lanes - xs, 1) if z % 2 else row
        at = int(z >= 0)
        rim = (zlow, zhigh)[at][y] if side is None else plane_rims[side][at]
        return rim[:c1].astype(f32)

    rim_places = jnp.concatenate([end[c1:] for rims in plane_rims for end in rims], 0)
    rim_places = dot(rim_places, spread_matrix(0, xs))

    def place_row(y, n):
        if 0 <= y < ys:
            return own_places_ref[y, n].astype(f32)
        side = int(y >= ys)
        if 0 < n <= zs:
            return side_places_ref[side, n - 1].astype(f32)
        at = 2 * side + int(n > 0)
        return rim_places[at * c1 : (at + 1) * c1]

    spread = spread_matrix(0, xs)
    weights = second_ref[...]
    second_sum = None
    for y in range(-1, ys + 1):
        zr = range(-1, zs + 1)
        around = jnp.concatenate(
            [
                jnp.concatenate([up_row(y + 1 - ty, z + 1 - tz) for z in zr], 1)
                for ty in range(3)
                for tz in range(3)
            ],
            0,
        )
        terms = dot(weights, around)
        rows = [pooled_row(y, z) for z in zr]
        grads = []
        for n, pooled in enumerate(rows):
            at = slice(n * lanes, (n + 1) * lanes)
            total = (
                pltpu.roll(terms[:c1, at], lanes - 1, 1)
                + terms[c1 : 2 * c1, at]
                + pltpu.roll(terms[2 * c1 :, at], 1, 1)
            )
            grads.append((total * jnp.where(pooled > 0, 1.0, leak_rate)).astype(bf16))
        values = dot(jnp.concatenate(grads, 0), spread)
        for n, z in enumerate(zr):
            cells = unpooled(values[n * c1 : (n + 1) * c1], place_row(y, n), parity)
            for dy in range(2):
                for dz in range(2):
                    down_ref[2 * y + 2 + dy, 2 * z + 2 + dz] = cells[dy][dz]
        if 0 <= y < ys:
            inputs = []
            for pooled in rows[1:-1]:
                act = jnp.where(pooled > 0, pooled, leak_rate * pooled)
                act = jnp.where(lane < xs, act, 0.0).astype(bf16).astype(f32)
                inputs.append(
                    jnp.concatenate(
                        [pltpu.roll(act, 1, 1), act, pltpu.roll(act, lanes - 1, 1)], 0
                    ).astype(bf16)
                )
            term = dot_nt(around[:, lanes:-lanes], jnp.concatenate(inputs, 1))
            second_sum = term if second_sum is None else second_sum + term

    weights = first_ref[...]
    c0 = grad_ref.shape[0]

    def leave(y):
        return pltpu.make_async_copy(leaving_ref.at[:, y], grad_ref.at[:, y], sent.at[y])

    def plane_step(y, first_sum):
        zr = range(2 * zs)
        around = jnp.concatenate(
            [
                jnp.concatenate([down_ref[y + 3 - ty, z + 3 - tz] for z in zr], 1)
                for ty in range(3)
                for tz in range(3)
            ],
            0,
        )
        terms = dot(weights, around)
        for z in zr:
            at = slice(z * lanes, (z + 1) * lanes)
            left = jnp.where(lane < lanes - 1, pltpu.roll(terms[:8, at], lanes - 1, 1), 0.0)
            right = jnp.where(lane > 0, pltpu.roll(terms[16:, at], 1, 1), 0.0)
            total = left + terms[8:16, at] + right
            for i in range(c0):
                cells_ref[i, y, z : z + 1, :] = total[i : i + 1]
        leaving_ref[:, y] = cells_ref[:, y].astype(bf16)
        leave(y).start()
        return first_sum + dot_nt(around, volume_ref[y])

    first_sum = lax.fori_loop(
        0, 2 * ys, plane_step, jnp.zeros((9 * c1, volume_ref.shape[1]), f32)
    )

    first, second = 0.0, 0.0
    for tap in range(9):
        first += dot(first_sum[tap * c1 : (tap + 1) * c1].astype(bf16), first_order_ref[tap])
        second += dot(second_sum[tap * c2 : (tap + 1) * c2].astype(bf16), second_order_ref[tap])

    shards_dp, count = sums_ref.shape[:2]
    seconds = flat_rows(second, 27 * c1, c2 // shards_dp, shards_dp)
    firsts = flat_rows(first, 27 * c0, c1 // shards_dp, shards_dp)
    for d in range(shards_dp):
        rows = seconds[d] + firsts[d]
        if len(rows) < count:
            rows = rows + [jnp.zeros((count - len(rows), lanes), f32)]
        sums_ref[d] = jnp.concatenate(rows, 0).astype(bf16)
    for y in range(2 * ys):
        leave(y).wait()


def shards(
    volume,
    pooled_first,
    where_first,
    pooled_second,
    where_second,
    upstream,
    kernel_first,
    kernel_second,
):
    dp, gy, gz = (lax.axis_size(a) for a in ("dp", "gy", "gz"))
    c0, c1, c2 = volume.shape[1], pooled_first.shape[1], pooled_second.shape[1]
    ys, zs, xs = pooled_first.shape[2:]

    odd_z, odd_y = lax.axis_index("gz") % 2 == 1, lax.axis_index("gy") % 2 == 1
    odd = jnp.stack([odd_z, odd_y]).astype(jnp.int32)
    smem = pl.BlockSpec(memory_space=pltpu.SMEM)
    vmem = pl.BlockSpec(memory_space=pltpu.VMEM)
    params = pltpu.CompilerParams(vmem_limit_bytes=48 * 1024 * 1024)

    def like(*shape):
        return jax.ShapeDtypeStruct(shape, bf16)

    def pairs_of(axis, begin):
        count = lax.axis_size(axis)
        pairs = [(i, i + 1) for i in range(begin, count - 1, 2)]
        return pairs + [(b, a) for a, b in pairs]

    kinds = 2 if gz > 2 else 1
    raw = (upstream, pooled_second, where_second, pooled_first, where_first)
    plane = like(zs // 2 + 2, 2 * c1, lanes)
    prepared = (plane, plane) + (like(2, 2 * c1, lanes),) * kinds
    even, other, *rims = pl.pallas_call(
        functools.partial(prepare_kernel, kinds),
        out_shape=tuple(pltpu.VMEM(a.shape, a.dtype) for a in prepared),
        in_specs=[smem] + [pl.BlockSpec(memory_space=pltpu.HBM)] * 5,
        out_specs=(vmem,) * (2 + kinds),
        scratch_shapes=[pltpu.VMEM(a.shape, a.dtype) for a in raw]
        + [pltpu.SemaphoreType.DMA((5,))],
        compiler_params=pltpu.CompilerParams(vmem_limit_bytes=49152 * 1024),
    )(odd, *[pltpu.with_memory_space_constraint(a, pltpu.HBM) for a in raw])

    def moved(block, axes, pairs):
        return lax.ppermute(block, axes, pairs) if pairs else jnp.zeros_like(block)

    got_rims = [moved(rim, "gz", pairs_of("gz", n)) for n, rim in enumerate(rims)]
    got_planes = [moved(plane, "gy", pairs_of("gy", n)) for n, plane in enumerate((even, other))]

    def facing(row, rim):
        return jnp.concatenate([row] + [rim[n, :, xs : xs + xs // 2] for n in range(2)], 1)

    low, high = ([facing(rim[y, :, :xs], rim) for rim in got_rims] for y in (0, ys - 1))
    low, high = jnp.stack(low), jnp.stack(high)
    got_rows = [
        moved(jnp.where(odd_y == (n == 0), low, high), "gy", pairs_of("gy", n)) for n in range(2)
    ]

    first = jnp.transpose(kernel_first, (2, 3, 4, 1, 0)).reshape(27, c0, c1)
    second = jnp.transpose(kernel_second, (2, 3, 4, 1, 0)).reshape(27, c1, c2)
    sizes = (ys, zs, xs, c1, c2)
    wide = rows_of(27 * c1) * lanes
    up, places, side_up, side_places, cells, first, second, *orders = pl.pallas_call(
        functools.partial(side_kernel, sizes),
        out_shape=(
            like(ys, zs + 4, c2, lanes),
            like(ys, zs + 2, c1, lanes),
            like(2, 2, zs, c2, lanes),
            like(2, zs, c1, lanes),
            like(2 * ys, 4 * c0, 2 * zs * lanes),
            like(24, 9 * c1),
            like(3 * c1, 9 * c2),
            like(9, 4 * c0, lanes),
            like(9, 3 * c1, wide),
        ),
        in_specs=[smem, [vmem] * 2, [vmem] * kinds, [vmem] * 2, vmem, vmem, vmem],
        out_specs=(vmem,) * 9,
        compiler_params=params,
        cost_estimate=pl.CostEstimate(flops=10**7, bytes_accessed=10**6, transcendentals=0),
    )(odd, [even, other], got_rims, got_planes, volume, first, second)

    sizes1, sizes2 = 27 * c0 * c1 // dp, 27 * c1 * c2 // dp
    sum_rows = -(-(rows_of(sizes1) + rows_of(sizes2)) // 16) * 16
    grad_vol, sums = pl.pallas_call(
        functools.partial(main_kernel, sizes),
        out_shape=(like(*volume.shape[1:]), like(dp, sum_rows, lanes)),
        in_specs=[smem, [vmem] * 2, [vmem] * kinds, [vmem] * 2, [vmem] * 2] + [vmem] * 9,
        out_specs=(pl.BlockSpec(memory_space=pl.ANY), vmem),
        scratch_shapes=[
            pltpu.VMEM((2, 2, 4, c2, lanes), bf16),
            pltpu.VMEM((2 * ys + 4, 2 * zs + 4, c1, lanes), bf16),
            pltpu.VMEM(volume.shape[1:], f32),
            pltpu.VMEM(volume.shape[1:], bf16),
            pltpu.SemaphoreType.DMA((2 * ys,)),
        ],
        compiler_params=params,
        cost_estimate=pl.CostEstimate(
            flops=200_000_000, bytes_accessed=2_000_000, transcendentals=0
        ),
    )(
        odd,
        [even, other],
        got_rims,
        got_planes,
        got_rows,
        up,
        places,
        side_up,
        side_places,
        cells,
        first,
        second,
        *orders,
    )

    sent = jnp.broadcast_to(sums[:, None], (dp, gy * gz) + sums.shape[1:])
    sent = sent.reshape((dp * gy * gz,) + sums.shape[1:])
    got = lax.all_to_all(sent, ("dp", "gy", "gz"), 0, 0, tiled=True)
    count = volume.shape[0] * volume.shape[2] * volume.shape[3] * volume.shape[4] * dp * gy * gz
    total = jnp.sum(got.astype(f32), axis=0)
    split = rows_of(sizes2)
    second_out = total[:split].reshape(-1)[:sizes2] * math.sqrt(64.0 / count)
    first_out = total[split : split + rows_of(sizes1)].reshape(-1)[:sizes1]
    return grad_vol[None], first_out * math.sqrt(8.0 / count), second_out


def solution(mesh):
    cells = P("dp", None, "gy", "gz", None)
    return jax.shard_map(
        shards,
        mesh=mesh,
        in_specs=(cells,) * 6 + (P(), P()),
        out_specs=(cells, P("dp"), P("dp")),
        check_vma=False,
    )
```

```python
import functools
import math

import jax
import jax.numpy as jnp
from jax import lax
from jax.experimental import pallas as pl
from jax.experimental.pallas import tpu as pltpu
from jax.sharding import PartitionSpec as P

leak_rate = 0.3
lanes = 128
f32, bf16 = jnp.float32, jnp.bfloat16


def dot(a, b):
    return lax.dot_general(a, b, (((1,), (0,)), ((), ())), preferred_element_type=f32)


def dot_nt(a, b):
    return lax.dot_general(a, b, (((1,), (1,)), ((), ())), preferred_element_type=f32)


def spread_matrix(first_row, count):
    row = lax.broadcasted_iota(jnp.int32, (lanes, lanes), 0)
    lane = lax.broadcasted_iota(jnp.int32, (lanes, lanes), 1)
    hit = (lane >> 1) + first_row == row
    return jnp.where(hit & (lane < 2 * count), 1.0, 0.0).astype(bf16)


def order_matrix(ins, shape, tap):
    row = lax.broadcasted_iota(jnp.int32, shape, 0)
    column = lax.broadcasted_iota(jnp.int32, shape, 1)
    hit = column == (row % ins) * 27 + 3 * tap + row // ins
    return jnp.where(hit & (row < 3 * ins), 1.0, 0.0).astype(bf16)


def rows_of(count):
    return -(-count // lanes)


def flat_rows(values, length, keep, shards_dp):
    starts = [length * k % lanes for k in range(keep)]
    width = rows_of(max(starts) + length) * lanes
    if values.shape[1] < width:
        blank = jnp.zeros((values.shape[0], width - values.shape[1]), f32)
        values = jnp.concatenate([values, blank], 1)
    turned = {n: pltpu.roll(values, n, 1) if n else values for n in sorted(set(starts))}
    shards = []
    for d in range(shards_dp):
        rows = [None] * rows_of(length * keep)
        for k, start in enumerate(starts):
            for t in range(rows_of(start + length)):
                at = length * k // lanes + t
                piece = turned[start][d * keep + k : d * keep + k + 1, t * lanes : (t + 1) * lanes]
                rows[at] = piece if rows[at] is None else rows[at] + piece
        shards.append(rows)
    return shards


def prepare_kernel(kinds, odd_ref, *refs):
    count = 2 + kinds
    inputs, outputs, refs = refs[:5], refs[5 : 5 + count], refs[5 + count :]
    copies, arrived = refs[:5], refs[5]
    moves = [
        pltpu.make_async_copy(source, target, arrived.at[n])
        for n, (source, target) in enumerate(zip(inputs, copies))
    ]
    for move in moves:
        move.start()
    for move in moves:
        move.wait()
    prepare(odd_ref, *copies, *outputs[:2], outputs[2:])


def prepare(
    odd_ref,
    upstream_ref,
    pooled_second_ref,
    where_second_ref,
    pooled_first_ref,
    where_first_ref,
    even_ref,
    odd_plane_ref,
    rim_refs,
):
    c1, ys, zs, xs = pooled_first_ref.shape[1:]
    zq = zs // 2
    odd_z, odd_y = odd_ref[0] > 0, odd_ref[1] > 0
    slope = jnp.where(pooled_second_ref[0, :, 0].astype(f32) > 0, 1.0, leak_rate)
    value = upstream_ref[0, :, 0].astype(f32) * slope
    place = (where_second_ref[0, :, 0] + 1).astype(f32)
    quarter = [jnp.transpose(part, (1, 0, 2)) for part in (value, place)]
    for n, part in enumerate(quarter):
        row = jnp.concatenate([part[z] for z in range(zq)], 1).astype(bf16)
        even_ref[zq + n] = row
        odd_plane_ref[zq + n] = row
    fill = jnp.zeros((2 * c1, lanes - xs - xs // 2), f32)
    packed = []
    for y in range(ys):
        pooled = jnp.transpose(pooled_first_ref[0, :, y].astype(f32), (1, 0, 2))
        places = jnp.transpose((where_first_ref[0, :, y] + 1).astype(f32), (1, 0, 2))
        rows = [jnp.concatenate([pooled[z], places[z]], 0) for z in range(zs)]
        packed.append(
            [jnp.concatenate([rows[2 * n], rows[2 * n + 1]], 1).astype(bf16) for n in range(zq)]
        )
        low = jnp.concatenate([rows[0], quarter[y][0], fill], 1)
        high = jnp.concatenate([rows[-1], quarter[y][-1], fill], 1)
        for n, ref in enumerate(rim_refs):
            ref[y] = jnp.where(odd_z == (n == 0), low, high).astype(bf16)
    for n in range(zq):
        even_ref[n] = jnp.where(odd_y, packed[0][n], packed[-1][n])
        odd_plane_ref[n] = jnp.where(odd_y, packed[-1][n], packed[0][n])


def sides_of(refs, odd):
    even = refs[0][...]
    other = refs[1][...] if len(refs) > 1 else jnp.zeros_like(even)
    return jnp.where(odd, even, other), jnp.where(odd, other, even)


def unpooled(values, places, parity):
    return [
        [
            jnp.where(places == parity + (4 * dy + 2 * dz), values, 0.0).astype(bf16)
            for dz in range(2)
        ]
        for dy in range(2)
    ]


def lane_parity():
    lane = lax.broadcasted_iota(jnp.int32, (1, lanes), 1)
    return (lane & 1).astype(f32) + 1.0


def spread_quarter(values, places, xs, c2, zq):
    wide = jnp.concatenate([spread_matrix(z * xs // 2, xs // 2) for z in range(zq)], 1)
    found = dot(jnp.concatenate([values, places], 0), wide)
    return [
        (found[:c2, z * lanes : (z + 1) * lanes], found[c2:, z * lanes : (z + 1) * lanes])
        for z in range(zq)
    ]


def spread_places(plane, ends, xs, c1, zq):
    wide = jnp.concatenate([spread_matrix(0, xs), spread_matrix(xs, xs)], 1)
    rows = [plane[n][c1:] for n in range(zq)] + [end[c1:] for end in ends]
    found = dot(jnp.concatenate(rows, 0), wide)
    inner = [
        found[n * c1 : (n + 1) * c1, m * lanes : (m + 1) * lanes]
        for n in range(zq)
        for m in range(2)
    ]
    outer = [found[n * c1 : (n + 1) * c1, :lanes] for n in range(zq, zq + len(ends))]
    return outer[:1] + inner + outer[1:]


def side_kernel(
    sizes,
    odd_ref,
    own_refs,
    rim_refs,
    plane_refs,
    volume_ref,
    first_ref,
    second_ref,
    up_ref,
    places_ref,
    side_up_ref,
    side_places_ref,
    cells_ref,
    first_out_ref,
    second_out_ref,
    first_order_ref,
    second_order_ref,
):
    ys, zs, xs, c1, c2 = sizes
    zlow, zhigh = sides_of(rim_refs, odd_ref[0] > 0)
    own = sides_of(own_refs, odd_ref[1] > 0)
    parity = lane_parity()
    zq = zs // 2
    rows = spread_quarter(own[0][zq], own[0][zq + 1], xs, c2, zq)
    rims = jnp.concatenate([zlow[0], zlow[1], zhigh[0], zhigh[1]], 0)
    rims = dot(rims, spread_matrix(xs, xs // 2))
    rims = [rims[n * c2 : (n + 1) * c2] for n in range(4)]
    rows = [(rims[0], rims[1])] + rows + [(rims[2], rims[3])]
    for n, (value, place) in enumerate(rows):
        cells = unpooled(value, place, parity)
        for dy in range(2):
            for dz in range(2):
                up_ref[dy, 2 * n + dz] = cells[dy][dz]
    for y in range(ys):
        for n, row in enumerate(spread_places(own[y], (zlow[y], zhigh[y]), xs, c1, zq)):
            places_ref[y, n] = row.astype(bf16)
    for side, plane in enumerate(sides_of(plane_refs, odd_ref[1] > 0)):
        for n, (value, place) in enumerate(spread_quarter(plane[zq], plane[zq + 1], xs, c2, zq)):
            cells = unpooled(value, place, parity)
            for dy in range(2):
                for dz in range(2):
                    side_up_ref[side, dy, 2 * n + dz] = cells[dy][dz]
        for n, row in enumerate(spread_places(plane, (), xs, c1, zq)):
            side_places_ref[side, n] = row.astype(bf16)

    lane = lax.broadcasted_iota(jnp.int32, (1, 1, lanes), 2)
    c0, _, zf = volume_ref.shape[1:4]
    for y in range(2 * ys):
        cell = volume_ref[0, :, y].astype(f32)
        moved = [
            jnp.where(lane > 0, pltpu.roll(cell, 1, 2), 0.0),
            cell,
            jnp.where(lane < lanes - 1, pltpu.roll(cell, lanes - 1, 2), 0.0),
            jnp.zeros_like(cell),
        ]
        turned = jnp.transpose(jnp.concatenate(moved, 0), (1, 0, 2))
        for z in range(zf):
            cells_ref[y, :, z * lanes : (z + 1) * lanes] = turned[z].astype(bf16)

    wide = []
    for tap in range(9):
        parts = []
        for tx in range(3):
            parts += [first_ref[3 * tap + tx].astype(f32), jnp.zeros((8 - c0, c1), f32)]
        wide.append(jnp.concatenate(parts, 0))
    first_out_ref[...] = jnp.concatenate(wide, 1).astype(bf16)
    wide = [
        jnp.concatenate([second_ref[3 * tap + tx].astype(f32) for tx in range(3)], 0)
        for tap in range(9)
    ]
    second_out_ref[...] = jnp.concatenate(wide, 1).astype(bf16)
    for tap in range(9):
        first_order_ref[tap] = order_matrix(c0, first_order_ref.shape[1:], tap)
        second_order_ref[tap] = order_matrix(c1, second_order_ref.shape[1:], tap)


def main_kernel(
    sizes,
    odd_ref,
    own_refs,
    rim_refs,
    plane_refs,
    row_refs,
    own_up_ref,
    own_places_ref,
    side_up_ref,
    side_places_ref,
    volume_ref,
    first_ref,
    second_ref,
    first_order_ref,
    second_order_ref,
    grad_ref,
    sums_ref,
    up_ref,
    down_ref,
    cells_ref,
    leaving_ref,
    sent,
):
    ys, zs, xs, c1, c2 = sizes
    zq = zs // 2
    odd_z, odd_y = odd_ref[0] > 0, odd_ref[1] > 0
    zlow, zhigh = sides_of(rim_refs, odd_z)
    own = sides_of(own_refs, odd_y)
    planes = sides_of(plane_refs, odd_y)
    even_rims, other_rims = [
        sides_of([ref[n] for n in range(len(rim_refs))], odd_z) for ref in row_refs
    ]
    plane_rims = [
        [jnp.where(odd_y, even_rims[n], other_rims[n]) for n in range(2)],
        [jnp.where(odd_y, other_rims[n], even_rims[n]) for n in range(2)],
    ]
    parity = lane_parity()
    lane = lax.broadcasted_iota(jnp.int32, (1, lanes), 1)

    near, far = spread_matrix(xs, xs // 2), spread_matrix(xs + xs // 2, xs // 2)
    for side in range(2):
        ends = jnp.concatenate(plane_rims[side], 0)
        values, places = dot(ends, near), dot(ends, far)
        for n in range(2):
            at = slice(n * c2, (n + 1) * c2)
            cells = unpooled(values[at], places[at], parity)
            for dy in range(2):
                for dz in range(2):
                    up_ref[side, dy, 2 * n + dz] = cells[dy][dz]

    def up_row(y, z):
        if 0 <= y < ys:
            return own_up_ref[y, z + 2]
        side, dy = (0, y + 2) if y < 0 else (1, y - ys)
        if 0 <= z < zs:
            return side_up_ref[side, dy, z]
        return up_ref[side, dy, z + 2 if z < 0 else z + 2 - zs]

    def pooled_row(y, z):
        side = None if 0 <= y < ys else int(y >= ys)
        if 0 <= z < zs:
            plane = own[y] if side is None else planes[side]
            row = plane[z // 2][:c1].astype(f32)
            return pltpu.roll(row, lanes - xs, 1) if z % 2 else row
        at = int(z >= 0)
        rim = (zlow, zhigh)[at][y] if side is None else plane_rims[side][at]
        return rim[:c1].astype(f32)

    rim_places = jnp.concatenate([end[c1:] for rims in plane_rims for end in rims], 0)
    rim_places = dot(rim_places, spread_matrix(0, xs))

    def place_row(y, n):
        if 0 <= y < ys:
            return own_places_ref[y, n].astype(f32)
        side = int(y >= ys)
        if 0 < n <= zs:
            return side_places_ref[side, n - 1].astype(f32)
        at = 2 * side + int(n > 0)
        return rim_places[at * c1 : (at + 1) * c1]

    spread = spread_matrix(0, xs)
    weights = second_ref[...]
    second_sum = None
    for y in range(-1, ys + 1):
        zr = range(-1, zs + 1)
        around = jnp.concatenate(
            [
                jnp.concatenate([up_row(y + 1 - ty, z + 1 - tz) for z in zr], 1)
                for ty in range(3)
                for tz in range(3)
            ],
            0,
        )
        terms = dot(weights, around)
        rows = [pooled_row(y, z) for z in zr]
        grads = []
        for n, pooled in enumerate(rows):
            at = slice(n * lanes, (n + 1) * lanes)
            total = (
                pltpu.roll(terms[:c1, at], lanes - 1, 1)
                + terms[c1 : 2 * c1, at]
                + pltpu.roll(terms[2 * c1 :, at], 1, 1)
            )
            grads.append((total * jnp.where(pooled > 0, 1.0, leak_rate)).astype(bf16))
        values = dot(jnp.concatenate(grads, 0), spread)
        for n, z in enumerate(zr):
            cells = unpooled(values[n * c1 : (n + 1) * c1], place_row(y, n), parity)
            for dy in range(2):
                for dz in range(2):
                    down_ref[2 * y + 2 + dy, 2 * z + 2 + dz] = cells[dy][dz]
        if 0 <= y < ys:
            inputs = []
            for pooled in rows[1:-1]:
                act = jnp.where(pooled > 0, pooled, leak_rate * pooled)
                act = jnp.where(lane < xs, act, 0.0).astype(bf16).astype(f32)
                inputs.append(
                    jnp.concatenate(
                        [pltpu.roll(act, 1, 1), act, pltpu.roll(act, lanes - 1, 1)], 0
                    ).astype(bf16)
                )
            term = dot_nt(around[:, lanes:-lanes], jnp.concatenate(inputs, 1))
            second_sum = term if second_sum is None else second_sum + term

    weights = first_ref[...]
    first_sum = None
    leaving = []
    c0 = grad_ref.shape[0]
    for y in range(2 * ys):
        zr = range(2 * zs)
        around = jnp.concatenate(
            [
                jnp.concatenate([down_ref[y + 3 - ty, z + 3 - tz] for z in zr], 1)
                for ty in range(3)
                for tz in range(3)
            ],
            0,
        )
        terms = dot(weights, around)
        for z in zr:
            at = slice(z * lanes, (z + 1) * lanes)
            left = jnp.where(lane < lanes - 1, pltpu.roll(terms[:8, at], lanes - 1, 1), 0.0)
            right = jnp.where(lane > 0, pltpu.roll(terms[16:, at], 1, 1), 0.0)
            total = left + terms[8:16, at] + right
            for i in range(c0):
                cells_ref[i, y, z : z + 1, :] = total[i : i + 1]
        leaving_ref[:, y] = cells_ref[:, y].astype(bf16)
        leaving.append(pltpu.make_async_copy(leaving_ref.at[:, y], grad_ref.at[:, y], sent.at[y]))
        leaving[y].start()
        term = dot_nt(around, volume_ref[y])
        first_sum = term if first_sum is None else first_sum + term

    first, second = 0.0, 0.0
    for tap in range(9):
        first += dot(first_sum[tap * c1 : (tap + 1) * c1].astype(bf16), first_order_ref[tap])
        second += dot(second_sum[tap * c2 : (tap + 1) * c2].astype(bf16), second_order_ref[tap])

    shards_dp, count = sums_ref.shape[:2]
    seconds = flat_rows(second, 27 * c1, c2 // shards_dp, shards_dp)
    firsts = flat_rows(first, 27 * c0, c1 // shards_dp, shards_dp)
    for d in range(shards_dp):
        rows = seconds[d] + firsts[d]
        if len(rows) < count:
            rows = rows + [jnp.zeros((count - len(rows), lanes), f32)]
        sums_ref[d] = jnp.concatenate(rows, 0).astype(bf16)
    for move in leaving:
        move.wait()


def shards(
    volume,
    pooled_first,
    where_first,
    pooled_second,
    where_second,
    upstream,
    kernel_first,
    kernel_second,
):
    dp, gy, gz = (lax.axis_size(a) for a in ("dp", "gy", "gz"))
    c0, c1, c2 = volume.shape[1], pooled_first.shape[1], pooled_second.shape[1]
    ys, zs, xs = pooled_first.shape[2:]

    odd_z, odd_y = lax.axis_index("gz") % 2 == 1, lax.axis_index("gy") % 2 == 1
    odd = jnp.stack([odd_z, odd_y]).astype(jnp.int32)
    smem = pl.BlockSpec(memory_space=pltpu.SMEM)
    vmem = pl.BlockSpec(memory_space=pltpu.VMEM)
    params = pltpu.CompilerParams(vmem_limit_bytes=48 * 1024 * 1024)

    def like(*shape):
        return jax.ShapeDtypeStruct(shape, bf16)

    def pairs_of(axis, begin):
        count = lax.axis_size(axis)
        pairs = [(i, i + 1) for i in range(begin, count - 1, 2)]
        return pairs + [(b, a) for a, b in pairs]

    kinds = 2 if gz > 2 else 1
    raw = (upstream, pooled_second, where_second, pooled_first, where_first)
    plane = like(zs // 2 + 2, 2 * c1, lanes)
    prepared = (plane, plane) + (like(2, 2 * c1, lanes),) * kinds
    even, other, *rims = pl.pallas_call(
        functools.partial(prepare_kernel, kinds),
        out_shape=tuple(pltpu.VMEM(a.shape, a.dtype) for a in prepared),
        in_specs=[smem] + [pl.BlockSpec(memory_space=pltpu.HBM)] * 5,
        out_specs=(vmem,) * (2 + kinds),
        scratch_shapes=[pltpu.VMEM(a.shape, a.dtype) for a in raw]
        + [pltpu.SemaphoreType.DMA((5,))],
        compiler_params=pltpu.CompilerParams(vmem_limit_bytes=49152 * 1024),
    )(odd, *[pltpu.with_memory_space_constraint(a, pltpu.HBM) for a in raw])

    def moved(block, axes, pairs):
        return lax.ppermute(block, axes, pairs) if pairs else jnp.zeros_like(block)

    got_rims = [moved(rim, "gz", pairs_of("gz", n)) for n, rim in enumerate(rims)]
    got_planes = [moved(plane, "gy", pairs_of("gy", n)) for n, plane in enumerate((even, other))]

    def facing(row, rim):
        return jnp.concatenate([row] + [rim[n, :, xs : xs + xs // 2] for n in range(2)], 1)

    low, high = ([facing(rim[y, :, :xs], rim) for rim in got_rims] for y in (0, ys - 1))
    low, high = jnp.stack(low), jnp.stack(high)
    got_rows = [
        moved(jnp.where(odd_y == (n == 0), low, high), "gy", pairs_of("gy", n)) for n in range(2)
    ]

    first = jnp.transpose(kernel_first, (2, 3, 4, 1, 0)).reshape(27, c0, c1)
    second = jnp.transpose(kernel_second, (2, 3, 4, 1, 0)).reshape(27, c1, c2)
    sizes = (ys, zs, xs, c1, c2)
    wide = rows_of(27 * c1) * lanes
    up, places, side_up, side_places, cells, first, second, *orders = pl.pallas_call(
        functools.partial(side_kernel, sizes),
        out_shape=(
            like(ys, zs + 4, c2, lanes),
            like(ys, zs + 2, c1, lanes),
            like(2, 2, zs, c2, lanes),
            like(2, zs, c1, lanes),
            like(2 * ys, 4 * c0, 2 * zs * lanes),
            like(24, 9 * c1),
            like(3 * c1, 9 * c2),
            like(9, 4 * c0, lanes),
            like(9, 3 * c1, wide),
        ),
        in_specs=[smem, [vmem] * 2, [vmem] * kinds, [vmem] * 2, vmem, vmem, vmem],
        out_specs=(vmem,) * 9,
        compiler_params=params,
        cost_estimate=pl.CostEstimate(flops=10**7, bytes_accessed=10**6, transcendentals=0),
    )(odd, [even, other], got_rims, got_planes, volume, first, second)

    sizes1, sizes2 = 27 * c0 * c1 // dp, 27 * c1 * c2 // dp
    sum_rows = -(-(rows_of(sizes1) + rows_of(sizes2)) // 32) * 32
    grad_vol, sums = pl.pallas_call(
        functools.partial(main_kernel, sizes),
        out_shape=(like(*volume.shape[1:]), like(dp, sum_rows, lanes)),
        in_specs=[smem, [vmem] * 2, [vmem] * kinds, [vmem] * 2, [vmem] * 2] + [vmem] * 9,
        out_specs=(pl.BlockSpec(memory_space=pl.ANY), vmem),
        scratch_shapes=[
            pltpu.VMEM((2, 2, 4, c2, lanes), bf16),
            pltpu.VMEM((2 * ys + 4, 2 * zs + 4, c1, lanes), bf16),
            pltpu.VMEM(volume.shape[1:], f32),
            pltpu.VMEM(volume.shape[1:], bf16),
            pltpu.SemaphoreType.DMA((2 * ys,)),
        ],
        compiler_params=params,
        cost_estimate=pl.CostEstimate(
            flops=200_000_000, bytes_accessed=2_000_000, transcendentals=0
        ),
    )(
        odd,
        [even, other],
        got_rims,
        got_planes,
        got_rows,
        up,
        places,
        side_up,
        side_places,
        cells,
        first,
        second,
        *orders,
    )

    half = sum_rows // 2
    low, high = sums[:, :half], sums[:, half:]
    other = lax.ppermute(jnp.where(odd_y, low, high), "gy", pairs_of("gy", 0))
    part = jnp.where(odd_y, high, low).astype(f32) + other.astype(f32)
    sent = jnp.broadcast_to(part.astype(bf16)[:, None], (dp, gy * gz) + part.shape[1:])
    sent = sent.reshape((dp * gy * gz,) + part.shape[1:])
    got = lax.all_to_all(sent, ("dp", "gy", "gz"), 0, 0, tiled=True)
    got = got.reshape((dp * gy // 2, 2, gz) + part.shape[1:])
    count = volume.shape[0] * volume.shape[2] * volume.shape[3] * volume.shape[4] * dp * gy * gz
    total = jnp.sum(got.astype(f32), axis=(0, 2)).reshape(sum_rows, lanes)
    split = rows_of(sizes2)
    second_out = total[:split].reshape(-1)[:sizes2] * math.sqrt(64.0 / count)
    first_out = total[split : split + rows_of(sizes1)].reshape(-1)[:sizes1]
    return grad_vol[None], first_out * math.sqrt(8.0 / count), second_out


def solution(mesh):
    cells = P("dp", None, "gy", "gz", None)
    return jax.shard_map(
        shards,
        mesh=mesh,
        in_specs=(cells,) * 6 + (P(), P()),
        out_specs=(cells, P("dp"), P("dp")),
        check_vma=False,
    )
```

```python
import functools
import math

import jax
import jax.numpy as jnp
from jax import lax
from jax.experimental import pallas as pl
from jax.experimental.pallas import tpu as pltpu
from jax.sharding import PartitionSpec as P

leak_rate = 0.3
lanes = 128
f32, bf16 = jnp.float32, jnp.bfloat16


def dot(a, b):
    return lax.dot_general(a, b, (((1,), (0,)), ((), ())), preferred_element_type=f32)


def dot_nt(a, b):
    return lax.dot_general(a, b, (((1,), (1,)), ((), ())), preferred_element_type=f32)


def spread_matrix(first_row, count):
    row = lax.broadcasted_iota(jnp.int32, (lanes, lanes), 0)
    lane = lax.broadcasted_iota(jnp.int32, (lanes, lanes), 1)
    hit = (lane >> 1) + first_row == row
    return jnp.where(hit & (lane < 2 * count), 1.0, 0.0).astype(bf16)


def order_matrix(ins, shape, tap):
    row = lax.broadcasted_iota(jnp.int32, shape, 0)
    column = lax.broadcasted_iota(jnp.int32, shape, 1)
    hit = column == (row % ins) * 27 + 3 * tap + row // ins
    return jnp.where(hit & (row < 3 * ins), 1.0, 0.0).astype(bf16)


def rows_of(count):
    return -(-count // lanes)


def flat_rows(values, length, keep, shards_dp):
    starts = [length * k % lanes for k in range(keep)]
    width = rows_of(max(starts) + length) * lanes
    if values.shape[1] < width:
        blank = jnp.zeros((values.shape[0], width - values.shape[1]), f32)
        values = jnp.concatenate([values, blank], 1)
    turned = {n: pltpu.roll(values, n, 1) if n else values for n in sorted(set(starts))}
    shards = []
    for d in range(shards_dp):
        rows = [None] * rows_of(length * keep)
        for k, start in enumerate(starts):
            for t in range(rows_of(start + length)):
                at = length * k // lanes + t
                piece = turned[start][d * keep + k : d * keep + k + 1, t * lanes : (t + 1) * lanes]
                rows[at] = piece if rows[at] is None else rows[at] + piece
        shards.append(rows)
    return shards


def prepare_kernel(kinds, odd_ref, *refs):
    count = 2 + kinds
    inputs, outputs, refs = refs[:5], refs[5 : 5 + count], refs[5 + count :]
    copies, arrived = refs[:5], refs[5]
    moves = [
        pltpu.make_async_copy(source, target, arrived.at[n])
        for n, (source, target) in enumerate(zip(inputs, copies))
    ]
    for move in moves:
        move.start()
    for move in moves:
        move.wait()
    prepare(odd_ref, *copies, *outputs[:2], outputs[2:])


def prepare(
    odd_ref,
    upstream_ref,
    pooled_second_ref,
    where_second_ref,
    pooled_first_ref,
    where_first_ref,
    even_ref,
    odd_plane_ref,
    rim_refs,
):
    c1, ys, zs, xs = pooled_first_ref.shape[1:]
    zq = zs // 2
    odd_z, odd_y = odd_ref[0] > 0, odd_ref[1] > 0
    slope = jnp.where(pooled_second_ref[0, :, 0].astype(f32) > 0, 1.0, leak_rate)
    value = upstream_ref[0, :, 0].astype(f32) * slope
    place = (where_second_ref[0, :, 0] + 1).astype(f32)
    quarter = [jnp.transpose(part, (1, 0, 2)) for part in (value, place)]
    for n, part in enumerate(quarter):
        row = jnp.concatenate([part[z] for z in range(zq)], 1).astype(bf16)
        even_ref[zq + n] = row
        odd_plane_ref[zq + n] = row
    fill = jnp.zeros((2 * c1, lanes - xs - xs // 2), f32)
    packed = []
    for y in range(ys):
        pooled = jnp.transpose(pooled_first_ref[0, :, y].astype(f32), (1, 0, 2))
        places = jnp.transpose((where_first_ref[0, :, y] + 1).astype(f32), (1, 0, 2))
        rows = [jnp.concatenate([pooled[z], places[z]], 0) for z in range(zs)]
        packed.append(
            [jnp.concatenate([rows[2 * n], rows[2 * n + 1]], 1).astype(bf16) for n in range(zq)]
        )
        low = jnp.concatenate([rows[0], quarter[y][0], fill], 1)
        high = jnp.concatenate([rows[-1], quarter[y][-1], fill], 1)
        for n, ref in enumerate(rim_refs):
            ref[y] = jnp.where(odd_z == (n == 0), low, high).astype(bf16)
    for n in range(zq):
        even_ref[n] = jnp.where(odd_y, packed[0][n], packed[-1][n])
        odd_plane_ref[n] = jnp.where(odd_y, packed[-1][n], packed[0][n])


def sides_of(refs, odd):
    even = refs[0][...]
    other = refs[1][...] if len(refs) > 1 else jnp.zeros_like(even)
    return jnp.where(odd, even, other), jnp.where(odd, other, even)


def unpooled(values, places, parity):
    return [
        [
            jnp.where(places == parity + (4 * dy + 2 * dz), values, 0.0).astype(bf16)
            for dz in range(2)
        ]
        for dy in range(2)
    ]


def lane_parity():
    lane = lax.broadcasted_iota(jnp.int32, (1, lanes), 1)
    return (lane & 1).astype(f32) + 1.0


def spread_quarter(values, places, xs, c2, zq):
    wide = jnp.concatenate([spread_matrix(z * xs // 2, xs // 2) for z in range(zq)], 1)
    found = dot(jnp.concatenate([values, places], 0), wide)
    return [
        (found[:c2, z * lanes : (z + 1) * lanes], found[c2:, z * lanes : (z + 1) * lanes])
        for z in range(zq)
    ]


def spread_places(plane, ends, xs, c1, zq):
    wide = jnp.concatenate([spread_matrix(0, xs), spread_matrix(xs, xs)], 1)
    rows = [plane[n][c1:] for n in range(zq)] + [end[c1:] for end in ends]
    found = dot(jnp.concatenate(rows, 0), wide)
    inner = [
        found[n * c1 : (n + 1) * c1, m * lanes : (m + 1) * lanes]
        for n in range(zq)
        for m in range(2)
    ]
    low, high = found[zq * c1 : (zq + 1) * c1, :lanes], found[(zq + 1) * c1 :, :lanes]
    return [low] + inner + [high]


def side_kernel(
    sizes,
    odd_ref,
    own_refs,
    rim_refs,
    volume_ref,
    first_ref,
    second_ref,
    up_ref,
    places_ref,
    cells_ref,
    first_out_ref,
    second_out_ref,
    first_order_ref,
    second_order_ref,
):
    ys, zs, xs, c1, c2 = sizes
    zlow, zhigh = sides_of(rim_refs, odd_ref[0] > 0)
    own = sides_of(own_refs, odd_ref[1] > 0)
    parity = lane_parity()
    zq = zs // 2
    rows = spread_quarter(own[0][zq], own[0][zq + 1], xs, c2, zq)
    rims = jnp.concatenate([zlow[0], zlow[1], zhigh[0], zhigh[1]], 0)
    rims = dot(rims, spread_matrix(xs, xs // 2))
    rims = [rims[n * c2 : (n + 1) * c2] for n in range(4)]
    rows = [(rims[0], rims[1])] + rows + [(rims[2], rims[3])]
    for n, (value, place) in enumerate(rows):
        cells = unpooled(value, place, parity)
        for dy in range(2):
            for dz in range(2):
                up_ref[dy, 2 * n + dz] = cells[dy][dz]
    for y in range(ys):
        for n, row in enumerate(spread_places(own[y], (zlow[y], zhigh[y]), xs, c1, zq)):
            places_ref[y, n] = row.astype(bf16)

    lane = lax.broadcasted_iota(jnp.int32, (1, 1, lanes), 2)
    c0, _, zf = volume_ref.shape[1:4]
    for y in range(2 * ys):
        cell = volume_ref[0, :, y].astype(f32)
        moved = [
            jnp.where(lane > 0, pltpu.roll(cell, 1, 2), 0.0),
            cell,
            jnp.where(lane < lanes - 1, pltpu.roll(cell, lanes - 1, 2), 0.0),
            jnp.zeros_like(cell),
        ]
        turned = jnp.transpose(jnp.concatenate(moved, 0), (1, 0, 2))
        for z in range(zf):
            cells_ref[y, :, z * lanes : (z + 1) * lanes] = turned[z].astype(bf16)

    wide = []
    for tap in range(9):
        parts = []
        for tx in range(3):
            parts += [first_ref[3 * tap + tx].astype(f32), jnp.zeros((8 - c0, c1), f32)]
        wide.append(jnp.concatenate(parts, 0))
    first_out_ref[...] = jnp.concatenate(wide, 1).astype(bf16)
    wide = [
        jnp.concatenate([second_ref[3 * tap + tx].astype(f32) for tx in range(3)], 0)
        for tap in range(9)
    ]
    second_out_ref[...] = jnp.concatenate(wide, 1).astype(bf16)
    for tap in range(9):
        first_order_ref[tap] = order_matrix(c0, first_order_ref.shape[1:], tap)
        second_order_ref[tap] = order_matrix(c1, second_order_ref.shape[1:], tap)


def main_kernel(
    sizes,
    odd_ref,
    own_refs,
    rim_refs,
    plane_refs,
    row_refs,
    own_up_ref,
    own_places_ref,
    volume_ref,
    first_ref,
    second_ref,
    first_order_ref,
    second_order_ref,
    grad_ref,
    sums_ref,
    up_ref,
    down_ref,
    cells_ref,
    leaving_ref,
    sent,
):
    ys, zs, xs, c1, c2 = sizes
    zq = zs // 2
    odd_z, odd_y = odd_ref[0] > 0, odd_ref[1] > 0
    zlow, zhigh = sides_of(rim_refs, odd_z)
    own = sides_of(own_refs, odd_y)
    planes = sides_of(plane_refs, odd_y)
    even_rims, other_rims = [
        sides_of([ref[n] for n in range(len(rim_refs))], odd_z) for ref in row_refs
    ]
    plane_rims = [
        [jnp.where(odd_y, even_rims[n], other_rims[n]) for n in range(2)],
        [jnp.where(odd_y, other_rims[n], even_rims[n]) for n in range(2)],
    ]
    parity = lane_parity()
    lane = lax.broadcasted_iota(jnp.int32, (1, lanes), 1)

    near, far = spread_matrix(xs, xs // 2), spread_matrix(xs + xs // 2, xs // 2)
    for side in range(2):
        plane, (low, high) = planes[side], plane_rims[side]
        ends = jnp.concatenate([low, high], 0)
        values, places = dot(ends, near), dot(ends, far)
        rows = spread_quarter(plane[zq], plane[zq + 1], xs, c2, zq)
        rows = [(values[:c2], places[:c2])] + rows + [(values[c2:], places[c2:])]
        for n, (value, place) in enumerate(rows):
            cells = unpooled(value, place, parity)
            for dy in range(2):
                for dz in range(2):
                    up_ref[side, dy, 2 * n + dz] = cells[dy][dz]

    def up_row(y, z):
        if y < 0:
            return up_ref[0, y + 2, z + 2]
        return own_up_ref[y, z + 2] if y < ys else up_ref[1, y - ys, z + 2]

    def pooled_row(y, z):
        side = None if 0 <= y < ys else int(y >= ys)
        if 0 <= z < zs:
            plane = own[y] if side is None else planes[side]
            row = plane[z // 2][:c1].astype(f32)
            return pltpu.roll(row, lanes - xs, 1) if z % 2 else row
        at = int(z >= 0)
        rim = (zlow, zhigh)[at][y] if side is None else plane_rims[side][at]
        return rim[:c1].astype(f32)

    plane_places = [
        spread_places(planes[side], plane_rims[side], xs, c1, zq) for side in range(2)
    ]

    spread = spread_matrix(0, xs)
    weights = second_ref[...]
    second_sum = None
    for y in range(-1, ys + 1):
        zr = range(-1, zs + 1)
        around = jnp.concatenate(
            [
                jnp.concatenate([up_row(y + 1 - ty, z + 1 - tz) for z in zr], 1)
                for ty in range(3)
                for tz in range(3)
            ],
            0,
        )
        terms = dot(weights, around)
        rows = [pooled_row(y, z) for z in zr]
        grads = []
        for n, pooled in enumerate(rows):
            at = slice(n * lanes, (n + 1) * lanes)
            total = (
                pltpu.roll(terms[:c1, at], lanes - 1, 1)
                + terms[c1 : 2 * c1, at]
                + pltpu.roll(terms[2 * c1 :, at], 1, 1)
            )
            grads.append((total * jnp.where(pooled > 0, 1.0, leak_rate)).astype(bf16))
        values = dot(jnp.concatenate(grads, 0), spread)
        for n, z in enumerate(zr):
            if 0 <= y < ys:
                place = own_places_ref[y, n].astype(f32)
            else:
                place = plane_places[int(y >= ys)][n]
            cells = unpooled(values[n * c1 : (n + 1) * c1], place, parity)
            for dy in range(2):
                for dz in range(2):
                    down_ref[2 * y + 2 + dy, 2 * z + 2 + dz] = cells[dy][dz]
        if 0 <= y < ys:
            inputs = []
            for pooled in rows[1:-1]:
                act = jnp.where(pooled > 0, pooled, leak_rate * pooled)
                act = jnp.where(lane < xs, act, 0.0).astype(bf16).astype(f32)
                inputs.append(
                    jnp.concatenate(
                        [pltpu.roll(act, 1, 1), act, pltpu.roll(act, lanes - 1, 1)], 0
                    ).astype(bf16)
                )
            term = dot_nt(jnp.concatenate(inputs, 1), around[:, lanes:-lanes])
            second_sum = term if second_sum is None else second_sum + term

    weights = first_ref[...]
    first_sum = None
    leaving = []
    c0 = grad_ref.shape[0]
    for y in range(2 * ys):
        zr = range(2 * zs)
        around = jnp.concatenate(
            [
                jnp.concatenate([down_ref[y + 3 - ty, z + 3 - tz] for z in zr], 1)
                for ty in range(3)
                for tz in range(3)
            ],
            0,
        )
        terms = dot(weights, around)
        for z in zr:
            at = slice(z * lanes, (z + 1) * lanes)
            left = jnp.where(lane < lanes - 1, pltpu.roll(terms[:8, at], lanes - 1, 1), 0.0)
            right = jnp.where(lane > 0, pltpu.roll(terms[16:, at], 1, 1), 0.0)
            total = left + terms[8:16, at] + right
            for i in range(c0):
                cells_ref[i, y, z : z + 1, :] = total[i : i + 1]
        leaving_ref[:, y] = cells_ref[:, y].astype(bf16)
        leaving.append(pltpu.make_async_copy(leaving_ref.at[:, y], grad_ref.at[:, y], sent.at[y]))
        leaving[y].start()
        term = dot_nt(volume_ref[y], around)
        first_sum = term if first_sum is None else first_sum + term

    first_sum, second_sum = first_sum.T, second_sum.T
    first, second = 0.0, 0.0
    for tap in range(9):
        first += dot(first_sum[tap * c1 : (tap + 1) * c1].astype(bf16), first_order_ref[tap])
        second += dot(second_sum[tap * c2 : (tap + 1) * c2].astype(bf16), second_order_ref[tap])

    shards_dp, count = sums_ref.shape[:2]
    seconds = flat_rows(second, 27 * c1, c2 // shards_dp, shards_dp)
    firsts = flat_rows(first, 27 * c0, c1 // shards_dp, shards_dp)
    for d in range(shards_dp):
        rows = seconds[d] + firsts[d]
        if len(rows) < count:
            rows = rows + [jnp.zeros((count - len(rows), lanes), f32)]
        sums_ref[d] = jnp.concatenate(rows, 0).astype(bf16)
    for move in leaving:
        move.wait()


def shards(
    volume,
    pooled_first,
    where_first,
    pooled_second,
    where_second,
    upstream,
    kernel_first,
    kernel_second,
):
    dp, gy, gz = (lax.axis_size(a) for a in ("dp", "gy", "gz"))
    c0, c1, c2 = volume.shape[1], pooled_first.shape[1], pooled_second.shape[1]
    ys, zs, xs = pooled_first.shape[2:]

    odd_z, odd_y = lax.axis_index("gz") % 2 == 1, lax.axis_index("gy") % 2 == 1
    odd = jnp.stack([odd_z, odd_y]).astype(jnp.int32)
    smem = pl.BlockSpec(memory_space=pltpu.SMEM)
    vmem = pl.BlockSpec(memory_space=pltpu.VMEM)
    params = pltpu.CompilerParams(vmem_limit_bytes=48 * 1024 * 1024)

    def like(*shape):
        return jax.ShapeDtypeStruct(shape, bf16)

    def pairs_of(axis, begin):
        count = lax.axis_size(axis)
        pairs = [(i, i + 1) for i in range(begin, count - 1, 2)]
        return pairs + [(b, a) for a, b in pairs]

    kinds = 2 if gz > 2 else 1
    raw = (upstream, pooled_second, where_second, pooled_first, where_first)
    plane = like(zs // 2 + 2, 2 * c1, lanes)
    prepared = (plane, plane) + (like(2, 2 * c1, lanes),) * kinds
    even, other, *rims = pl.pallas_call(
        functools.partial(prepare_kernel, kinds),
        out_shape=tuple(pltpu.VMEM(a.shape, a.dtype) for a in prepared),
        in_specs=[smem] + [pl.BlockSpec(memory_space=pltpu.HBM)] * 5,
        out_specs=(vmem,) * (2 + kinds),
        scratch_shapes=[pltpu.VMEM(a.shape, a.dtype) for a in raw]
        + [pltpu.SemaphoreType.DMA((5,))],
        compiler_params=pltpu.CompilerParams(vmem_limit_bytes=49152 * 1024),
    )(odd, *[pltpu.with_memory_space_constraint(a, pltpu.HBM) for a in raw])

    def moved(block, axes, pairs):
        return lax.ppermute(block, axes, pairs) if pairs else jnp.zeros_like(block)

    got_rims = [moved(rim, "gz", pairs_of("gz", n)) for n, rim in enumerate(rims)]
    got_planes = [moved(plane, "gy", pairs_of("gy", n)) for n, plane in enumerate((even, other))]

    def facing(row, rim):
        return jnp.concatenate([row] + [rim[n, :, xs : xs + xs // 2] for n in range(2)], 1)

    low, high = ([facing(rim[y, :, :xs], rim) for rim in got_rims] for y in (0, ys - 1))
    low, high = jnp.stack(low), jnp.stack(high)
    got_rows = [
        moved(jnp.where(odd_y == (n == 0), low, high), "gy", pairs_of("gy", n)) for n in range(2)
    ]

    first = jnp.transpose(kernel_first, (2, 3, 4, 1, 0)).reshape(27, c0, c1)
    second = jnp.transpose(kernel_second, (2, 3, 4, 1, 0)).reshape(27, c1, c2)
    sizes = (ys, zs, xs, c1, c2)
    wide = rows_of(27 * c1) * lanes
    up, places, cells, first, second, *orders = pl.pallas_call(
        functools.partial(side_kernel, sizes),
        out_shape=(
            like(ys, zs + 4, c2, lanes),
            like(ys, zs + 2, c1, lanes),
            like(2 * ys, 4 * c0, 2 * zs * lanes),
            like(24, 9 * c1),
            like(3 * c1, 9 * c2),
            like(9, 4 * c0, lanes),
            like(9, 3 * c1, wide),
        ),
        in_specs=[smem, [vmem] * 2, [vmem] * kinds, vmem, vmem, vmem],
        out_specs=(vmem,) * 7,
        compiler_params=params,
        cost_estimate=pl.CostEstimate(flops=10**7, bytes_accessed=10**6, transcendentals=0),
    )(odd, [even, other], got_rims, volume, first, second)

    sizes1, sizes2 = 27 * c0 * c1 // dp, 27 * c1 * c2 // dp
    sum_rows = -(-(rows_of(sizes1) + rows_of(sizes2)) // 32) * 32
    grad_vol, sums = pl.pallas_call(
        functools.partial(main_kernel, sizes),
        out_shape=(like(*volume.shape[1:]), like(dp, sum_rows, lanes)),
        in_specs=[smem, [vmem] * 2, [vmem] * kinds, [vmem] * 2, [vmem] * 2] + [vmem] * 7,
        out_specs=(pl.BlockSpec(memory_space=pl.ANY), vmem),
        scratch_shapes=[
            pltpu.VMEM((2, 2, zs + 4, c2, lanes), bf16),
            pltpu.VMEM((2 * ys + 4, 2 * zs + 4, c1, lanes), bf16),
            pltpu.VMEM(volume.shape[1:], f32),
            pltpu.VMEM(volume.shape[1:], bf16),
            pltpu.SemaphoreType.DMA((2 * ys,)),
        ],
        compiler_params=params,
        cost_estimate=pl.CostEstimate(
            flops=200_000_000, bytes_accessed=2_000_000, transcendentals=0
        ),
    )(
        odd,
        [even, other],
        got_rims,
        got_planes,
        got_rows,
        up,
        places,
        cells,
        first,
        second,
        *orders,
    )

    half = sum_rows // 2
    low, high = sums[:, :half], sums[:, half:]
    other = lax.ppermute(jnp.where(odd_y, low, high), "gy", pairs_of("gy", 0))
    part = jnp.where(odd_y, high, low).astype(f32) + other.astype(f32)
    sent = jnp.broadcast_to(part.astype(bf16)[:, None], (dp, gy * gz) + part.shape[1:])
    sent = sent.reshape((dp * gy * gz,) + part.shape[1:])
    got = lax.all_to_all(sent, ("dp", "gy", "gz"), 0, 0, tiled=True)
    got = got.reshape((dp * gy // 2, 2, gz) + part.shape[1:])
    count = volume.shape[0] * volume.shape[2] * volume.shape[3] * volume.shape[4] * dp * gy * gz
    total = jnp.sum(got.astype(f32), axis=(0, 2)).reshape(sum_rows, lanes)
    split = rows_of(sizes2)
    second_out = total[:split].reshape(-1)[:sizes2] * math.sqrt(64.0 / count)
    first_out = total[split : split + rows_of(sizes1)].reshape(-1)[:sizes1]
    return grad_vol[None], first_out * math.sqrt(8.0 / count), second_out


def solution(mesh):
    cells = P("dp", None, "gy", "gz", None)
    return jax.shard_map(
        shards,
        mesh=mesh,
        in_specs=(cells,) * 6 + (P(), P()),
        out_specs=(cells, P("dp"), P("dp")),
        check_vma=False,
    )
```

```python
import functools
import math

import jax
import jax.numpy as jnp
from jax import lax
from jax.experimental import pallas as pl
from jax.experimental.pallas import tpu as pltpu
from jax.sharding import PartitionSpec as P

leak_rate = 0.3
lanes = 128
f32, bf16 = jnp.float32, jnp.bfloat16


def dot(a, b):
    return lax.dot_general(a, b, (((1,), (0,)), ((), ())), preferred_element_type=f32)


def dot_nt(a, b):
    return lax.dot_general(a, b, (((1,), (1,)), ((), ())), preferred_element_type=f32)


def spread_matrix(first_row, count):
    row = lax.broadcasted_iota(jnp.int32, (lanes, lanes), 0)
    lane = lax.broadcasted_iota(jnp.int32, (lanes, lanes), 1)
    hit = (lane >> 1) + first_row == row
    return jnp.where(hit & (lane < 2 * count), 1.0, 0.0).astype(bf16)


def order_matrix(ins, step, shape, tz):
    row = lax.broadcasted_iota(jnp.int32, shape, 0)
    column = lax.broadcasted_iota(jnp.int32, shape, 1)
    at = row % step
    hit = column == (at % ins) * 27 + 9 * (row // step) + 3 * tz + at // ins
    return jnp.where(hit & (at < 3 * ins), 1.0, 0.0).astype(bf16)


def rows_of(count):
    return -(-count // lanes)


def flat_rows(values, length, keep, shards_dp):
    starts = [length * k % lanes for k in range(keep)]
    width = rows_of(max(starts) + length) * lanes
    if values.shape[1] < width:
        blank = jnp.zeros((values.shape[0], width - values.shape[1]), f32)
        values = jnp.concatenate([values, blank], 1)
    turned = {n: pltpu.roll(values, n, 1) if n else values for n in sorted(set(starts))}
    shards = []
    for d in range(shards_dp):
        rows = [None] * rows_of(length * keep)
        for k, start in enumerate(starts):
            for t in range(rows_of(start + length)):
                at = length * k // lanes + t
                piece = turned[start][d * keep + k : d * keep + k + 1, t * lanes : (t + 1) * lanes]
                rows[at] = piece if rows[at] is None else rows[at] + piece
        shards.append(rows)
    return shards


def prepare_kernel(kinds, odd_ref, *refs):
    count = 2 + kinds
    inputs, outputs, refs = refs[:5], refs[5 : 5 + count], refs[5 + count :]
    copies, arrived = refs[:5], refs[5]
    moves = [
        pltpu.make_async_copy(source, target, arrived.at[n])
        for n, (source, target) in enumerate(zip(inputs, copies))
    ]
    for move in moves:
        move.start()
    for move in moves:
        move.wait()
    prepare(odd_ref, *copies, *outputs[:2], outputs[2:])


def prepare(
    odd_ref,
    upstream_ref,
    pooled_second_ref,
    where_second_ref,
    pooled_first_ref,
    where_first_ref,
    even_ref,
    odd_plane_ref,
    rim_refs,
):
    c1, ys, zs, xs = pooled_first_ref.shape[1:]
    zq = zs // 2
    odd_z, odd_y = odd_ref[0] > 0, odd_ref[1] > 0
    slope = jnp.where(pooled_second_ref[0, :, 0].astype(f32) > 0, 1.0, leak_rate)
    value = upstream_ref[0, :, 0].astype(f32) * slope
    place = (where_second_ref[0, :, 0] + 1).astype(f32)
    quarter = [jnp.transpose(part, (1, 0, 2)) for part in (value, place)]
    for n, part in enumerate(quarter):
        row = jnp.concatenate([part[z] for z in range(zq)], 1).astype(bf16)
        even_ref[zq + n] = row
        odd_plane_ref[zq + n] = row
    fill = jnp.zeros((2 * c1, lanes - xs - xs // 2), f32)
    packed = []
    for y in range(ys):
        pooled = jnp.transpose(pooled_first_ref[0, :, y].astype(f32), (1, 0, 2))
        places = jnp.transpose((where_first_ref[0, :, y] + 1).astype(f32), (1, 0, 2))
        rows = [jnp.concatenate([pooled[z], places[z]], 0) for z in range(zs)]
        packed.append(
            [jnp.concatenate([rows[2 * n], rows[2 * n + 1]], 1).astype(bf16) for n in range(zq)]
        )
        low = jnp.concatenate([rows[0], quarter[y][0], fill], 1)
        high = jnp.concatenate([rows[-1], quarter[y][-1], fill], 1)
        for n, ref in enumerate(rim_refs):
            ref[y] = jnp.where(odd_z == (n == 0), low, high).astype(bf16)
    for n in range(zq):
        even_ref[n] = jnp.where(odd_y, packed[0][n], packed[-1][n])
        odd_plane_ref[n] = jnp.where(odd_y, packed[-1][n], packed[0][n])


def sides_of(refs, odd):
    even = refs[0][...]
    other = refs[1][...] if len(refs) > 1 else jnp.zeros_like(even)
    return jnp.where(odd, even, other), jnp.where(odd, other, even)


def unpooled(values, places, parity):
    return [
        [
            jnp.where(places == parity + (4 * dy + 2 * dz), values, 0.0).astype(bf16)
            for dz in range(2)
        ]
        for dy in range(2)
    ]


def lane_parity():
    lane = lax.broadcasted_iota(jnp.int32, (1, lanes), 1)
    return (lane & 1).astype(f32) + 1.0


def spread_quarter(values, places, xs, c2, zq):
    wide = jnp.concatenate([spread_matrix(z * xs // 2, xs // 2) for z in range(zq)], 1)
    found = dot(jnp.concatenate([values, places], 0), wide)
    return [
        (found[:c2, z * lanes : (z + 1) * lanes], found[c2:, z * lanes : (z + 1) * lanes])
        for z in range(zq)
    ]


def spread_places(plane, ends, xs, c1, zq):
    wide = jnp.concatenate([spread_matrix(0, xs), spread_matrix(xs, xs)], 1)
    rows = [plane[n][c1:] for n in range(zq)] + [end[c1:] for end in ends]
    found = dot(jnp.concatenate(rows, 0), wide)
    inner = [
        found[n * c1 : (n + 1) * c1, m * lanes : (m + 1) * lanes]
        for n in range(zq)
        for m in range(2)
    ]
    low, high = found[zq * c1 : (zq + 1) * c1, :lanes], found[(zq + 1) * c1 :, :lanes]
    return [low] + inner + [high]


def side_kernel(
    sizes,
    odd_ref,
    own_refs,
    rim_refs,
    volume_ref,
    first_ref,
    second_ref,
    up_ref,
    places_ref,
    cells_ref,
    first_out_ref,
    second_out_ref,
    first_order_ref,
    second_order_ref,
):
    ys, zs, xs, c1, c2 = sizes
    zlow, zhigh = sides_of(rim_refs, odd_ref[0] > 0)
    own = sides_of(own_refs, odd_ref[1] > 0)
    parity = lane_parity()
    zq = zs // 2
    rows = spread_quarter(own[0][zq], own[0][zq + 1], xs, c2, zq)
    rims = jnp.concatenate([zlow[0], zlow[1], zhigh[0], zhigh[1]], 0)
    rims = dot(rims, spread_matrix(xs, xs // 2))
    rims = [rims[n * c2 : (n + 1) * c2] for n in range(4)]
    rows = [(rims[0], rims[1])] + rows + [(rims[2], rims[3])]
    for n, (value, place) in enumerate(rows):
        cells = unpooled(value, place, parity)
        for dy in range(2):
            for dz in range(2):
                up_ref[dy, 2 * n + dz] = cells[dy][dz]
    for y in range(ys):
        for n, row in enumerate(spread_places(own[y], (zlow[y], zhigh[y]), xs, c1, zq)):
            places_ref[y, n] = row.astype(bf16)

    lane = lax.broadcasted_iota(jnp.int32, (1, 1, lanes), 2)
    c0, _, zf = volume_ref.shape[1:4]
    for y in range(2 * ys):
        cell = volume_ref[0, :, y].astype(f32)
        moved = [
            jnp.where(lane > 0, pltpu.roll(cell, 1, 2), 0.0),
            cell,
            jnp.where(lane < lanes - 1, pltpu.roll(cell, lanes - 1, 2), 0.0),
            jnp.zeros_like(cell),
        ]
        turned = jnp.transpose(jnp.concatenate(moved, 0), (1, 0, 2))
        for z in range(zf):
            cells_ref[y, :, z * lanes : (z + 1) * lanes] = turned[z].astype(bf16)

    wide = []
    for tz in range(3):
        parts = []
        for n in range(9):
            tap = 9 * (n // 3) + 3 * tz + n % 3
            parts += [first_ref[tap].astype(f32), jnp.zeros((8 - c0, c1), f32)]
        wide.append(jnp.concatenate(parts, 0))
    first_out_ref[...] = jnp.concatenate(wide, 1).astype(bf16)
    wide = [
        jnp.concatenate(
            [second_ref[9 * (n // 3) + 3 * tz + n % 3].astype(f32) for n in range(9)], 0
        )
        for tz in range(3)
    ]
    second_out_ref[...] = jnp.concatenate(wide, 1).astype(bf16)
    for tz in range(3):
        first_order_ref[tz] = order_matrix(c0, 4 * c0, first_order_ref.shape[1:], tz)
        second_order_ref[tz] = order_matrix(c1, 3 * c1, second_order_ref.shape[1:], tz)


def main_kernel(
    sizes,
    odd_ref,
    own_refs,
    rim_refs,
    plane_refs,
    row_refs,
    own_up_ref,
    own_places_ref,
    volume_ref,
    first_ref,
    second_ref,
    first_order_ref,
    second_order_ref,
    grad_ref,
    sums_ref,
    up_ref,
    down_ref,
    cells_ref,
    leaving_ref,
    sent,
):
    ys, zs, xs, c1, c2 = sizes
    zq = zs // 2
    odd_z, odd_y = odd_ref[0] > 0, odd_ref[1] > 0
    zlow, zhigh = sides_of(rim_refs, odd_z)
    own = sides_of(own_refs, odd_y)
    planes = sides_of(plane_refs, odd_y)
    even_rims, other_rims = [
        sides_of([ref[n] for n in range(len(rim_refs))], odd_z) for ref in row_refs
    ]
    plane_rims = [
        [jnp.where(odd_y, even_rims[n], other_rims[n]) for n in range(2)],
        [jnp.where(odd_y, other_rims[n], even_rims[n]) for n in range(2)],
    ]
    parity = lane_parity()
    lane = lax.broadcasted_iota(jnp.int32, (1, lanes), 1)

    near, far = spread_matrix(xs, xs // 2), spread_matrix(xs + xs // 2, xs // 2)
    for side in range(2):
        plane, (low, high) = planes[side], plane_rims[side]
        ends = jnp.concatenate([low, high], 0)
        values, places = dot(ends, near), dot(ends, far)
        rows = spread_quarter(plane[zq], plane[zq + 1], xs, c2, zq)
        rows = [(values[:c2], places[:c2])] + rows + [(values[c2:], places[c2:])]
        for n, (value, place) in enumerate(rows):
            cells = unpooled(value, place, parity)
            for dy in range(2):
                for dz in range(2):
                    up_ref[side, dy, 2 * n + dz] = cells[dy][dz]

    def up_row(y, z):
        if y < 0:
            return up_ref[0, y + 2, z + 2]
        return own_up_ref[y, z + 2] if y < ys else up_ref[1, y - ys, z + 2]

    def pooled_row(y, z):
        side = None if 0 <= y < ys else int(y >= ys)
        if 0 <= z < zs:
            plane = own[y] if side is None else planes[side]
            row = plane[z // 2][:c1].astype(f32)
            return pltpu.roll(row, lanes - xs, 1) if z % 2 else row
        at = int(z >= 0)
        rim = (zlow, zhigh)[at][y] if side is None else plane_rims[side][at]
        return rim[:c1].astype(f32)

    plane_places = [
        spread_places(planes[side], plane_rims[side], xs, c1, zq) for side in range(2)
    ]

    zr = range(-1, zs + 1)
    weights = second_ref[...]
    inputs = {}
    for y in range(ys):
        row = []
        for z in range(zs):
            pooled = pooled_row(y, z)
            act = jnp.where(pooled > 0, pooled, leak_rate * pooled)
            act = jnp.where(lane < xs, act, 0.0).astype(bf16).astype(f32)
            row.append(
                jnp.concatenate(
                    [pltpu.roll(act, 1, 1), act, pltpu.roll(act, lanes - 1, 1)], 0
                ).astype(bf16)
            )
        inputs[y] = jnp.concatenate(row, 1)
    second_sum, products = None, {}
    nothing = jnp.zeros((3 * c1, zs * lanes), bf16)
    for y in range(-2, ys + 2):
        around = jnp.concatenate(
            [
                jnp.concatenate([up_row(y, z + 1 - tz) for z in zr], 1)
                for tz in range(3)
            ],
            0,
        )
        products[y] = dot(weights, around)
        if -1 <= y <= ys:
            meet = jnp.concatenate([inputs.get(y - 1 + ty, nothing) for ty in range(3)], 0)
            term = dot_nt(meet, around[:, lanes:-lanes])
            second_sum = term if second_sum is None else second_sum + term

    spread = spread_matrix(0, xs)
    for y in range(-1, ys + 1):
        terms = sum(
            products[y + 1 - ty][3 * c1 * ty : 3 * c1 * (ty + 1)] for ty in range(3)
        )
        grads = []
        for n, z in enumerate(zr):
            pooled = pooled_row(y, z)
            at = slice(n * lanes, (n + 1) * lanes)
            total = (
                pltpu.roll(terms[:c1, at], lanes - 1, 1)
                + terms[c1 : 2 * c1, at]
                + pltpu.roll(terms[2 * c1 :, at], 1, 1)
            )
            grads.append((total * jnp.where(pooled > 0, 1.0, leak_rate)).astype(bf16))
        values = dot(jnp.concatenate(grads, 0), spread)
        for n, z in enumerate(zr):
            if 0 <= y < ys:
                place = own_places_ref[y, n].astype(f32)
            else:
                place = plane_places[int(y >= ys)][n]
            cells = unpooled(values[n * c1 : (n + 1) * c1], place, parity)
            for dy in range(2):
                for dz in range(2):
                    down_ref[2 * y + 2 + dy, 2 * z + 2 + dz] = cells[dy][dz]

    weights = first_ref[...]
    c0 = grad_ref.shape[0]
    zr = range(2 * zs)
    nothing = jnp.zeros(volume_ref.shape[1:], bf16)
    first_sum, products, leaving = None, {}, []
    for plane in range(-1, 2 * ys + 1):
        around = jnp.concatenate(
            [
                jnp.concatenate([down_ref[plane + 2, z + 3 - tz] for z in zr], 1)
                for tz in range(3)
            ],
            0,
        )
        products[plane] = dot(weights, around)
        meet = jnp.concatenate(
            [
                volume_ref[plane - 1 + ty] if 0 <= plane - 1 + ty < 2 * ys else nothing
                for ty in range(3)
            ],
            0,
        )
        term = dot_nt(meet, around)
        first_sum = term if first_sum is None else first_sum + term
        y = plane - 1
        if y < 0:
            continue
        terms = sum(products[y + 1 - ty][24 * ty : 24 * (ty + 1)] for ty in range(3))
        for z in zr:
            at = slice(z * lanes, (z + 1) * lanes)
            left = jnp.where(lane < lanes - 1, pltpu.roll(terms[:8, at], lanes - 1, 1), 0.0)
            right = jnp.where(lane > 0, pltpu.roll(terms[16:, at], 1, 1), 0.0)
            total = left + terms[8:16, at] + right
            for i in range(c0):
                cells_ref[i, y, z : z + 1, :] = total[i : i + 1]
        leaving_ref[:, y] = cells_ref[:, y].astype(bf16)
        leaving.append(pltpu.make_async_copy(leaving_ref.at[:, y], grad_ref.at[:, y], sent.at[y]))
        leaving[y].start()

    first_sum, second_sum = first_sum.T, second_sum.T
    first, second = 0.0, 0.0
    for tz in range(3):
        first += dot(first_sum[tz * c1 : (tz + 1) * c1].astype(bf16), first_order_ref[tz])
        second += dot(second_sum[tz * c2 : (tz + 1) * c2].astype(bf16), second_order_ref[tz])

    shards_dp, count = sums_ref.shape[:2]
    seconds = flat_rows(second, 27 * c1, c2 // shards_dp, shards_dp)
    firsts = flat_rows(first, 27 * c0, c1 // shards_dp, shards_dp)
    for d in range(shards_dp):
        rows = seconds[d] + firsts[d]
        if len(rows) < count:
            rows = rows + [jnp.zeros((count - len(rows), lanes), f32)]
        sums_ref[d] = jnp.concatenate(rows, 0).astype(bf16)
    for move in leaving:
        move.wait()


def shards(
    volume,
    pooled_first,
    where_first,
    pooled_second,
    where_second,
    upstream,
    kernel_first,
    kernel_second,
):
    dp, gy, gz = (lax.axis_size(a) for a in ("dp", "gy", "gz"))
    c0, c1, c2 = volume.shape[1], pooled_first.shape[1], pooled_second.shape[1]
    ys, zs, xs = pooled_first.shape[2:]

    odd_z, odd_y = lax.axis_index("gz") % 2 == 1, lax.axis_index("gy") % 2 == 1
    odd = jnp.stack([odd_z, odd_y]).astype(jnp.int32)
    smem = pl.BlockSpec(memory_space=pltpu.SMEM)
    vmem = pl.BlockSpec(memory_space=pltpu.VMEM)
    params = pltpu.CompilerParams(vmem_limit_bytes=48 * 1024 * 1024)

    def like(*shape):
        return jax.ShapeDtypeStruct(shape, bf16)

    def pairs_of(axis, begin):
        count = lax.axis_size(axis)
        pairs = [(i, i + 1) for i in range(begin, count - 1, 2)]
        return pairs + [(b, a) for a, b in pairs]

    kinds = 2 if gz > 2 else 1
    raw = (upstream, pooled_second, where_second, pooled_first, where_first)
    plane = like(zs // 2 + 2, 2 * c1, lanes)
    prepared = (plane, plane) + (like(2, 2 * c1, lanes),) * kinds
    even, other, *rims = pl.pallas_call(
        functools.partial(prepare_kernel, kinds),
        out_shape=tuple(pltpu.VMEM(a.shape, a.dtype) for a in prepared),
        in_specs=[smem] + [pl.BlockSpec(memory_space=pltpu.HBM)] * 5,
        out_specs=(vmem,) * (2 + kinds),
        scratch_shapes=[pltpu.VMEM(a.shape, a.dtype) for a in raw]
        + [pltpu.SemaphoreType.DMA((5,))],
        compiler_params=pltpu.CompilerParams(vmem_limit_bytes=49152 * 1024),
    )(odd, *[pltpu.with_memory_space_constraint(a, pltpu.HBM) for a in raw])

    def moved(block, axes, pairs):
        return lax.ppermute(block, axes, pairs) if pairs else jnp.zeros_like(block)

    got_rims = [moved(rim, "gz", pairs_of("gz", n)) for n, rim in enumerate(rims)]
    got_planes = [moved(plane, "gy", pairs_of("gy", n)) for n, plane in enumerate((even, other))]

    def facing(row, rim):
        return jnp.concatenate([row] + [rim[n, :, xs : xs + xs // 2] for n in range(2)], 1)

    low, high = ([facing(rim[y, :, :xs], rim) for rim in got_rims] for y in (0, ys - 1))
    low, high = jnp.stack(low), jnp.stack(high)
    got_rows = [
        moved(jnp.where(odd_y == (n == 0), low, high), "gy", pairs_of("gy", n)) for n in range(2)
    ]

    first = jnp.transpose(kernel_first, (2, 3, 4, 1, 0)).reshape(27, c0, c1)
    second = jnp.transpose(kernel_second, (2, 3, 4, 1, 0)).reshape(27, c1, c2)
    sizes = (ys, zs, xs, c1, c2)
    wide = rows_of(27 * c1) * lanes
    up, places, cells, first, second, *orders = pl.pallas_call(
        functools.partial(side_kernel, sizes),
        out_shape=(
            like(ys, zs + 4, c2, lanes),
            like(ys, zs + 2, c1, lanes),
            like(2 * ys, 4 * c0, 2 * zs * lanes),
            like(72, 3 * c1),
            like(9 * c1, 3 * c2),
            like(3, 12 * c0, lanes),
            like(3, 9 * c1, wide),
        ),
        in_specs=[smem, [vmem] * 2, [vmem] * kinds, vmem, vmem, vmem],
        out_specs=(vmem,) * 7,
        compiler_params=params,
        cost_estimate=pl.CostEstimate(flops=10**7, bytes_accessed=10**6, transcendentals=0),
    )(odd, [even, other], got_rims, volume, first, second)

    sizes1, sizes2 = 27 * c0 * c1 // dp, 27 * c1 * c2 // dp
    sum_rows = -(-(rows_of(sizes1) + rows_of(sizes2)) // 32) * 32
    grad_vol, sums = pl.pallas_call(
        functools.partial(main_kernel, sizes),
        out_shape=(like(*volume.shape[1:]), like(dp, sum_rows, lanes)),
        in_specs=[smem, [vmem] * 2, [vmem] * kinds, [vmem] * 2, [vmem] * 2] + [vmem] * 7,
        out_specs=(pl.BlockSpec(memory_space=pl.ANY), vmem),
        scratch_shapes=[
            pltpu.VMEM((2, 2, zs + 4, c2, lanes), bf16),
            pltpu.VMEM((2 * ys + 4, 2 * zs + 4, c1, lanes), bf16),
            pltpu.VMEM(volume.shape[1:], f32),
            pltpu.VMEM(volume.shape[1:], bf16),
            pltpu.SemaphoreType.DMA((2 * ys,)),
        ],
        compiler_params=params,
        cost_estimate=pl.CostEstimate(
            flops=200_000_000, bytes_accessed=2_000_000, transcendentals=0
        ),
    )(
        odd,
        [even, other],
        got_rims,
        got_planes,
        got_rows,
        up,
        places,
        cells,
        first,
        second,
        *orders,
    )

    half = sum_rows // 2
    low, high = sums[:, :half], sums[:, half:]
    other = lax.ppermute(jnp.where(odd_y, low, high), "gy", pairs_of("gy", 0))
    part = jnp.where(odd_y, high, low).astype(f32) + other.astype(f32)
    sent = jnp.broadcast_to(part.astype(bf16)[:, None], (dp, gy * gz) + part.shape[1:])
    sent = sent.reshape((dp * gy * gz,) + part.shape[1:])
    got = lax.all_to_all(sent, ("dp", "gy", "gz"), 0, 0, tiled=True)
    got = got.reshape((dp * gy // 2, 2, gz) + part.shape[1:])
    count = volume.shape[0] * volume.shape[2] * volume.shape[3] * volume.shape[4] * dp * gy * gz
    total = jnp.sum(got.astype(f32), axis=(0, 2)).reshape(sum_rows, lanes)
    split = rows_of(sizes2)
    second_out = total[:split].reshape(-1)[:sizes2] * math.sqrt(64.0 / count)
    first_out = total[split : split + rows_of(sizes1)].reshape(-1)[:sizes1]
    return grad_vol[None], first_out * math.sqrt(8.0 / count), second_out


def solution(mesh):
    cells = P("dp", None, "gy", "gz", None)
    return jax.shard_map(
        shards,
        mesh=mesh,
        in_specs=(cells,) * 6 + (P(), P()),
        out_specs=(cells, P("dp"), P("dp")),
        check_vma=False,
    )
```

```python
import functools
import math

import jax
import jax.numpy as jnp
from jax import lax
from jax.experimental import pallas as pl
from jax.experimental.pallas import tpu as pltpu
from jax.sharding import PartitionSpec as P

leak_rate = 0.3
lanes = 128
f32, bf16 = jnp.float32, jnp.bfloat16


def dot(a, b):
    return lax.dot_general(a, b, (((1,), (0,)), ((), ())), preferred_element_type=f32)


def dot_nt(a, b):
    return lax.dot_general(a, b, (((1,), (1,)), ((), ())), preferred_element_type=f32)


def spread_matrix(first_row, count):
    row = lax.broadcasted_iota(jnp.int32, (lanes, lanes), 0)
    lane = lax.broadcasted_iota(jnp.int32, (lanes, lanes), 1)
    hit = (lane >> 1) + first_row == row
    return jnp.where(hit & (lane < 2 * count), 1.0, 0.0).astype(bf16)


def order_matrix(ins, step, shape, tz):
    row = lax.broadcasted_iota(jnp.int32, shape, 0)
    column = lax.broadcasted_iota(jnp.int32, shape, 1)
    at = row % step
    hit = column == (at % ins) * 27 + 9 * (row // step) + 3 * tz + at // ins
    return jnp.where(hit & (at < 3 * ins), 1.0, 0.0).astype(bf16)


def rows_of(count):
    return -(-count // lanes)


def flat_rows(values, length, keep, shards_dp):
    starts = [length * k % lanes for k in range(keep)]
    width = rows_of(max(starts) + length) * lanes
    if values.shape[1] < width:
        blank = jnp.zeros((values.shape[0], width - values.shape[1]), f32)
        values = jnp.concatenate([values, blank], 1)
    turned = {n: pltpu.roll(values, n, 1) if n else values for n in sorted(set(starts))}
    shards = []
    for d in range(shards_dp):
        rows = [None] * rows_of(length * keep)
        for k, start in enumerate(starts):
            for t in range(rows_of(start + length)):
                at = length * k // lanes + t
                piece = turned[start][d * keep + k : d * keep + k + 1, t * lanes : (t + 1) * lanes]
                rows[at] = piece if rows[at] is None else rows[at] + piece
        shards.append(rows)
    return shards


def prepare_kernel(kinds, odd_ref, *refs):
    count = 2 + kinds
    inputs, outputs, refs = refs[:5], refs[5 : 5 + count], refs[5 + count :]
    copies, arrived = refs[:5], refs[5]
    moves = [
        pltpu.make_async_copy(source, target, arrived.at[n])
        for n, (source, target) in enumerate(zip(inputs, copies))
    ]
    for move in moves:
        move.start()
    for move in moves:
        move.wait()
    prepare(odd_ref, *copies, *outputs[:2], outputs[2:])


def prepare(
    odd_ref,
    upstream_ref,
    pooled_second_ref,
    where_second_ref,
    pooled_first_ref,
    where_first_ref,
    even_ref,
    odd_plane_ref,
    rim_refs,
):
    c1, ys, zs, xs = pooled_first_ref.shape[1:]
    zq = zs // 2
    odd_z, odd_y = odd_ref[0] > 0, odd_ref[1] > 0
    slope = jnp.where(pooled_second_ref[0, :, 0].astype(f32) > 0, 1.0, leak_rate)
    value = upstream_ref[0, :, 0].astype(f32) * slope
    place = (where_second_ref[0, :, 0] + 1).astype(f32)
    quarter = [jnp.transpose(part, (1, 0, 2)) for part in (value, place)]
    for n, part in enumerate(quarter):
        row = jnp.concatenate([part[z] for z in range(zq)], 1).astype(bf16)
        even_ref[zq + n] = row
        odd_plane_ref[zq + n] = row
    fill = jnp.zeros((2 * c1, lanes - xs - xs // 2), f32)
    packed = []
    for y in range(ys):
        pooled = jnp.transpose(pooled_first_ref[0, :, y].astype(f32), (1, 0, 2))
        places = jnp.transpose((where_first_ref[0, :, y] + 1).astype(f32), (1, 0, 2))
        rows = [jnp.concatenate([pooled[z], places[z]], 0) for z in range(zs)]
        packed.append(
            [jnp.concatenate([rows[2 * n], rows[2 * n + 1]], 1).astype(bf16) for n in range(zq)]
        )
        low = jnp.concatenate([rows[0], quarter[y][0], fill], 1)
        high = jnp.concatenate([rows[-1], quarter[y][-1], fill], 1)
        for n, ref in enumerate(rim_refs):
            ref[y] = jnp.where(odd_z == (n == 0), low, high).astype(bf16)
    for n in range(zq):
        even_ref[n] = jnp.where(odd_y, packed[0][n], packed[-1][n])
        odd_plane_ref[n] = jnp.where(odd_y, packed[-1][n], packed[0][n])


def sides_of(refs, odd):
    even = refs[0][...]
    other = refs[1][...] if len(refs) > 1 else jnp.zeros_like(even)
    return jnp.where(odd, even, other), jnp.where(odd, other, even)


def unpooled(values, places, parity):
    return [
        [
            jnp.where(places == parity + (4 * dy + 2 * dz), values, 0.0).astype(bf16)
            for dz in range(2)
        ]
        for dy in range(2)
    ]


def lane_parity():
    lane = lax.broadcasted_iota(jnp.int32, (1, lanes), 1)
    return (lane & 1).astype(f32) + 1.0


def spread_quarter(values, places, xs, c2, zq):
    wide = jnp.concatenate([spread_matrix(z * xs // 2, xs // 2) for z in range(zq)], 1)
    found = dot(jnp.concatenate([values, places], 0), wide)
    return [
        (found[:c2, z * lanes : (z + 1) * lanes], found[c2:, z * lanes : (z + 1) * lanes])
        for z in range(zq)
    ]


def spread_places(plane, ends, xs, c1, zq):
    wide = jnp.concatenate([spread_matrix(0, xs), spread_matrix(xs, xs)], 1)
    rows = [plane[n][c1:] for n in range(zq)] + [end[c1:] for end in ends]
    found = dot(jnp.concatenate(rows, 0), wide)
    inner = [
        found[n * c1 : (n + 1) * c1, m * lanes : (m + 1) * lanes]
        for n in range(zq)
        for m in range(2)
    ]
    low, high = found[zq * c1 : (zq + 1) * c1, :lanes], found[(zq + 1) * c1 :, :lanes]
    return [low] + inner + [high]


def z_stack(row_of, zs):
    zr = range(-1, zs + 1)
    return jnp.concatenate(
        [jnp.concatenate([row_of(z + 1 - tz) for z in zr], 1) for tz in range(3)], 0
    )


def y_terms(products, y, rows):
    return sum(
        products[y + 1 - ty][rows * ty : rows * (ty + 1)]
        for ty in range(3)
        if y + 1 - ty in products
    )


def half_row(plane, z, c1, xs):
    row = plane[z // 2][:c1].astype(f32)
    return pltpu.roll(row, lanes - xs, 1) if z % 2 else row


def shifted_inputs(plane, zs, c1, xs):
    lane = lax.broadcasted_iota(jnp.int32, (1, lanes), 1)
    row = []
    for z in range(zs):
        pooled = half_row(plane, z, c1, xs)
        act = jnp.where(pooled > 0, pooled, leak_rate * pooled)
        act = jnp.where(lane < xs, act, 0.0).astype(bf16).astype(f32)
        row.append(
            jnp.concatenate(
                [pltpu.roll(act, 1, 1), act, pltpu.roll(act, lanes - 1, 1)], 0
            ).astype(bf16)
        )
    return jnp.concatenate(row, 1)


def side_kernel(
    sizes,
    odd_ref,
    own_refs,
    rim_refs,
    volume_ref,
    first_ref,
    second_ref,
    inputs_ref,
    terms_ref,
    second_sum_ref,
    places_ref,
    cells_ref,
    first_out_ref,
    second_out_ref,
    first_order_ref,
    second_order_ref,
    up_ref,
):
    ys, zs, xs, c1, c2 = sizes
    zlow, zhigh = sides_of(rim_refs, odd_ref[0] > 0)
    own = sides_of(own_refs, odd_ref[1] > 0)
    parity = lane_parity()
    zq = zs // 2
    rows = spread_quarter(own[0][zq], own[0][zq + 1], xs, c2, zq)
    rims = jnp.concatenate([zlow[0], zlow[1], zhigh[0], zhigh[1]], 0)
    rims = dot(rims, spread_matrix(xs, xs // 2))
    rims = [rims[n * c2 : (n + 1) * c2] for n in range(4)]
    rows = [(rims[0], rims[1])] + rows + [(rims[2], rims[3])]
    for n, (value, place) in enumerate(rows):
        cells = unpooled(value, place, parity)
        for dy in range(2):
            for dz in range(2):
                up_ref[dy, 2 * n + dz] = cells[dy][dz]
    for y in range(ys):
        for n, row in enumerate(spread_places(own[y], (zlow[y], zhigh[y]), xs, c1, zq)):
            places_ref[y, n] = row.astype(bf16)

    lane = lax.broadcasted_iota(jnp.int32, (1, 1, lanes), 2)
    c0, _, zf = volume_ref.shape[1:4]
    for y in range(2 * ys):
        cell = volume_ref[0, :, y].astype(f32)
        moved = [
            jnp.where(lane > 0, pltpu.roll(cell, 1, 2), 0.0),
            cell,
            jnp.where(lane < lanes - 1, pltpu.roll(cell, lanes - 1, 2), 0.0),
            jnp.zeros_like(cell),
        ]
        turned = jnp.transpose(jnp.concatenate(moved, 0), (1, 0, 2))
        for z in range(zf):
            cells_ref[y, :, z * lanes : (z + 1) * lanes] = turned[z].astype(bf16)

    wide = []
    for tz in range(3):
        parts = []
        for n in range(9):
            tap = 9 * (n // 3) + 3 * tz + n % 3
            parts += [first_ref[tap].astype(f32), jnp.zeros((8 - c0, c1), f32)]
        wide.append(jnp.concatenate(parts, 0))
    first_out_ref[...] = jnp.concatenate(wide, 1).astype(bf16)
    wide = [
        jnp.concatenate(
            [second_ref[9 * (n // 3) + 3 * tz + n % 3].astype(f32) for n in range(9)], 0
        )
        for tz in range(3)
    ]
    second_out_ref[...] = jnp.concatenate(wide, 1).astype(bf16)
    for tz in range(3):
        first_order_ref[tz] = order_matrix(c0, 4 * c0, first_order_ref.shape[1:], tz)
        second_order_ref[tz] = order_matrix(c1, 3 * c1, second_order_ref.shape[1:], tz)

    weights = second_out_ref[...]
    inputs = {y: shifted_inputs(own[y], zs, c1, xs) for y in range(ys)}
    for y in range(ys):
        inputs_ref[y] = inputs[y]
    nothing = jnp.zeros((3 * c1, zs * lanes), bf16)
    second_sum, products = 0.0, {}
    for y in range(ys):
        around = z_stack(lambda z: up_ref[y, z + 2], zs)
        products[y] = dot(weights, around)
        meet = jnp.concatenate([inputs.get(y - 1 + ty, nothing) for ty in range(3)], 0)
        second_sum += dot_nt(meet, around[:, lanes:-lanes])
    second_sum_ref[...] = second_sum
    for y in range(-1, ys + 1):
        terms_ref[y + 1] = y_terms(products, y, 3 * c1)


def main_kernel(
    sizes,
    odd_ref,
    own_refs,
    rim_refs,
    plane_refs,
    row_refs,
    inputs_ref,
    terms_ref,
    second_sum_ref,
    own_places_ref,
    volume_ref,
    first_ref,
    second_ref,
    first_order_ref,
    second_order_ref,
    grad_ref,
    sums_ref,
    up_ref,
    down_ref,
    cells_ref,
    leaving_ref,
    sent,
):
    ys, zs, xs, c1, c2 = sizes
    zq = zs // 2
    odd_z, odd_y = odd_ref[0] > 0, odd_ref[1] > 0
    zlow, zhigh = sides_of(rim_refs, odd_z)
    own = sides_of(own_refs, odd_y)
    planes = sides_of(plane_refs, odd_y)
    even_rims, other_rims = [
        sides_of([ref[n] for n in range(len(rim_refs))], odd_z) for ref in row_refs
    ]
    plane_rims = [
        [jnp.where(odd_y, even_rims[n], other_rims[n]) for n in range(2)],
        [jnp.where(odd_y, other_rims[n], even_rims[n]) for n in range(2)],
    ]
    parity = lane_parity()
    lane = lax.broadcasted_iota(jnp.int32, (1, lanes), 1)

    near, far = spread_matrix(xs, xs // 2), spread_matrix(xs + xs // 2, xs // 2)
    for side in range(2):
        plane, (low, high) = planes[side], plane_rims[side]
        ends = jnp.concatenate([low, high], 0)
        values, places = dot(ends, near), dot(ends, far)
        rows = spread_quarter(plane[zq], plane[zq + 1], xs, c2, zq)
        rows = [(values[:c2], places[:c2])] + rows + [(values[c2:], places[c2:])]
        for n, (value, place) in enumerate(rows):
            cells = unpooled(value, place, parity)
            for dy in range(2):
                for dz in range(2):
                    up_ref[side, dy, 2 * n + dz] = cells[dy][dz]

    def pooled_row(y, z):
        side = None if 0 <= y < ys else int(y >= ys)
        if 0 <= z < zs:
            return half_row(own[y] if side is None else planes[side], z, c1, xs)
        at = int(z >= 0)
        rim = (zlow, zhigh)[at][y] if side is None else plane_rims[side][at]
        return rim[:c1].astype(f32)

    plane_places = [
        spread_places(planes[side], plane_rims[side], xs, c1, zq) for side in range(2)
    ]

    zr = range(-1, zs + 1)
    weights = second_ref[...]
    second_sum, products = second_sum_ref[...], {}
    nothing = jnp.zeros((3 * c1, zs * lanes), bf16)
    for y in (-2, -1, ys, ys + 1):
        side, dy = (0, y + 2) if y < 0 else (1, y - ys)
        around = z_stack(lambda z: up_ref[side, dy, z + 2], zs)
        products[y] = dot(weights, around)
        if -1 <= y <= ys:
            meet = [
                inputs_ref[y - 1 + ty] if 0 <= y - 1 + ty < ys else nothing for ty in range(3)
            ]
            second_sum += dot_nt(jnp.concatenate(meet, 0), around[:, lanes:-lanes])

    spread = spread_matrix(0, xs)
    for y in range(-1, ys + 1):
        terms = terms_ref[y + 1] + y_terms(products, y, 3 * c1)
        grads = []
        for n, z in enumerate(zr):
            pooled = pooled_row(y, z)
            at = slice(n * lanes, (n + 1) * lanes)
            total = (
                pltpu.roll(terms[:c1, at], lanes - 1, 1)
                + terms[c1 : 2 * c1, at]
                + pltpu.roll(terms[2 * c1 :, at], 1, 1)
            )
            grads.append((total * jnp.where(pooled > 0, 1.0, leak_rate)).astype(bf16))
        values = dot(jnp.concatenate(grads, 0), spread)
        for n, z in enumerate(zr):
            if 0 <= y < ys:
                place = own_places_ref[y, n].astype(f32)
            else:
                place = plane_places[int(y >= ys)][n]
            cells = unpooled(values[n * c1 : (n + 1) * c1], place, parity)
            for dy in range(2):
                for dz in range(2):
                    down_ref[2 * y + 2 + dy, 2 * z + 2 + dz] = cells[dy][dz]

    weights = first_ref[...]
    c0 = grad_ref.shape[0]
    zr = range(2 * zs)
    nothing = jnp.zeros(volume_ref.shape[1:], bf16)
    first_sum, products, leaving = None, {}, []
    for plane in range(-1, 2 * ys + 1):
        around = jnp.concatenate(
            [
                jnp.concatenate([down_ref[plane + 2, z + 3 - tz] for z in zr], 1)
                for tz in range(3)
            ],
            0,
        )
        products[plane] = dot(weights, around)
        meet = jnp.concatenate(
            [
                volume_ref[plane - 1 + ty] if 0 <= plane - 1 + ty < 2 * ys else nothing
                for ty in range(3)
            ],
            0,
        )
        term = dot_nt(meet, around)
        first_sum = term if first_sum is None else first_sum + term
        y = plane - 1
        if y < 0:
            continue
        terms = y_terms(products, y, 24)
        for z in zr:
            at = slice(z * lanes, (z + 1) * lanes)
            left = jnp.where(lane < lanes - 1, pltpu.roll(terms[:8, at], lanes - 1, 1), 0.0)
            right = jnp.where(lane > 0, pltpu.roll(terms[16:, at], 1, 1), 0.0)
            total = left + terms[8:16, at] + right
            for i in range(c0):
                cells_ref[i, y, z : z + 1, :] = total[i : i + 1]
        leaving_ref[:, y] = cells_ref[:, y].astype(bf16)
        leaving.append(pltpu.make_async_copy(leaving_ref.at[:, y], grad_ref.at[:, y], sent.at[y]))
        leaving[y].start()

    first_sum, second_sum = first_sum.T, second_sum.T
    first, second = 0.0, 0.0
    for tz in range(3):
        first += dot(first_sum[tz * c1 : (tz + 1) * c1].astype(bf16), first_order_ref[tz])
        second += dot(second_sum[tz * c2 : (tz + 1) * c2].astype(bf16), second_order_ref[tz])

    shards_dp, count = sums_ref.shape[:2]
    seconds = flat_rows(second, 27 * c1, c2 // shards_dp, shards_dp)
    firsts = flat_rows(first, 27 * c0, c1 // shards_dp, shards_dp)
    for d in range(shards_dp):
        rows = seconds[d] + firsts[d]
        if len(rows) < count:
            rows = rows + [jnp.zeros((count - len(rows), lanes), f32)]
        sums_ref[d] = jnp.concatenate(rows, 0).astype(bf16)
    for move in leaving:
        move.wait()


def shards(
    volume,
    pooled_first,
    where_first,
    pooled_second,
    where_second,
    upstream,
    kernel_first,
    kernel_second,
):
    dp, gy, gz = (lax.axis_size(a) for a in ("dp", "gy", "gz"))
    c0, c1, c2 = volume.shape[1], pooled_first.shape[1], pooled_second.shape[1]
    ys, zs, xs = pooled_first.shape[2:]

    odd_z, odd_y = lax.axis_index("gz") % 2 == 1, lax.axis_index("gy") % 2 == 1
    odd = jnp.stack([odd_z, odd_y]).astype(jnp.int32)
    smem = pl.BlockSpec(memory_space=pltpu.SMEM)
    vmem = pl.BlockSpec(memory_space=pltpu.VMEM)
    params = pltpu.CompilerParams(vmem_limit_bytes=48 * 1024 * 1024)

    def like(*shape):
        return jax.ShapeDtypeStruct(shape, bf16)

    def pairs_of(axis, begin):
        count = lax.axis_size(axis)
        pairs = [(i, i + 1) for i in range(begin, count - 1, 2)]
        return pairs + [(b, a) for a, b in pairs]

    kinds = 2 if gz > 2 else 1
    raw = (upstream, pooled_second, where_second, pooled_first, where_first)
    plane = like(zs // 2 + 2, 2 * c1, lanes)
    prepared = (plane, plane) + (like(2, 2 * c1, lanes),) * kinds
    even, other, *rims = pl.pallas_call(
        functools.partial(prepare_kernel, kinds),
        out_shape=tuple(pltpu.VMEM(a.shape, a.dtype) for a in prepared),
        in_specs=[smem] + [pl.BlockSpec(memory_space=pltpu.HBM)] * 5,
        out_specs=(vmem,) * (2 + kinds),
        scratch_shapes=[pltpu.VMEM(a.shape, a.dtype) for a in raw]
        + [pltpu.SemaphoreType.DMA((5,))],
        compiler_params=pltpu.CompilerParams(vmem_limit_bytes=49152 * 1024),
    )(odd, *[pltpu.with_memory_space_constraint(a, pltpu.HBM) for a in raw])

    def moved(block, axes, pairs):
        return lax.ppermute(block, axes, pairs) if pairs else jnp.zeros_like(block)

    got_rims = [moved(rim, "gz", pairs_of("gz", n)) for n, rim in enumerate(rims)]
    got_planes = [moved(plane, "gy", pairs_of("gy", n)) for n, plane in enumerate((even, other))]

    def facing(row, rim):
        return jnp.concatenate([row] + [rim[n, :, xs : xs + xs // 2] for n in range(2)], 1)

    low, high = ([facing(rim[y, :, :xs], rim) for rim in got_rims] for y in (0, ys - 1))
    low, high = jnp.stack(low), jnp.stack(high)
    got_rows = [
        moved(jnp.where(odd_y == (n == 0), low, high), "gy", pairs_of("gy", n)) for n in range(2)
    ]

    first = jnp.transpose(kernel_first, (2, 3, 4, 1, 0)).reshape(27, c0, c1)
    second = jnp.transpose(kernel_second, (2, 3, 4, 1, 0)).reshape(27, c1, c2)
    sizes = (ys, zs, xs, c1, c2)
    wide = rows_of(27 * c1) * lanes
    inputs, terms, partial, places, cells, first, second, *orders = pl.pallas_call(
        functools.partial(side_kernel, sizes),
        out_shape=(
            like(ys, 3 * c1, zs * lanes),
            jax.ShapeDtypeStruct((ys + 2, 3 * c1, (zs + 2) * lanes), f32),
            jax.ShapeDtypeStruct((9 * c1, 3 * c2), f32),
            like(ys, zs + 2, c1, lanes),
            like(2 * ys, 4 * c0, 2 * zs * lanes),
            like(72, 3 * c1),
            like(9 * c1, 3 * c2),
            like(3, 12 * c0, lanes),
            like(3, 9 * c1, wide),
        ),
        in_specs=[smem, [vmem] * 2, [vmem] * kinds, vmem, vmem, vmem],
        out_specs=(vmem,) * 9,
        scratch_shapes=[pltpu.VMEM((ys, zs + 4, c2, lanes), bf16)],
        compiler_params=params,
        cost_estimate=pl.CostEstimate(flops=10**7, bytes_accessed=10**6, transcendentals=0),
    )(odd, [even, other], got_rims, volume, first, second)

    sizes1, sizes2 = 27 * c0 * c1 // dp, 27 * c1 * c2 // dp
    sum_rows = -(-(rows_of(sizes1) + rows_of(sizes2)) // 32) * 32
    grad_vol, sums = pl.pallas_call(
        functools.partial(main_kernel, sizes),
        out_shape=(like(*volume.shape[1:]), like(dp, sum_rows, lanes)),
        in_specs=[smem, [vmem] * 2, [vmem] * kinds, [vmem] * 2, [vmem] * 2] + [vmem] * 9,
        out_specs=(pl.BlockSpec(memory_space=pl.ANY), vmem),
        scratch_shapes=[
            pltpu.VMEM((2, 2, zs + 4, c2, lanes), bf16),
            pltpu.VMEM((2 * ys + 4, 2 * zs + 4, c1, lanes), bf16),
            pltpu.VMEM(volume.shape[1:], f32),
            pltpu.VMEM(volume.shape[1:], bf16),
            pltpu.SemaphoreType.DMA((2 * ys,)),
        ],
        compiler_params=params,
        cost_estimate=pl.CostEstimate(
            flops=200_000_000, bytes_accessed=2_000_000, transcendentals=0
        ),
    )(
        odd,
        [even, other],
        got_rims,
        got_planes,
        got_rows,
        inputs,
        terms,
        partial,
        places,
        cells,
        first,
        second,
        *orders,
    )

    half = sum_rows // 2
    low, high = sums[:, :half], sums[:, half:]
    other = lax.ppermute(jnp.where(odd_y, low, high), "gy", pairs_of("gy", 0))
    part = jnp.where(odd_y, high, low).astype(f32) + other.astype(f32)
    sent = jnp.broadcast_to(part.astype(bf16)[:, None], (dp, gy * gz) + part.shape[1:])
    sent = sent.reshape((dp * gy * gz,) + part.shape[1:])
    got = lax.all_to_all(sent, ("dp", "gy", "gz"), 0, 0, tiled=True)
    got = got.reshape((dp * gy // 2, 2, gz) + part.shape[1:])
    count = volume.shape[0] * volume.shape[2] * volume.shape[3] * volume.shape[4] * dp * gy * gz
    total = jnp.sum(got.astype(f32), axis=(0, 2)).reshape(sum_rows, lanes)
    split = rows_of(sizes2)
    second_out = total[:split].reshape(-1)[:sizes2] * math.sqrt(64.0 / count)
    first_out = total[split : split + rows_of(sizes1)].reshape(-1)[:sizes1]
    return grad_vol[None], first_out * math.sqrt(8.0 / count), second_out


def solution(mesh):
    cells = P("dp", None, "gy", "gz", None)
    return jax.shard_map(
        shards,
        mesh=mesh,
        in_specs=(cells,) * 6 + (P(), P()),
        out_specs=(cells, P("dp"), P("dp")),
        check_vma=False,
    )
```

```python
import functools
import math

import jax
import jax.numpy as jnp
from jax import lax
from jax.experimental import pallas as pl
from jax.experimental.pallas import tpu as pltpu
from jax.sharding import PartitionSpec as P

leak_rate = 0.3
lanes = 128
f32, bf16 = jnp.float32, jnp.bfloat16


def dot(a, b):
    return lax.dot_general(a, b, (((1,), (0,)), ((), ())), preferred_element_type=f32)


def dot_nt(a, b):
    return lax.dot_general(a, b, (((1,), (1,)), ((), ())), preferred_element_type=f32)


def spread_matrix(first_row, count):
    row = lax.broadcasted_iota(jnp.int32, (lanes, lanes), 0)
    lane = lax.broadcasted_iota(jnp.int32, (lanes, lanes), 1)
    hit = (lane >> 1) + first_row == row
    return jnp.where(hit & (lane < 2 * count), 1.0, 0.0).astype(bf16)


def order_matrix(ins, step, shape, tz):
    row = lax.broadcasted_iota(jnp.int32, shape, 0)
    column = lax.broadcasted_iota(jnp.int32, shape, 1)
    at = row % step
    hit = column == (at % ins) * 27 + 9 * (row // step) + 3 * tz + at // ins
    return jnp.where(hit & (at < 3 * ins), 1.0, 0.0).astype(bf16)


def rows_of(count):
    return -(-count // lanes)


def flat_rows(values, length, keep, shards_dp):
    starts = [length * k % lanes for k in range(keep)]
    width = rows_of(max(starts) + length) * lanes
    if values.shape[1] < width:
        blank = jnp.zeros((values.shape[0], width - values.shape[1]), f32)
        values = jnp.concatenate([values, blank], 1)
    turned = {n: pltpu.roll(values, n, 1) if n else values for n in sorted(set(starts))}
    shards = []
    for d in range(shards_dp):
        rows = [None] * rows_of(length * keep)
        for k, start in enumerate(starts):
            for t in range(rows_of(start + length)):
                at = length * k // lanes + t
                piece = turned[start][d * keep + k : d * keep + k + 1, t * lanes : (t + 1) * lanes]
                rows[at] = piece if rows[at] is None else rows[at] + piece
        shards.append(rows)
    return shards


def prepare_kernel(kinds, odd_ref, *refs):
    count = 2 + kinds
    inputs, outputs, refs = refs[:5], refs[5 : 5 + count], refs[5 + count :]
    copies, arrived = refs[:5], refs[5]
    moves = [
        pltpu.make_async_copy(source, target, arrived.at[n])
        for n, (source, target) in enumerate(zip(inputs, copies))
    ]
    for move in moves:
        move.start()
    prepare(moves, odd_ref, *copies, *outputs[:2], outputs[2:])


def prepare(
    moves,
    odd_ref,
    upstream_ref,
    pooled_second_ref,
    where_second_ref,
    pooled_first_ref,
    where_first_ref,
    even_ref,
    odd_plane_ref,
    rim_refs,
):
    c1, ys, zs, xs = pooled_first_ref.shape[1:]
    zq = zs // 2
    odd_z, odd_y = odd_ref[0] > 0, odd_ref[1] > 0
    for move in moves[:3]:
        move.wait()
    slope = jnp.where(pooled_second_ref[0, :, 0].astype(f32) > 0, 1.0, leak_rate)
    value = upstream_ref[0, :, 0].astype(f32) * slope
    place = (where_second_ref[0, :, 0] + 1).astype(f32)
    quarter = [jnp.transpose(part, (1, 0, 2)) for part in (value, place)]
    for n, part in enumerate(quarter):
        row = jnp.concatenate([part[z] for z in range(zq)], 1).astype(bf16)
        even_ref[zq + n] = row
        odd_plane_ref[zq + n] = row
    fill = jnp.zeros((2 * c1, lanes - xs - xs // 2), f32)
    packed = []
    for move in moves[3:]:
        move.wait()
    for y in range(ys):
        pooled = jnp.transpose(pooled_first_ref[0, :, y].astype(f32), (1, 0, 2))
        places = jnp.transpose((where_first_ref[0, :, y] + 1).astype(f32), (1, 0, 2))
        rows = [jnp.concatenate([pooled[z], places[z]], 0) for z in range(zs)]
        packed.append(
            [jnp.concatenate([rows[2 * n], rows[2 * n + 1]], 1).astype(bf16) for n in range(zq)]
        )
        low = jnp.concatenate([rows[0], quarter[y][0], fill], 1)
        high = jnp.concatenate([rows[-1], quarter[y][-1], fill], 1)
        for n, ref in enumerate(rim_refs):
            ref[y] = jnp.where(odd_z == (n == 0), low, high).astype(bf16)
    for n in range(zq):
        even_ref[n] = jnp.where(odd_y, packed[0][n], packed[-1][n])
        odd_plane_ref[n] = jnp.where(odd_y, packed[-1][n], packed[0][n])


def sides_of(refs, odd):
    even = refs[0][...]
    other = refs[1][...] if len(refs) > 1 else jnp.zeros_like(even)
    return jnp.where(odd, even, other), jnp.where(odd, other, even)


def unpooled(values, places, parity):
    return [
        [
            jnp.where(places == parity + (4 * dy + 2 * dz), values, 0.0).astype(bf16)
            for dz in range(2)
        ]
        for dy in range(2)
    ]


def lane_parity():
    lane = lax.broadcasted_iota(jnp.int32, (1, lanes), 1)
    return (lane & 1).astype(f32) + 1.0


def spread_quarter(values, places, xs, c2, zq):
    wide = jnp.concatenate([spread_matrix(z * xs // 2, xs // 2) for z in range(zq)], 1)
    found = dot(jnp.concatenate([values, places], 0), wide)
    return [
        (found[:c2, z * lanes : (z + 1) * lanes], found[c2:, z * lanes : (z + 1) * lanes])
        for z in range(zq)
    ]


def spread_places(plane, ends, xs, c1, zq):
    wide = jnp.concatenate([spread_matrix(0, xs), spread_matrix(xs, xs)], 1)
    rows = [plane[n][c1:] for n in range(zq)] + [end[c1:] for end in ends]
    found = dot(jnp.concatenate(rows, 0), wide)
    inner = [
        found[n * c1 : (n + 1) * c1, m * lanes : (m + 1) * lanes]
        for n in range(zq)
        for m in range(2)
    ]
    low, high = found[zq * c1 : (zq + 1) * c1, :lanes], found[(zq + 1) * c1 :, :lanes]
    return [low] + inner + [high]


def z_stack(row_of, zs):
    zr = range(-1, zs + 1)
    return jnp.concatenate(
        [jnp.concatenate([row_of(z + 1 - tz) for z in zr], 1) for tz in range(3)], 0
    )


def y_terms(products, y, rows):
    return sum(
        products[y + 1 - ty][rows * ty : rows * (ty + 1)]
        for ty in range(3)
        if y + 1 - ty in products
    )


def half_row(plane, z, c1, xs):
    row = plane[z // 2][:c1].astype(f32)
    return pltpu.roll(row, lanes - xs, 1) if z % 2 else row


def shifted_inputs(plane, zs, c1, xs):
    lane = lax.broadcasted_iota(jnp.int32, (1, lanes), 1)
    row = []
    for z in range(zs):
        pooled = half_row(plane, z, c1, xs)
        act = jnp.where(pooled > 0, pooled, leak_rate * pooled)
        act = jnp.where(lane < xs, act, 0.0).astype(bf16).astype(f32)
        row.append(
            jnp.concatenate(
                [pltpu.roll(act, 1, 1), act, pltpu.roll(act, lanes - 1, 1)], 0
            ).astype(bf16)
        )
    return jnp.concatenate(row, 1)


def side_kernel(
    sizes,
    odd_ref,
    own_refs,
    rim_refs,
    volume_ref,
    first_ref,
    second_ref,
    inputs_ref,
    terms_ref,
    second_sum_ref,
    places_ref,
    cells_ref,
    first_out_ref,
    second_out_ref,
    first_order_ref,
    second_order_ref,
    up_ref,
):
    ys, zs, xs, c1, c2 = sizes
    zlow, zhigh = sides_of(rim_refs, odd_ref[0] > 0)
    own = sides_of(own_refs, odd_ref[1] > 0)
    parity = lane_parity()
    zq = zs // 2
    rows = spread_quarter(own[0][zq], own[0][zq + 1], xs, c2, zq)
    rims = jnp.concatenate([zlow[0], zlow[1], zhigh[0], zhigh[1]], 0)
    rims = dot(rims, spread_matrix(xs, xs // 2))
    rims = [rims[n * c2 : (n + 1) * c2] for n in range(4)]
    rows = [(rims[0], rims[1])] + rows + [(rims[2], rims[3])]
    for n, (value, place) in enumerate(rows):
        cells = unpooled(value, place, parity)
        for dy in range(2):
            for dz in range(2):
                up_ref[dy, 2 * n + dz] = cells[dy][dz]
    for y in range(ys):
        for n, row in enumerate(spread_places(own[y], (zlow[y], zhigh[y]), xs, c1, zq)):
            places_ref[y, n] = row.astype(bf16)

    lane = lax.broadcasted_iota(jnp.int32, (1, 1, lanes), 2)
    c0, _, zf = volume_ref.shape[1:4]
    for y in range(2 * ys):
        cell = volume_ref[0, :, y].astype(f32)
        moved = [
            jnp.where(lane > 0, pltpu.roll(cell, 1, 2), 0.0),
            cell,
            jnp.where(lane < lanes - 1, pltpu.roll(cell, lanes - 1, 2), 0.0),
            jnp.zeros_like(cell),
        ]
        turned = jnp.transpose(jnp.concatenate(moved, 0), (1, 0, 2))
        for z in range(zf):
            cells_ref[y, :, z * lanes : (z + 1) * lanes] = turned[z].astype(bf16)

    wide = []
    for tz in range(3):
        parts = []
        for n in range(9):
            tap = 9 * (n // 3) + 3 * tz + n % 3
            parts += [first_ref[tap].astype(f32), jnp.zeros((8 - c0, c1), f32)]
        wide.append(jnp.concatenate(parts, 0))
    first_out_ref[...] = jnp.concatenate(wide, 1).astype(bf16)
    wide = [
        jnp.concatenate(
            [second_ref[9 * (n // 3) + 3 * tz + n % 3].astype(f32) for n in range(9)], 0
        )
        for tz in range(3)
    ]
    second_out_ref[...] = jnp.concatenate(wide, 1).astype(bf16)
    for tz in range(3):
        first_order_ref[tz] = order_matrix(c0, 4 * c0, first_order_ref.shape[1:], tz)
        second_order_ref[tz] = order_matrix(c1, 3 * c1, second_order_ref.shape[1:], tz)

    weights = second_out_ref[...]
    inputs = {y: shifted_inputs(own[y], zs, c1, xs) for y in range(ys)}
    for y in range(ys):
        inputs_ref[y] = inputs[y]
    nothing = jnp.zeros((3 * c1, zs * lanes), bf16)
    second_sum, products = 0.0, {}
    for y in range(ys):
        around = z_stack(lambda z: up_ref[y, z + 2], zs)
        products[y] = dot(weights, around)
        meet = jnp.concatenate([inputs.get(y - 1 + ty, nothing) for ty in range(3)], 0)
        second_sum += dot_nt(meet, around[:, lanes:-lanes])
    second_sum_ref[...] = second_sum
    for y in range(-1, ys + 1):
        terms_ref[y + 1] = y_terms(products, y, 3 * c1)


def main_kernel(
    sizes,
    odd_ref,
    own_refs,
    rim_refs,
    plane_refs,
    row_refs,
    inputs_ref,
    terms_ref,
    second_sum_ref,
    own_places_ref,
    volume_ref,
    second_ref,
    first_order_ref,
    second_order_ref,
    sums_ref,
    down_ref,
    up_ref,
):
    ys, zs, xs, c1, c2 = sizes
    zq = zs // 2
    odd_z, odd_y = odd_ref[0] > 0, odd_ref[1] > 0
    zlow, zhigh = sides_of(rim_refs, odd_z)
    own = sides_of(own_refs, odd_y)
    planes = sides_of(plane_refs, odd_y)
    even_rims, other_rims = [
        sides_of([ref[n] for n in range(len(rim_refs))], odd_z) for ref in row_refs
    ]
    plane_rims = [
        [jnp.where(odd_y, even_rims[n], other_rims[n]) for n in range(2)],
        [jnp.where(odd_y, other_rims[n], even_rims[n]) for n in range(2)],
    ]
    parity = lane_parity()
    lane = lax.broadcasted_iota(jnp.int32, (1, lanes), 1)

    near, far = spread_matrix(xs, xs // 2), spread_matrix(xs + xs // 2, xs // 2)
    for side in range(2):
        plane, (low, high) = planes[side], plane_rims[side]
        ends = jnp.concatenate([low, high], 0)
        values, places = dot(ends, near), dot(ends, far)
        rows = spread_quarter(plane[zq], plane[zq + 1], xs, c2, zq)
        rows = [(values[:c2], places[:c2])] + rows + [(values[c2:], places[c2:])]
        for n, (value, place) in enumerate(rows):
            cells = unpooled(value, place, parity)
            for dy in range(2):
                for dz in range(2):
                    up_ref[side, dy, 2 * n + dz] = cells[dy][dz]

    def pooled_row(y, z):
        side = None if 0 <= y < ys else int(y >= ys)
        if 0 <= z < zs:
            return half_row(own[y] if side is None else planes[side], z, c1, xs)
        at = int(z >= 0)
        rim = (zlow, zhigh)[at][y] if side is None else plane_rims[side][at]
        return rim[:c1].astype(f32)

    plane_places = [
        spread_places(planes[side], plane_rims[side], xs, c1, zq) for side in range(2)
    ]

    zr = range(-1, zs + 1)
    weights = second_ref[...]
    second_sum, products = second_sum_ref[...], {}
    nothing = jnp.zeros((3 * c1, zs * lanes), bf16)
    for y in (-2, -1, ys, ys + 1):
        side, dy = (0, y + 2) if y < 0 else (1, y - ys)
        around = z_stack(lambda z: up_ref[side, dy, z + 2], zs)
        products[y] = dot(weights, around)
        if -1 <= y <= ys:
            meet = [
                inputs_ref[y - 1 + ty] if 0 <= y - 1 + ty < ys else nothing for ty in range(3)
            ]
            second_sum += dot_nt(jnp.concatenate(meet, 0), around[:, lanes:-lanes])

    spread = spread_matrix(0, xs)
    for y in range(-1, ys + 1):
        terms = terms_ref[y + 1] + y_terms(products, y, 3 * c1)
        grads = []
        for n, z in enumerate(zr):
            pooled = pooled_row(y, z)
            at = slice(n * lanes, (n + 1) * lanes)
            total = (
                pltpu.roll(terms[:c1, at], lanes - 1, 1)
                + terms[c1 : 2 * c1, at]
                + pltpu.roll(terms[2 * c1 :, at], 1, 1)
            )
            grads.append((total * jnp.where(pooled > 0, 1.0, leak_rate)).astype(bf16))
        values = dot(jnp.concatenate(grads, 0), spread)
        for n, z in enumerate(zr):
            if 0 <= y < ys:
                place = own_places_ref[y, n].astype(f32)
            else:
                place = plane_places[int(y >= ys)][n]
            cells = unpooled(values[n * c1 : (n + 1) * c1], place, parity)
            for dy in range(2):
                for dz in range(2):
                    down_ref[2 * y + 2 + dy, 2 * z + 2 + dz] = cells[dy][dz]

    nothing = jnp.zeros(volume_ref.shape[1:], bf16)
    first_sum = None
    for plane in range(-1, 2 * ys + 1):
        meet = [
            volume_ref[plane - 1 + ty] if 0 <= plane - 1 + ty < 2 * ys else nothing
            for ty in range(3)
        ]
        term = dot_nt(jnp.concatenate(meet, 0), full_stack(down_ref, plane, 2 * zs))
        first_sum = term if first_sum is None else first_sum + term

    first_sum, second_sum = first_sum.T, second_sum.T
    first, second = 0.0, 0.0
    for tz in range(3):
        first += dot(first_sum[tz * c1 : (tz + 1) * c1].astype(bf16), first_order_ref[tz])
        second += dot(second_sum[tz * c2 : (tz + 1) * c2].astype(bf16), second_order_ref[tz])

    shards_dp, count = sums_ref.shape[:2]
    seconds = flat_rows(second, 27 * c1, c2 // shards_dp, shards_dp)
    firsts = flat_rows(first, 27 * (volume_ref.shape[1] // 4), c1 // shards_dp, shards_dp)
    for d in range(shards_dp):
        rows = seconds[d] + firsts[d]
        if len(rows) < count:
            rows = rows + [jnp.zeros((count - len(rows), lanes), f32)]
        sums_ref[d] = jnp.concatenate(rows, 0).astype(bf16)


def full_stack(down_ref, plane, count):
    return jnp.concatenate(
        [
            jnp.concatenate([down_ref[plane + 2, z + 3 - tz] for z in range(count)], 1)
            for tz in range(3)
        ],
        0,
    )


def volume_kernel(down_ref, first_ref, grad_ref, cells_ref, leaving_ref, sent):
    weights = first_ref[...]
    c0, yf, zf = grad_ref.shape[:3]
    lane = lax.broadcasted_iota(jnp.int32, (1, lanes), 1)
    products, leaving = {}, []
    for plane in range(-1, yf + 1):
        products[plane] = dot(weights, full_stack(down_ref, plane, zf))
        y = plane - 1
        if y < 0:
            continue
        terms = y_terms(products, y, 24)
        for z in range(zf):
            at = slice(z * lanes, (z + 1) * lanes)
            left = jnp.where(lane < lanes - 1, pltpu.roll(terms[:8, at], lanes - 1, 1), 0.0)
            right = jnp.where(lane > 0, pltpu.roll(terms[16:, at], 1, 1), 0.0)
            total = left + terms[8:16, at] + right
            for i in range(c0):
                cells_ref[i, y, z : z + 1, :] = total[i : i + 1]
        leaving_ref[:, y] = cells_ref[:, y].astype(bf16)
        leaving.append(pltpu.make_async_copy(leaving_ref.at[:, y], grad_ref.at[:, y], sent.at[y]))
        leaving[y].start()
    for move in leaving:
        move.wait()


def shards(
    volume,
    pooled_first,
    where_first,
    pooled_second,
    where_second,
    upstream,
    kernel_first,
    kernel_second,
):
    dp, gy, gz = (lax.axis_size(a) for a in ("dp", "gy", "gz"))
    c0, c1, c2 = volume.shape[1], pooled_first.shape[1], pooled_second.shape[1]
    ys, zs, xs = pooled_first.shape[2:]

    odd_z, odd_y = lax.axis_index("gz") % 2 == 1, lax.axis_index("gy") % 2 == 1
    odd = jnp.stack([odd_z, odd_y]).astype(jnp.int32)
    smem = pl.BlockSpec(memory_space=pltpu.SMEM)
    vmem = pl.BlockSpec(memory_space=pltpu.VMEM)
    params = pltpu.CompilerParams(vmem_limit_bytes=48 * 1024 * 1024)

    def like(*shape):
        return jax.ShapeDtypeStruct(shape, bf16)

    def pairs_of(axis, begin):
        count = lax.axis_size(axis)
        pairs = [(i, i + 1) for i in range(begin, count - 1, 2)]
        return pairs + [(b, a) for a, b in pairs]

    kinds = 2 if gz > 2 else 1
    raw = (upstream, pooled_second, where_second, pooled_first, where_first)
    plane = like(zs // 2 + 2, 2 * c1, lanes)
    prepared = (plane, plane) + (like(2, 2 * c1, lanes),) * kinds
    even, other, *rims = pl.pallas_call(
        functools.partial(prepare_kernel, kinds),
        out_shape=tuple(pltpu.VMEM(a.shape, a.dtype) for a in prepared),
        in_specs=[smem] + [pl.BlockSpec(memory_space=pltpu.HBM)] * 5,
        out_specs=(vmem,) * (2 + kinds),
        scratch_shapes=[pltpu.VMEM(a.shape, a.dtype) for a in raw]
        + [pltpu.SemaphoreType.DMA((5,))],
        compiler_params=pltpu.CompilerParams(vmem_limit_bytes=49152 * 1024),
    )(odd, *[pltpu.with_memory_space_constraint(a, pltpu.HBM) for a in raw])

    def moved(block, axes, pairs):
        return lax.ppermute(block, axes, pairs) if pairs else jnp.zeros_like(block)

    got_rims = [moved(rim, "gz", pairs_of("gz", n)) for n, rim in enumerate(rims)]
    got_planes = [moved(plane, "gy", pairs_of("gy", n)) for n, plane in enumerate((even, other))]

    def facing(row, rim):
        return jnp.concatenate([row] + [rim[n, :, xs : xs + xs // 2] for n in range(2)], 1)

    low, high = ([facing(rim[y, :, :xs], rim) for rim in got_rims] for y in (0, ys - 1))
    low, high = jnp.stack(low), jnp.stack(high)
    got_rows = [
        moved(jnp.where(odd_y == (n == 0), low, high), "gy", pairs_of("gy", n)) for n in range(2)
    ]

    first = jnp.transpose(kernel_first, (2, 3, 4, 1, 0)).reshape(27, c0, c1)
    second = jnp.transpose(kernel_second, (2, 3, 4, 1, 0)).reshape(27, c1, c2)
    sizes = (ys, zs, xs, c1, c2)
    wide = rows_of(27 * c1) * lanes
    inputs, terms, partial, places, cells, first, second, *orders = pl.pallas_call(
        functools.partial(side_kernel, sizes),
        out_shape=(
            like(ys, 3 * c1, zs * lanes),
            jax.ShapeDtypeStruct((ys + 2, 3 * c1, (zs + 2) * lanes), f32),
            jax.ShapeDtypeStruct((9 * c1, 3 * c2), f32),
            like(ys, zs + 2, c1, lanes),
            like(2 * ys, 4 * c0, 2 * zs * lanes),
            like(72, 3 * c1),
            like(9 * c1, 3 * c2),
            like(3, 12 * c0, lanes),
            like(3, 9 * c1, wide),
        ),
        in_specs=[smem, [vmem] * 2, [vmem] * kinds, vmem, vmem, vmem],
        out_specs=(vmem,) * 9,
        scratch_shapes=[pltpu.VMEM((ys, zs + 4, c2, lanes), bf16)],
        compiler_params=params,
        cost_estimate=pl.CostEstimate(flops=10**7, bytes_accessed=10**6, transcendentals=0),
    )(odd, [even, other], got_rims, volume, first, second)

    sizes1, sizes2 = 27 * c0 * c1 // dp, 27 * c1 * c2 // dp
    sum_rows = -(-(rows_of(sizes1) + rows_of(sizes2)) // 32) * 32
    sums, down = pl.pallas_call(
        functools.partial(main_kernel, sizes),
        out_shape=(
            like(dp, sum_rows, lanes),
            like(2 * ys + 4, 2 * zs + 4, c1, lanes),
        ),
        in_specs=[smem, [vmem] * 2, [vmem] * kinds, [vmem] * 2, [vmem] * 2] + [vmem] * 8,
        out_specs=(vmem, vmem),
        scratch_shapes=[pltpu.VMEM((2, 2, zs + 4, c2, lanes), bf16)],
        compiler_params=params,
        cost_estimate=pl.CostEstimate(
            flops=200_000_000, bytes_accessed=2_000_000, transcendentals=0
        ),
    )(
        odd,
        [even, other],
        got_rims,
        got_planes,
        got_rows,
        inputs,
        terms,
        partial,
        places,
        cells,
        second,
        *orders,
    )
    grad_vol = pl.pallas_call(
        volume_kernel,
        out_shape=like(*volume.shape[1:]),
        in_specs=[vmem, vmem],
        out_specs=pl.BlockSpec(memory_space=pl.ANY),
        scratch_shapes=[
            pltpu.VMEM(volume.shape[1:], f32),
            pltpu.VMEM(volume.shape[1:], bf16),
            pltpu.SemaphoreType.DMA((2 * ys,)),
        ],
        compiler_params=params,
        cost_estimate=pl.CostEstimate(flops=10**7, bytes_accessed=10**6, transcendentals=0),
    )(down, first)

    half = sum_rows // 2
    low, high = sums[:, :half], sums[:, half:]
    other = lax.ppermute(jnp.where(odd_y, low, high), "gy", pairs_of("gy", 0))
    part = jnp.where(odd_y, high, low).astype(f32) + other.astype(f32)
    sent = jnp.broadcast_to(part.astype(bf16)[:, None], (dp, gy * gz) + part.shape[1:])
    sent = sent.reshape((dp * gy * gz,) + part.shape[1:])
    got = lax.all_to_all(sent, ("dp", "gy", "gz"), 0, 0, tiled=True)
    got = got.reshape((dp * gy // 2, 2, gz) + part.shape[1:])
    count = volume.shape[0] * volume.shape[2] * volume.shape[3] * volume.shape[4] * dp * gy * gz
    total = jnp.sum(got.astype(f32), axis=(0, 2)).reshape(sum_rows, lanes)
    split = rows_of(sizes2)
    second_out = total[:split].reshape(-1)[:sizes2] * math.sqrt(64.0 / count)
    first_out = total[split : split + rows_of(sizes1)].reshape(-1)[:sizes1]
    return grad_vol[None], first_out * math.sqrt(8.0 / count), second_out


def solution(mesh):
    cells = P("dp", None, "gy", "gz", None)
    return jax.shard_map(
        shards,
        mesh=mesh,
        in_specs=(cells,) * 6 + (P(), P()),
        out_specs=(cells, P("dp"), P("dp")),
        check_vma=False,
    )
```

```python
import functools
import math

import jax
import jax.numpy as jnp
from jax import lax
from jax.experimental import pallas as pl
from jax.experimental.pallas import tpu as pltpu
from jax.sharding import PartitionSpec as P

leak_rate = 0.3
lanes = 128
f32, bf16 = jnp.float32, jnp.bfloat16


def dot(a, b):
    return lax.dot_general(a, b, (((1,), (0,)), ((), ())), preferred_element_type=f32)


def dot_nt(a, b):
    return lax.dot_general(a, b, (((1,), (1,)), ((), ())), preferred_element_type=f32)


def spread_matrix(first_row, count):
    row = lax.broadcasted_iota(jnp.int32, (lanes, lanes), 0)
    lane = lax.broadcasted_iota(jnp.int32, (lanes, lanes), 1)
    hit = (lane >> 1) + first_row == row
    return jnp.where(hit & (lane < 2 * count), 1.0, 0.0).astype(bf16)


def order_matrix(ins, step, shape, tz):
    row = lax.broadcasted_iota(jnp.int32, shape, 0)
    column = lax.broadcasted_iota(jnp.int32, shape, 1)
    at = row % step
    hit = column == (at % ins) * 27 + 9 * (row // step) + 3 * tz + at // ins
    return jnp.where(hit & (at < 3 * ins), 1.0, 0.0).astype(bf16)


def rows_of(count):
    return -(-count // lanes)


def flat_rows(values, length, keep, shards_dp):
    starts = [length * k % lanes for k in range(keep)]
    width = rows_of(max(starts) + length) * lanes
    if values.shape[1] < width:
        blank = jnp.zeros((values.shape[0], width - values.shape[1]), f32)
        values = jnp.concatenate([values, blank], 1)
    turned = {n: pltpu.roll(values, n, 1) if n else values for n in sorted(set(starts))}
    shards = []
    for d in range(shards_dp):
        rows = [None] * rows_of(length * keep)
        for k, start in enumerate(starts):
            for t in range(rows_of(start + length)):
                at = length * k // lanes + t
                piece = turned[start][d * keep + k : d * keep + k + 1, t * lanes : (t + 1) * lanes]
                rows[at] = piece if rows[at] is None else rows[at] + piece
        shards.append(rows)
    return shards


def prepare_kernel(kinds, odd_ref, *refs):
    count = 2 + kinds
    inputs, outputs, refs = refs[:5], refs[5 : 5 + count], refs[5 + count :]
    copies, arrived = refs[:5], refs[5]
    moves = [
        pltpu.make_async_copy(source, target, arrived.at[n])
        for n, (source, target) in enumerate(zip(inputs, copies))
    ]
    for move in moves:
        move.start()
    prepare(moves, odd_ref, *copies, *outputs[:2], outputs[2:])


def prepare(
    moves,
    odd_ref,
    upstream_ref,
    pooled_second_ref,
    where_second_ref,
    pooled_first_ref,
    where_first_ref,
    even_ref,
    odd_plane_ref,
    rim_refs,
):
    c1, ys, zs, xs = pooled_first_ref.shape[1:]
    zq = zs // 2
    odd_z, odd_y = odd_ref[0] > 0, odd_ref[1] > 0
    for move in moves[:3]:
        move.wait()
    slope = jnp.where(pooled_second_ref[0, :, 0].astype(f32) > 0, 1.0, leak_rate)
    value = upstream_ref[0, :, 0].astype(f32) * slope
    place = (where_second_ref[0, :, 0] + 1).astype(f32)
    quarter = [jnp.transpose(part, (1, 0, 2)) for part in (value, place)]
    for n, part in enumerate(quarter):
        row = jnp.concatenate([part[z] for z in range(zq)], 1).astype(bf16)
        even_ref[zq + n] = row
        odd_plane_ref[zq + n] = row
    fill = jnp.zeros((2 * c1, lanes - xs - xs // 2), f32)
    packed = []
    for move in moves[3:]:
        move.wait()
    for y in range(ys):
        pooled = jnp.transpose(pooled_first_ref[0, :, y].astype(f32), (1, 0, 2))
        places = jnp.transpose((where_first_ref[0, :, y] + 1).astype(f32), (1, 0, 2))
        rows = [jnp.concatenate([pooled[z], places[z]], 0) for z in range(zs)]
        packed.append(
            [jnp.concatenate([rows[2 * n], rows[2 * n + 1]], 1).astype(bf16) for n in range(zq)]
        )
        low = jnp.concatenate([rows[0], quarter[y][0], fill], 1)
        high = jnp.concatenate([rows[-1], quarter[y][-1], fill], 1)
        for n, ref in enumerate(rim_refs):
            ref[y] = jnp.where(odd_z == (n == 0), low, high).astype(bf16)
    for n in range(zq):
        even_ref[n] = jnp.where(odd_y, packed[0][n], packed[-1][n])
        odd_plane_ref[n] = jnp.where(odd_y, packed[-1][n], packed[0][n])


def sides_of(refs, odd):
    even = refs[0][...]
    other = refs[1][...] if len(refs) > 1 else jnp.zeros_like(even)
    return jnp.where(odd, even, other), jnp.where(odd, other, even)


def unpooled(values, places, parity):
    return [
        [
            jnp.where(places == parity + (4 * dy + 2 * dz), values, 0.0).astype(bf16)
            for dz in range(2)
        ]
        for dy in range(2)
    ]


def lane_parity():
    lane = lax.broadcasted_iota(jnp.int32, (1, lanes), 1)
    return (lane & 1).astype(f32) + 1.0


def spread_quarter(values, places, xs, c2, zq):
    wide = jnp.concatenate([spread_matrix(z * xs // 2, xs // 2) for z in range(zq)], 1)
    found = dot(jnp.concatenate([values, places], 0), wide)
    return [
        (found[:c2, z * lanes : (z + 1) * lanes], found[c2:, z * lanes : (z + 1) * lanes])
        for z in range(zq)
    ]


def spread_places(plane, ends, xs, c1, zq):
    wide = jnp.concatenate([spread_matrix(0, xs), spread_matrix(xs, xs)], 1)
    rows = [plane[n][c1:] for n in range(zq)] + [end[c1:] for end in ends]
    found = dot(jnp.concatenate(rows, 0), wide)
    inner = [
        found[n * c1 : (n + 1) * c1, m * lanes : (m + 1) * lanes]
        for n in range(zq)
        for m in range(2)
    ]
    low, high = found[zq * c1 : (zq + 1) * c1, :lanes], found[(zq + 1) * c1 :, :lanes]
    return [low] + inner + [high]


def z_stack(row_of, zs):
    zr = range(-1, zs + 1)
    return jnp.concatenate(
        [jnp.concatenate([row_of(z + 1 - tz) for z in zr], 1) for tz in range(3)], 0
    )


def y_terms(products, y, rows):
    return sum(
        products[y + 1 - ty][rows * ty : rows * (ty + 1)]
        for ty in range(3)
        if y + 1 - ty in products
    )


def half_row(plane, z, c1, xs):
    row = plane[z // 2][:c1].astype(f32)
    return pltpu.roll(row, lanes - xs, 1) if z % 2 else row


def shifted_inputs(plane, zs, c1, xs):
    lane = lax.broadcasted_iota(jnp.int32, (1, lanes), 1)
    row = []
    for z in range(zs):
        pooled = half_row(plane, z, c1, xs)
        act = jnp.where(pooled > 0, pooled, leak_rate * pooled)
        act = jnp.where(lane < xs, act, 0.0).astype(bf16).astype(f32)
        row.append(
            jnp.concatenate(
                [pltpu.roll(act, 1, 1), act, pltpu.roll(act, lanes - 1, 1)], 0
            ).astype(bf16)
        )
    return jnp.concatenate(row, 1)


def side_kernel(
    sizes,
    odd_ref,
    own_refs,
    rim_refs,
    volume_ref,
    first_ref,
    second_ref,
    inputs_ref,
    terms_ref,
    second_sum_ref,
    places_ref,
    cells_ref,
    first_out_ref,
    second_out_ref,
    first_order_ref,
    second_order_ref,
    up_ref,
):
    ys, zs, xs, c1, c2 = sizes
    zlow, zhigh = sides_of(rim_refs, odd_ref[0] > 0)
    own = sides_of(own_refs, odd_ref[1] > 0)
    parity = lane_parity()
    zq = zs // 2
    rows = spread_quarter(own[0][zq], own[0][zq + 1], xs, c2, zq)
    rims = jnp.concatenate([zlow[0], zlow[1], zhigh[0], zhigh[1]], 0)
    rims = dot(rims, spread_matrix(xs, xs // 2))
    rims = [rims[n * c2 : (n + 1) * c2] for n in range(4)]
    rows = [(rims[0], rims[1])] + rows + [(rims[2], rims[3])]
    for n, (value, place) in enumerate(rows):
        cells = unpooled(value, place, parity)
        for dy in range(2):
            for dz in range(2):
                up_ref[dy, 2 * n + dz] = cells[dy][dz]
    for y in range(ys):
        for n, row in enumerate(spread_places(own[y], (zlow[y], zhigh[y]), xs, c1, zq)):
            places_ref[y, n] = row.astype(bf16)

    lane = lax.broadcasted_iota(jnp.int32, (1, 1, lanes), 2)
    c0, _, zf = volume_ref.shape[1:4]
    for y in range(2 * ys):
        cell = volume_ref[0, :, y].astype(f32)
        moved = [
            jnp.where(lane > 0, pltpu.roll(cell, 1, 2), 0.0),
            cell,
            jnp.where(lane < lanes - 1, pltpu.roll(cell, lanes - 1, 2), 0.0),
            jnp.zeros_like(cell),
        ]
        turned = jnp.transpose(jnp.concatenate(moved, 0), (1, 0, 2))
        for z in range(zf):
            cells_ref[y, :, z * lanes : (z + 1) * lanes] = turned[z].astype(bf16)

    wide = []
    for tz in range(3):
        parts = []
        for n in range(9):
            tap = 9 * (n // 3) + 3 * tz + n % 3
            parts += [first_ref[tap].astype(f32), jnp.zeros((8 - c0, c1), f32)]
        wide.append(jnp.concatenate(parts, 0))
    first_out_ref[...] = jnp.concatenate(wide, 1).astype(bf16)
    wide = [
        jnp.concatenate(
            [second_ref[9 * (n // 3) + 3 * tz + n % 3].astype(f32) for n in range(9)], 0
        )
        for tz in range(3)
    ]
    second_out_ref[...] = jnp.concatenate(wide, 1).astype(bf16)
    for tz in range(3):
        first_order_ref[tz] = order_matrix(c0, 4 * c0, first_order_ref.shape[1:], tz)
        second_order_ref[tz] = order_matrix(c1, 3 * c1, second_order_ref.shape[1:], tz)

    weights = second_out_ref[...]
    inputs = {y: shifted_inputs(own[y], zs, c1, xs) for y in range(ys)}
    for y in range(ys):
        inputs_ref[y] = inputs[y]
    nothing = jnp.zeros((3 * c1, zs * lanes), bf16)
    second_sum, products = 0.0, {}
    for y in range(ys):
        around = z_stack(lambda z: up_ref[y, z + 2], zs)
        products[y] = dot(weights, around)
        meet = jnp.concatenate([inputs.get(y - 1 + ty, nothing) for ty in range(3)], 0)
        second_sum += dot_nt(meet, around[:, lanes:-lanes])
    second_sum_ref[...] = second_sum
    for y in range(-1, ys + 1):
        terms_ref[y + 1] = y_terms(products, y, 3 * c1)


def main_kernel(
    sizes,
    odd_ref,
    own_refs,
    rim_refs,
    plane_refs,
    row_refs,
    inputs_ref,
    terms_ref,
    second_sum_ref,
    own_places_ref,
    volume_ref,
    second_ref,
    first_order_ref,
    second_order_ref,
    sums_ref,
    down_ref,
    up_ref,
):
    ys, zs, xs, c1, c2 = sizes
    zq = zs // 2
    odd_z, odd_y = odd_ref[0] > 0, odd_ref[1] > 0
    zlow, zhigh = sides_of(rim_refs, odd_z)
    own = sides_of(own_refs, odd_y)
    planes = sides_of(plane_refs, odd_y)
    even_rims, other_rims = [
        sides_of([ref[n] for n in range(len(rim_refs))], odd_z) for ref in row_refs
    ]
    plane_rims = [
        [jnp.where(odd_y, even_rims[n], other_rims[n]) for n in range(2)],
        [jnp.where(odd_y, other_rims[n], even_rims[n]) for n in range(2)],
    ]
    parity = lane_parity()
    lane = lax.broadcasted_iota(jnp.int32, (1, lanes), 1)

    near, far = spread_matrix(xs, xs // 2), spread_matrix(xs + xs // 2, xs // 2)
    for side in range(2):
        plane, (low, high) = planes[side], plane_rims[side]
        ends = jnp.concatenate([low, high], 0)
        values, places = dot(ends, near), dot(ends, far)
        rows = spread_quarter(plane[zq], plane[zq + 1], xs, c2, zq)
        rows = [(values[:c2], places[:c2])] + rows + [(values[c2:], places[c2:])]
        for n, (value, place) in enumerate(rows):
            cells = unpooled(value, place, parity)
            for dy in range(2):
                for dz in range(2):
                    up_ref[side, dy, 2 * n + dz] = cells[dy][dz]

    def pooled_row(y, z):
        side = None if 0 <= y < ys else int(y >= ys)
        if 0 <= z < zs:
            return half_row(own[y] if side is None else planes[side], z, c1, xs)
        at = int(z >= 0)
        rim = (zlow, zhigh)[at][y] if side is None else plane_rims[side][at]
        return rim[:c1].astype(f32)

    plane_places = [
        spread_places(planes[side], plane_rims[side], xs, c1, zq) for side in range(2)
    ]

    zr = range(-1, zs + 1)
    weights = second_ref[...]
    second_sum, products = second_sum_ref[...], {}
    nothing = jnp.zeros((3 * c1, zs * lanes), bf16)
    for y in (-2, -1, ys, ys + 1):
        side, dy = (0, y + 2) if y < 0 else (1, y - ys)
        around = z_stack(lambda z: up_ref[side, dy, z + 2], zs)
        products[y] = dot(weights, around)
        if -1 <= y <= ys:
            meet = [
                inputs_ref[y - 1 + ty] if 0 <= y - 1 + ty < ys else nothing for ty in range(3)
            ]
            second_sum += dot_nt(jnp.concatenate(meet, 0), around[:, lanes:-lanes])

    spread = spread_matrix(0, xs)
    for y in range(-1, ys + 1):
        terms = terms_ref[y + 1] + y_terms(products, y, 3 * c1)
        grads = []
        for n, z in enumerate(zr):
            pooled = pooled_row(y, z)
            at = slice(n * lanes, (n + 1) * lanes)
            total = (
                pltpu.roll(terms[:c1, at], lanes - 1, 1)
                + terms[c1 : 2 * c1, at]
                + pltpu.roll(terms[2 * c1 :, at], 1, 1)
            )
            grads.append((total * jnp.where(pooled > 0, 1.0, leak_rate)).astype(bf16))
        values = dot(jnp.concatenate(grads, 0), spread)
        for n, z in enumerate(zr):
            if 0 <= y < ys:
                place = own_places_ref[y, n].astype(f32)
            else:
                place = plane_places[int(y >= ys)][n]
            cells = unpooled(values[n * c1 : (n + 1) * c1], place, parity)
            for dy in range(2):
                for dz in range(2):
                    down_ref[2 * y + 2 + dy, 2 * z + 2 + dz] = cells[dy][dz]

    nothing = jnp.zeros(volume_ref.shape[1:], bf16)
    first_sum = None
    for plane in range(-1, 2 * ys + 1):
        meet = [
            volume_ref[plane - 1 + ty] if 0 <= plane - 1 + ty < 2 * ys else nothing
            for ty in range(3)
        ]
        term = dot_nt(jnp.concatenate(meet, 0), full_stack(down_ref, plane, 2 * zs))
        first_sum = term if first_sum is None else first_sum + term

    first_sum, second_sum = first_sum.T, second_sum.T
    first, second = 0.0, 0.0
    for tz in range(3):
        first += dot(first_sum[tz * c1 : (tz + 1) * c1].astype(bf16), first_order_ref[tz])
        second += dot(second_sum[tz * c2 : (tz + 1) * c2].astype(bf16), second_order_ref[tz])

    shards_dp, count = sums_ref.shape[:2]
    seconds = flat_rows(second, 27 * c1, c2 // shards_dp, shards_dp)
    firsts = flat_rows(first, 27 * (volume_ref.shape[1] // 4), c1 // shards_dp, shards_dp)
    for d in range(shards_dp):
        rows = seconds[d] + firsts[d]
        if len(rows) < count:
            rows = rows + [jnp.zeros((count - len(rows), lanes), f32)]
        sums_ref[d] = jnp.concatenate(rows, 0).astype(bf16)


def full_stack(down_ref, plane, count):
    return jnp.concatenate(
        [
            jnp.concatenate([down_ref[plane + 2, z + 3 - tz] for z in range(count)], 1)
            for tz in range(3)
        ],
        0,
    )


def volume_kernel(down_ref, first_ref, grad_ref, cells_ref, leaving_ref, sent):
    weights = first_ref[...]
    c0, yf, zf = grad_ref.shape[:3]
    lane = lax.broadcasted_iota(jnp.int32, (1, lanes), 1)
    products, leaving = {}, []
    for plane in range(-1, yf + 1):
        products[plane] = dot(weights, full_stack(down_ref, plane, zf))
        y = plane - 1
        if y < 0:
            continue
        terms = y_terms(products, y, 24)
        for z in range(zf):
            at = slice(z * lanes, (z + 1) * lanes)
            left = jnp.where(lane < lanes - 1, pltpu.roll(terms[:8, at], lanes - 1, 1), 0.0)
            right = jnp.where(lane > 0, pltpu.roll(terms[16:, at], 1, 1), 0.0)
            total = left + terms[8:16, at] + right
            for i in range(c0):
                cells_ref[i, y, z : z + 1, :] = total[i : i + 1]
        leaving_ref[:, y] = cells_ref[:, y].astype(bf16)
        leaving.append(pltpu.make_async_copy(leaving_ref.at[:, y], grad_ref.at[:, y], sent.at[y]))
        leaving[y].start()
    for move in leaving:
        move.wait()


def shards(
    volume,
    pooled_first,
    where_first,
    pooled_second,
    where_second,
    upstream,
    kernel_first,
    kernel_second,
):
    dp, gy, gz = (lax.axis_size(a) for a in ("dp", "gy", "gz"))
    c0, c1, c2 = volume.shape[1], pooled_first.shape[1], pooled_second.shape[1]
    ys, zs, xs = pooled_first.shape[2:]

    odd_z, odd_y = lax.axis_index("gz") % 2 == 1, lax.axis_index("gy") % 2 == 1
    odd = jnp.stack([odd_z, odd_y]).astype(jnp.int32)
    smem = pl.BlockSpec(memory_space=pltpu.SMEM)
    vmem = pl.BlockSpec(memory_space=pltpu.VMEM)
    params = pltpu.CompilerParams(vmem_limit_bytes=48 * 1024 * 1024)

    def like(*shape):
        return jax.ShapeDtypeStruct(shape, bf16)

    def pairs_of(axis, begin):
        count = lax.axis_size(axis)
        pairs = [(i, i + 1) for i in range(begin, count - 1, 2)]
        return pairs + [(b, a) for a, b in pairs]

    kinds = 2 if gz > 2 else 1
    raw = (upstream, pooled_second, where_second, pooled_first, where_first)
    plane = like(zs // 2 + 2, 2 * c1, lanes)
    prepared = (plane, plane) + (like(2, 2 * c1, lanes),) * kinds
    even, other, *rims = pl.pallas_call(
        functools.partial(prepare_kernel, kinds),
        out_shape=tuple(pltpu.VMEM(a.shape, a.dtype) for a in prepared),
        in_specs=[smem] + [pl.BlockSpec(memory_space=pltpu.HBM)] * 5,
        out_specs=(vmem,) * (2 + kinds),
        scratch_shapes=[pltpu.VMEM(a.shape, a.dtype) for a in raw]
        + [pltpu.SemaphoreType.DMA((5,))],
        compiler_params=pltpu.CompilerParams(vmem_limit_bytes=49152 * 1024),
    )(odd, *[pltpu.with_memory_space_constraint(a, pltpu.HBM) for a in raw])

    def moved(block, axes, pairs):
        return lax.ppermute(block, axes, pairs) if pairs else jnp.zeros_like(block)

    got_rims = [moved(rim, "gz", pairs_of("gz", n)) for n, rim in enumerate(rims)]
    got_planes = [moved(plane, "gy", pairs_of("gy", n)) for n, plane in enumerate((even, other))]

    def facing(row, rim):
        return jnp.concatenate([row] + [rim[n, :, xs : xs + xs // 2] for n in range(2)], 1)

    low, high = ([facing(rim[y, :, :xs], rim) for rim in got_rims] for y in (0, ys - 1))
    low, high = jnp.stack(low), jnp.stack(high)
    got_rows = [
        moved(jnp.where(odd_y == (n == 0), low, high), "gy", pairs_of("gy", n)) for n in range(2)
    ]

    first = jnp.transpose(kernel_first, (2, 3, 4, 1, 0)).reshape(27, c0, c1)
    second = jnp.transpose(kernel_second, (2, 3, 4, 1, 0)).reshape(27, c1, c2)
    sizes = (ys, zs, xs, c1, c2)
    wide = rows_of(27 * c1) * lanes
    inputs, terms, partial, places, cells, first, second, *orders = pl.pallas_call(
        functools.partial(side_kernel, sizes),
        out_shape=(
            like(ys, 3 * c1, zs * lanes),
            jax.ShapeDtypeStruct((ys + 2, 3 * c1, (zs + 2) * lanes), f32),
            jax.ShapeDtypeStruct((9 * c1, 3 * c2), f32),
            like(ys, zs + 2, c1, lanes),
            like(2 * ys, 4 * c0, 2 * zs * lanes),
            like(72, 3 * c1),
            like(9 * c1, 3 * c2),
            like(3, 12 * c0, lanes),
            like(3, 9 * c1, wide),
        ),
        in_specs=[smem, [vmem] * 2, [vmem] * kinds, vmem, vmem, vmem],
        out_specs=(vmem,) * 9,
        scratch_shapes=[pltpu.VMEM((ys, zs + 4, c2, lanes), bf16)],
        compiler_params=params,
        cost_estimate=pl.CostEstimate(flops=10**7, bytes_accessed=10**6, transcendentals=0),
    )(odd, [even, other], got_rims, volume, first, second)

    sizes1, sizes2 = 27 * c0 * c1 // dp, 27 * c1 * c2 // dp
    sum_rows = -(-(rows_of(sizes1) + rows_of(sizes2)) // 32) * 32
    sums, down = pl.pallas_call(
        functools.partial(main_kernel, sizes),
        out_shape=(
            like(dp, sum_rows, lanes),
            like(2 * ys + 4, 2 * zs + 4, c1, lanes),
        ),
        in_specs=[smem, [vmem] * 2, [vmem] * kinds, [vmem] * 2, [vmem] * 2] + [vmem] * 8,
        out_specs=(vmem, vmem),
        scratch_shapes=[pltpu.VMEM((2, 2, zs + 4, c2, lanes), bf16)],
        compiler_params=params,
        cost_estimate=pl.CostEstimate(
            flops=200_000_000, bytes_accessed=2_000_000, transcendentals=0
        ),
    )(
        odd,
        [even, other],
        got_rims,
        got_planes,
        got_rows,
        inputs,
        terms,
        partial,
        places,
        cells,
        second,
        *orders,
    )
    grad_vol = pl.pallas_call(
        volume_kernel,
        out_shape=like(*volume.shape[1:]),
        in_specs=[vmem, vmem],
        out_specs=pl.BlockSpec(memory_space=pl.ANY),
        scratch_shapes=[
            pltpu.VMEM(volume.shape[1:], f32),
            pltpu.VMEM(volume.shape[1:], bf16),
            pltpu.SemaphoreType.DMA((2 * ys,)),
        ],
        compiler_params=pltpu.CompilerParams(vmem_limit_bytes=16 * 1024 * 1024),
        cost_estimate=pl.CostEstimate(flops=10**7, bytes_accessed=10**6, transcendentals=0),
    )(down, first)

    half = sum_rows // 2
    low, high = sums[:, :half], sums[:, half:]
    other = lax.ppermute(jnp.where(odd_y, low, high), "gy", pairs_of("gy", 0))
    part = jnp.where(odd_y, high, low).astype(f32) + other.astype(f32)
    sent = jnp.broadcast_to(part.astype(bf16)[:, None], (dp, gy * gz) + part.shape[1:])
    sent = sent.reshape((dp * gy * gz,) + part.shape[1:])
    got = lax.all_to_all(sent, ("dp", "gy", "gz"), 0, 0, tiled=True)
    got = got.reshape((dp * gy // 2, 2, gz) + part.shape[1:])
    count = volume.shape[0] * volume.shape[2] * volume.shape[3] * volume.shape[4] * dp * gy * gz
    total = jnp.sum(got.astype(f32), axis=(0, 2)).reshape(sum_rows, lanes)
    split = rows_of(sizes2)
    second_out = total[:split].reshape(-1)[:sizes2] * math.sqrt(64.0 / count)
    first_out = total[split : split + rows_of(sizes1)].reshape(-1)[:sizes1]
    return grad_vol[None], first_out * math.sqrt(8.0 / count), second_out


def solution(mesh):
    cells = P("dp", None, "gy", "gz", None)
    return jax.shard_map(
        shards,
        mesh=mesh,
        in_specs=(cells,) * 6 + (P(), P()),
        out_specs=(cells, P("dp"), P("dp")),
        check_vma=False,
    )
```
